32 devices in a mesh: member: 2 (over core), band: 16 (over z, y, x).
Axes of the slice: x: 2, y: 2, z: 4, core: 2. Of those that a mesh axis runs over, the one named last changes fastest.
Arguments:
- parent_state: float32 [16, 3, 256, 4096], P('member', None, 'band'), parts along dimension 0, may hold values from -6 to 6
- nest_state: float32 [16, 3, 384, 384], P('member', None, 'band'), parts along dimension 0, may hold values from -6 to 6
- offsets: int32 [16, 2], P('member'), parts along dimension 0, may hold values from 2 to 3966, as said below
Outputs:
- parent_out: float32 [16, 3, 256, 4096], P('member', None, 'band'), parts along dimension 0
- nest_out: float32 [16, 3, 384, 384], P('member', None, 'band'), parts along dimension 0
The draws below stay inside these ranges and needn't reach their ends.
There are 2 independent parts, one for each index of `member`. The reference program is written for one: setup_inputs(seed, part) draws one part's arguments, and reference() takes and returns one part's arrays. A program takes and returns all parts, laid end to end along the dimension named above; each array names one. Nothing has to cross between parts.
Inputs may be any that keep to these rules, and one draw needn't show every extreme that they name: Column 0 holds row offsets from 2 to 126, column 1 column offsets from 2 to 3966; in each column some member takes the lowest and some member the highest of its range.
All inputs are finite; a program needn't handle non-finite values.
Results may differ from the reference program's by a relative error of at most 0.00012.
Values sent between devices are 32-bit elements; how exact they have to be, the bound alone decides.
A program may use at most 256 MiB of HBM per device.

```python
import jax
import jax.numpy as jnp
from jax import lax

MEMB = 8
NX = 4096
NSTEPS = 3
NY = 256
NN = 384
NC = 128


def draw_offsets(key, part):
    keys = jax.random.split(jax.random.fold_in(key, 11), 4)
    row_top = NY - NC - 2
    col_top = NX - NC - 2
    rows = jax.random.randint(keys[0], (MEMB,), 2, row_top + 1)
    rows = rows.at[0].set(2).at[1].set(row_top)
    rows = jax.random.permutation(keys[1], rows)
    cols = jax.random.randint(keys[2], (MEMB,), 2, col_top + 1)
    cols = cols.at[0].set(2).at[1].set(col_top)
    cols = jax.random.permutation(keys[3], cols)
    return jnp.stack([rows, cols], axis=1).astype(jnp.int32)


def block_levels(own_key, dims, cuts, least, top_value):
    def one(position, blocks):
        steps = jax.random.uniform(jax.random.fold_in(jax.random.fold_in(own_key, 6), position), (blocks,), jnp.float32, least / len(cuts), top_value / len(cuts))
        return jnp.repeat(jnp.exp(steps), dims[position] // blocks).reshape((-1,) + (1,) * (len(dims) - position - 1))

    level = one(*cuts[0])
    for cut in cuts[1:]:
        level = level * one(*cut)
    return level


def centred(rng, dims, deviation, limit, shards=(), kind=jnp.bfloat16):
    values = jax.random.normal(rng, dims, jnp.float32) * deviation
    if len(shards) > 0:
        values = block_levels(rng, dims, shards, -0.22, 0.18) * values
    return jnp.clip(values, min=-limit, max=limit).astype(kind)


def setup_inputs(seed: int = 0, part: int = 0) -> dict:
    seeds = jax.random.split(jax.random.key(seed), 4)
    part_splits = jax.random.split(jax.random.fold_in(seeds[3], part), 4)
    parent_state = centred(part_splits[0], (MEMB, 3, NY, NX), 1.0, 6.0, ((2, 16),), jnp.float32)
    nest_state = centred(part_splits[1], (MEMB, 3, NN, NN), 1.0, 6.0, ((2, 16),), jnp.float32)
    offsets = draw_offsets(jax.random.fold_in(jax.random.fold_in(seeds[3], part), 71), part)
    return {"parent_state": parent_state, "nest_state": nest_state, "offsets": offsets}


courant = 0.9
friction = 0.02
rotation = 0.05
highest = lax.Precision.HIGHEST


def interp_matrix(fine, coarse_count):
    rows = jnp.arange(fine, dtype=jnp.int32)[:, None] + 1
    cols = jnp.arange(coarse_count, dtype=jnp.int32)[None, :]
    base = rows // 3
    frac = rows % 3
    upper = frac.astype(jnp.float32) / 3.0
    lower = (3 - frac).astype(jnp.float32) / 3.0
    return jnp.where(cols == base, lower, 0.0) + jnp.where(cols == base + 1, upper, 0.0)


def shift_cols(field):
    return 0.5 * (jnp.roll(field, -1, axis=-1) - jnp.roll(field, 1, axis=-1))


def shift_rows(field):
    padded = jnp.pad(field, ((0, 0), (1, 1), (0, 0)))
    return 0.5 * (padded[:, 2:] - padded[:, :-2])


def parent_step(state):
    height, zonal, meridional = state[:, 0], state[:, 1], state[:, 2]
    height_new = height - courant * (shift_cols(zonal) + shift_rows(meridional))
    zonal_new = (1.0 - friction) * zonal - courant * shift_cols(height_new) + rotation * meridional
    merid_new = (1.0 - friction) * meridional - courant * shift_rows(height_new) - rotation * zonal
    return jnp.stack([height_new, zonal_new, merid_new], axis=1)


def embed(inner, loop):
    return loop.at[:, :, 1:-1, 1:-1].set(inner)


def nest_step(state, loop):
    height, zonal, meridional = state[:, 0], state[:, 1], state[:, 2]
    flows = embed(state[:, 1:3], loop[:, 1:3])
    height_new = height - courant * (0.5 * (flows[:, 0, 1:-1, 2:] - flows[:, 0, 1:-1, :-2]) + 0.5 * (flows[:, 1, 2:, 1:-1] - flows[:, 1, :-2, 1:-1]))
    padded = embed(height_new[:, None], loop[:, 0:1])[:, 0]
    zonal_new = (1.0 - friction) * zonal - courant * (0.5 * (padded[:, 1:-1, 2:] - padded[:, 1:-1, :-2])) + rotation * meridional
    merid_new = (1.0 - friction) * meridional - courant * (0.5 * (padded[:, 2:, 1:-1] - padded[:, :-2, 1:-1])) - rotation * zonal
    return jnp.stack([height_new, zonal_new, merid_new], axis=1)


def reference(parent_state, nest_state, offsets):
    members = parent_state.shape[0]
    stepped = parent_step(parent_state)
    rows_off = offsets[:, 0].astype(jnp.int32)
    cols_off = offsets[:, 1].astype(jnp.int32)
    zero_index = jnp.zeros((), jnp.int32)

    def window(field, row0, col0):
        return lax.dynamic_slice(field, (zero_index, row0 - 1, col0 - 1), (3, NC + 2, NC + 2))

    windows = jax.vmap(window)(stepped, rows_off, cols_off)
    weights = interp_matrix(NN + 2, NC + 2)
    along = jnp.einsum('ip,mfpq->mfiq', weights, windows, precision=highest)
    loop = jnp.einsum('mfiq,jq->mfij', along, weights, precision=highest)
    nest = nest_state
    for _ in range(NSTEPS):
        nest = nest_step(nest, loop)
    coarse = nest.reshape(members, 3, NC, 3, NC, 3).mean(axis=(3, 5))

    def put(field, patch, row0, col0):
        return lax.dynamic_update_slice(field, patch, (zero_index, row0, col0))

    parent_out = jax.vmap(put)(stepped, coarse, rows_off, cols_off)
    return parent_out, nest
```

```python
import functools

import jax
import jax.numpy as jnp
from jax import lax
from jax.experimental import pallas as pl
from jax.experimental.pallas import tpu as pltpu
from jax.sharding import PartitionSpec as P

NSTEPS = 3
MESH = pl.DeviceIdType.MESH

courant = 0.9
friction = 0.02
rotation = 0.05
half = 0.5 * courant
keep = 1.0 - friction
highest = lax.Precision.HIGHEST
LANES = 128
HALO = 8


def lane_roll(x, shift):
    size = x.shape[-1]
    return pltpu.roll(x, shift % size, x.ndim - 1)


def row_roll(x, shift):
    size = x.shape[-2]
    return pltpu.roll(x, shift % size, x.ndim - 2)


def dx(x):
    return 0.5 * (lane_roll(x, -1) - lane_roll(x, 1))


def iota(shape, dim):
    return lax.broadcasted_iota(jnp.int32, shape, dim)


def gather_kernel(span, bands, off_ref, band_ref, par_ref, edge_ref, strip_ref, ends_ref):
    mem = pl.program_id(0)
    rows, width = par_ref.shape[2], par_ref.shape[3]
    row0, col0 = off_ref[mem, 0], off_ref[mem, 1]
    band = band_ref[0]

    z_top, z_bot = par_ref[0, 1, 0:1, :], par_ref[0, 1, rows - 1 : rows, :]
    m_top, m_bot = par_ref[0, 2, 0:1, :], par_ref[0, 2, rows - 1 : rows, :]
    edge_ref[0, 0, 0:1, :] = m_top
    edge_ref[0, 0, 1:2, :] = par_ref[0, 0, 0:1, :] - courant * dx(z_top) - half * par_ref[0, 2, 1:2, :]
    edge_ref[1, 0, 0:1, :] = m_bot
    edge_ref[1, 0, 1:2, :] = (
        par_ref[0, 0, rows - 1 : rows, :] - courant * dx(z_bot) + half * par_ref[0, 2, rows - 2 : rows - 1, :]
    )

    blocks = width // LANES
    count = span // LANES + 2
    first = lax.rem(col0 - 4 + width, width)
    block0 = first // LANES
    shift = first - block0 * LANES
    parts = [
        par_ref[0, :, :, pl.ds(pl.multiple_of(lax.rem(block0 + k, blocks) * LANES, LANES), LANES)]
        for k in range(count)
    ]
    wide = jnp.concatenate(parts, axis=-1).reshape(3 * rows, count * LANES)
    wide = pltpu.roll(wide, lax.rem(count * LANES - shift, count * LANES), 1)
    wide = wide[:, : span + LANES].reshape(3, rows, span + LANES)
    h, z, m = wide[0], wide[1], wide[2]
    a = h - courant * dx(z)
    b = keep * z - courant * dx(a) + rotation * m
    cc = keep * m - rotation * z
    shape = h.shape
    lane = iota(shape, 1)
    west = jnp.where(lane == 3, 2.0 / 3.0, 0.0) + jnp.where(lane == 4, 1.0 / 3.0, 0.0)
    east = jnp.where(lane == span + 3, 1.0 / 3.0, 0.0) + jnp.where(lane == span + 4, 2.0 / 3.0, 0.0)
    slot = iota((rows, LANES), 1)
    total = jnp.zeros((rows, LANES), jnp.float32)
    for q, field in enumerate((a, m, b, dx(m), cc)):
        for s, weight in enumerate((west, east)):
            value = jnp.sum(field * weight, axis=1, keepdims=True)
            total = total + jnp.where(slot == q * 16 + s + 2 * mem, value, 0.0)

    @pl.when(mem == 0)
    def _():
        strip_ref[...] = jnp.zeros_like(strip_ref)

    strip_ref[...] += total

    row = iota(shape, 0) + band * rows
    for end in range(2):
        near = row0 - 1 if end == 0 else row0 + span - 1
        lo, hi = (2.0 / 3.0, 1.0 / 3.0) if end == 0 else (1.0 / 3.0, 2.0 / 3.0)

        def w(i):
            return jnp.where(i == near, lo, 0.0) + jnp.where(i == near + 1, hi, 0.0)

        def u(i):
            return -half * (w(i - 1) - w(i + 1))

        wr, ur = w(row), u(row)
        vr = -half * (u(row - 1) - u(row + 1))
        h1 = jnp.sum(wr * a + ur * m, axis=0, keepdims=True)
        z1 = jnp.sum(wr * (keep * z + rotation * m), axis=0, keepdims=True) - courant * dx(h1)
        m1 = jnp.sum(wr * cc + ur * a + vr * m, axis=0, keepdims=True)
        for f, value in enumerate((h1, z1, m1)):
            ends_ref[end, f, pl.ds(mem, 1), :] = value


def nest_kernel(
    bands,
    span,
    off_ref,
    nest_ref,
    edge_ref,
    strip_ref,
    ends_ref,
    nest_out,
    patch,
    halo,
    ext,
    strips,
    endbuf,
    ghost,
    acc,
    coarse,
    dealt,
    cbuf,
    sbuf,
    nest_send,
    nest_recv,
    edge_send,
    edge_recv,
    strip_send,
    strip_recv,
    end_send,
    end_recv,
    mid_send,
    mid_recv,
    out_send,
    out_recv,
    local_sem,
):
    me = lax.axis_index("band")
    group = lax.axis_index("member")
    members, _, nrows, nwidth = nest_ref.shape
    prows = strip_ref.shape[0]
    tile = nrows // 3
    per = bands // members
    top_senders = bands // 2 + 1

    def remote(src, dst, send, recv, to):
        return pltpu.make_async_remote_copy(
            src_ref=src, dst_ref=dst, send_sem=send, recv_sem=recv, device_id=(group, to), device_id_type=MESH
        )

    barrier = pltpu.get_barrier_semaphore()

    def greet(j, _):
        pl.semaphore_signal(barrier, inc=1, device_id=(group, lax.rem(me + j, bands)), device_id_type=MESH)
        return 0

    lax.fori_loop(1, bands, greet, 0)
    own = pltpu.make_async_copy(nest_ref, ext.at[:, :, pl.ds(HALO, nrows), :], local_sem)
    own.start()
    pl.semaphore_wait(barrier, bands - 1)

    def nest_down(to):
        return remote(
            nest_ref.at[:, :, pl.ds(nrows - HALO, HALO), :], ext.at[:, :, pl.ds(0, HALO), :], nest_send.at[0], nest_recv.at[0], to
        )

    def nest_up(to):
        return remote(
            nest_ref.at[:, :, pl.ds(0, HALO), :],
            ext.at[:, :, pl.ds(HALO + nrows, HALO), :],
            nest_send.at[1],
            nest_recv.at[1],
            to,
        )

    def edge_down(to):
        return remote(edge_ref.at[1], halo.at[0], edge_send.at[0], edge_recv.at[0], to)

    def edge_up(to):
        return remote(edge_ref.at[0], halo.at[1], edge_send.at[1], edge_recv.at[1], to)

    def strip_copy(slot, to, index):
        return remote(strip_ref, strips.at[pl.ds(pl.multiple_of((slot + 1) * prows, prows), prows), :], strip_send.at[index], strip_recv.at[slot], to)

    def end_copy(end, slot, to):
        return remote(ends_ref.at[end], endbuf.at[slot], end_send.at[end], end_recv.at[slot], to)

    first, last = me == 0, me == bands - 1

    @pl.when(jnp.logical_not(first))
    def _():
        nest_up(me - 1).start()

    @pl.when(jnp.logical_not(last))
    def _():
        nest_down(me + 1).start()

    def send_strip(j, _):
        strip_copy(me, lax.rem(me + j, bands), j).start()
        return 0

    lax.fori_loop(1, bands, send_strip, 0)

    sends_top = jnp.logical_and(me > 0, me < top_senders)
    sends_bottom = jnp.logical_and(me < bands - 1, me >= bands - top_senders)

    @pl.when(sends_top)
    def _():
        end_copy(0, me, 0).start()

    @pl.when(sends_bottom)
    def _():
        end_copy(1, bands - 1 - me, bands - 1).start()

    @pl.when(jnp.logical_not(first))
    def _():
        edge_up(me - 1).start()

    @pl.when(jnp.logical_not(last))
    def _():
        edge_down(me + 1).start()

    pad = strips.shape[0] - (bands + 1) * prows
    strips[pl.ds(0, prows), :] = jnp.zeros((prows, LANES), jnp.float32)
    strips[pl.ds((bands + 1) * prows, pad), :] = jnp.zeros((pad, LANES), jnp.float32)
    strips[pl.ds(pl.multiple_of((me + 1) * prows, prows), prows), :] = strip_ref[...]
    cpad = (cbuf.shape[2] - bands * tile) // 2
    blank = jnp.zeros((span // LANES, 3, cpad, LANES), jnp.float32)
    cbuf[:, :, pl.ds(0, cpad), :] = blank
    cbuf[:, :, pl.ds(cpad + bands * tile, cpad), :] = blank

    def recv_strip(j, _):
        strip_copy(lax.rem(me + j, bands), me, j).wait_recv()
        return 0

    lax.fori_loop(1, bands, recv_strip, 0)

    g = strips[...]
    lane = iota((1, LANES), 1)
    turn = lane_roll(g, -16)
    height = g + jnp.where(lane < 16, -half, courant * half) * (row_roll(turn, -1) - row_roll(turn, 1))
    turn = lane_roll(height, 64)
    columns = jnp.where(lane < 64, height, g - half * (row_roll(turn, -1) - row_roll(turn, 1)))

    acc[...] = jnp.zeros_like(acc)

    def add_end(k, _):
        @pl.when(k > 0)
        def _():
            end_copy(0, k, 0).wait_recv()

        acc[...] += endbuf[k]
        return 0

    ends_lane = span + LANES

    @pl.when(first)
    def _():
        endbuf[0] = ends_ref[0]

    @pl.when(last)
    def _():
        endbuf[0] = ends_ref[1]

    @pl.when(jnp.logical_or(first, last))
    def _():
        lax.fori_loop(0, top_senders, add_end, 0)

    j = iota((ends_lane, nwidth), 1) + 2
    q, t = j // 3, j % 3
    k = iota((ends_lane, nwidth), 0) - 3
    fine = jnp.where(k == q, (3 - t).astype(jnp.float32) / 3.0, 0.0) + jnp.where(
        k == q + 1, t.astype(jnp.float32) / 3.0, 0.0
    )
    summed = acc[...].reshape(3 * members, ends_lane)
    ghost_rows = jnp.dot(summed, fine, precision=highest, preferred_element_type=jnp.float32)
    ghost[...] = ghost_rows.reshape(3, members, nwidth)

    own.wait()

    @pl.when(jnp.logical_not(first))
    def _():
        nest_down(me).wait_recv()

    @pl.when(jnp.logical_not(last))
    def _():
        nest_up(me).wait_recv()

    erows = nrows + 2 * HALO
    row = iota((erows, nwidth), 0)
    col = iota((erows, nwidth), 1)
    is_ghost = jnp.logical_or(
        jnp.logical_and(row == HALO - 1, first), jnp.logical_and(row == HALO + nrows, last)
    )
    at_west, at_east = col == 0, col == nwidth - 1
    total_rows = strips.shape[0]
    n = iota((erows, total_rows), 0) + (me * nrows - HALO + 2 + 9)
    wq, wt = n // 3 - 3, n % 3
    lower = (3 - wt).astype(jnp.float32) / 3.0
    upper = wt.astype(jnp.float32) / 3.0
    prow = iota((erows, total_rows), 1) - prows
    lanes = iota((erows, LANES), 1)
    pick_rows = iota((tile, erows), 1) - HALO
    pick = jnp.where(pick_rows // 3 == iota((tile, erows), 0), 1.0, 0.0)
    pick = jnp.where(pick_rows >= 0, pick, 0.0)

    def one_member(mem, _):
        row0 = off_ref[mem, 0]
        rel = prow - row0 + 1
        weights = jnp.where(rel == wq, lower, 0.0) + jnp.where(rel == wq + 1, upper, 0.0)
        side = jnp.dot(weights, columns, precision=highest, preferred_element_type=jnp.float32)

        def side_of(f, s):
            return jnp.sum(jnp.where(lanes == 32 * f + s + 2 * mem, side, 0.0), axis=1, keepdims=True)

        sides = [[side_of(f, s) for s in range(2)] for f in range(2)]
        ends = [ghost[f, pl.ds(mem, 1), :] for f in range(3)]

        def ddx(x, f):
            left = jnp.where(at_west, sides[f][0], lane_roll(x, 1))
            right = jnp.where(at_east, sides[f][1], lane_roll(x, -1))
            return right - left

        def ddy(x):
            return row_roll(x, -1) - row_roll(x, 1)

        def bound(x, f):
            return jnp.where(is_ghost, ends[f], x)

        h, z, m = ext[mem, 0], bound(ext[mem, 1], 1), bound(ext[mem, 2], 2)
        for _ in range(NSTEPS):
            h = bound(h - half * (ddx(z, 1) + ddy(m)), 0)
            z, m = (
                bound(keep * z - half * ddx(h, 0) + rotation * m, 1),
                bound(keep * m - half * ddy(h) - rotation * z, 2),
            )
        for f, x in enumerate((h, z, m)):
            nest_out[mem, f] = x[HALO : HALO + nrows]
            x = jnp.where(jnp.logical_and(row >= HALO, row < HALO + nrows), x, 0.0)
            coarse[mem, f, :, :] = jnp.dot(pick, x, precision=highest, preferred_element_type=jnp.float32)
        return 0

    lax.fori_loop(0, members, one_member, 0)

    thin = jnp.where(
        iota((nwidth, span), 0) // 3 == iota((nwidth, span), 1), 1.0 / 9.0, 0.0
    )
    block = coarse[...].reshape(members * 3 * tile, nwidth)
    means = jnp.dot(block, thin, precision=highest, preferred_element_type=jnp.float32)
    for k in range(0, span, LANES):
        dealt[:, k // LANES] = means[:, k : k + LANES].reshape(members, 3, tile, LANES)

    turn_of = lax.rem(group, per)

    def mid_copy(mem, slot, to):
        return remote(
            dealt.at[mem],
            cbuf.at[:, :, pl.ds(pl.multiple_of(cpad + slot * tile, tile), tile), :],
            mid_send.at[mem],
            mid_recv.at[slot],
            to,
        )

    def to_mid(mem, _):
        to = per * mem + turn_of

        @pl.when(to != me)
        def _():
            mid_copy(mem, me, to).start()

        @pl.when(to == me)
        def _():
            cbuf[:, :, pl.ds(pl.multiple_of(cpad + me * tile, tile), tile), :] = dealt[mem]

        return 0

    lax.fori_loop(0, members, to_mid, 0)
    is_mid = lax.rem(me, per) == turn_of
    mine = me // per

    def out_copy(to):
        return remote(sbuf.at[to], patch.at[mine], out_send.at[to], out_recv.at[mine], to)

    @pl.when(is_mid)
    def _():
        def recv(j, _):
            mid_copy(0, lax.rem(me + j, bands), me).wait_recv()
            return 0

        lax.fori_loop(1, bands, recv, 0)
        start_row = off_ref[mine, 0]

        def deal(j, _):
            to = lax.rem(me + j, bands)
            begin = jnp.clip(to * prows - start_row, -cpad, bands * tile) + cpad
            for k in range(0, span, LANES):
                sbuf[to, :, :, pl.ds(k, LANES)] = cbuf[k // LANES, :, pl.ds(begin, prows), :]

            @pl.when(to != me)
            def _():
                out_copy(to).start()

            return 0

        lax.fori_loop(1, bands + 1, deal, 0)
        patch[mine] = sbuf[me]

    def recv_patch(mem, _):
        @pl.when(per * mem + turn_of != me)
        def _():
            remote(sbuf.at[0], patch.at[mem], out_send.at[0], out_recv.at[mem], me).wait_recv()

        return 0

    lax.fori_loop(0, members, recv_patch, 0)

    @pl.when(jnp.logical_not(first))
    def _():
        edge_down(me).wait_recv()
        edge_up(me).wait_send()
        nest_up(me).wait_send()

    @pl.when(jnp.logical_not(last))
    def _():
        edge_up(me).wait_recv()
        edge_down(me).wait_send()
        nest_down(me).wait_send()

    @pl.when(sends_top)
    def _():
        end_copy(0, me, 0).wait_send()

    @pl.when(sends_bottom)
    def _():
        end_copy(1, bands - 1 - me, bands - 1).wait_send()

    def sent_strip(j, _):
        strip_copy(me, lax.rem(me + j, bands), j).wait_send()
        return 0

    lax.fori_loop(1, bands, sent_strip, 0)

    def sent_mid(mem, _):
        @pl.when(per * mem + turn_of != me)
        def _():
            mid_copy(mem, me, me).wait_send()

        return 0

    lax.fori_loop(0, members, sent_mid, 0)

    @pl.when(is_mid)
    def _():
        def sent_out(j, _):
            out_copy(lax.rem(me + j, bands)).wait_send()
            return 0

        lax.fori_loop(1, bands, sent_out, 0)


def parent_kernel(span, bands, off_ref, band_ref, par_ref, halo_ref, patch_ref, out_ref):
    mem = pl.program_id(0)
    rows, width = par_ref.shape[2], par_ref.shape[3]
    row0, col0 = off_ref[mem, 0], off_ref[mem, 1]
    band = band_ref[0]
    first, last = band == 0, band == bands - 1
    h, z, m = par_ref[0, 0], par_ref[0, 1], par_ref[0, 2]
    row = iota(h.shape, 0)

    def ddy(x, above, below):
        up = jnp.where(row == 0, above, row_roll(x, 1))
        down = jnp.where(row == rows - 1, below, row_roll(x, -1))
        return down - up

    m_above = jnp.where(first, 0.0, halo_ref[0, 0, 0:1, :])
    m_below = jnp.where(last, 0.0, halo_ref[1, 0, 0:1, :])
    h_above = jnp.where(first, 0.0, halo_ref[0, 0, 1:2, :] - half * m[0:1])
    h_below = jnp.where(last, 0.0, halo_ref[1, 0, 1:2, :] + half * m[rows - 1 : rows])
    h1 = h - courant * dx(z) - half * ddy(m, m_above, m_below)
    out_ref[0, 0] = h1
    out_ref[0, 1] = keep * z - courant * dx(h1) + rotation * m
    out_ref[0, 2] = keep * m - half * ddy(h1, h_above, h_below) - rotation * z

    block0 = col0 // LANES
    shift = col0 - block0 * LANES
    place = pl.ds(pl.multiple_of(block0 * LANES, LANES), span + LANES)
    wide = jnp.concatenate([patch_ref[0], jnp.zeros((3, rows, LANES), jnp.float32)], axis=-1)
    wide = pltpu.roll(wide.reshape(3 * rows, span + LANES), shift, 1).reshape(3, rows, span + LANES)
    lane = iota(wide.shape, 2)
    at = iota(wide.shape, 1) + (band * rows - row0)
    inside = (lane >= shift) & (lane < shift + span) & (at >= 0) & (at < span)
    out_ref[0, :, :, place] = jnp.where(inside, wide, out_ref[0, :, :, place])


def per_device(bands, parent_state, nest_state, offsets):
    members, _, prows, width = parent_state.shape
    nrows, nwidth = nest_state.shape[2:]
    span = nwidth // 3
    tile = nrows // 3
    f32 = jnp.float32
    band = lax.axis_index("band").reshape(1).astype(jnp.int32)
    shape = jax.ShapeDtypeStruct
    limit = 48 * 1024 * 1024
    parent_spec = pl.BlockSpec((1, 3, prows, width), lambda i, *_: (i, 0, 0, 0))
    edge_spec = pl.BlockSpec((2, 1, 2, width), lambda i, *_: (0, i, 0, 0))

    edges, strip, ends = pl.pallas_call(
        functools.partial(gather_kernel, span, bands),
        out_shape=(
            shape((2, members, 2, width), f32),
            shape((prows, LANES), f32),
            shape((2, 3, members, span + LANES), f32),
        ),
        grid_spec=pltpu.PrefetchScalarGridSpec(
            num_scalar_prefetch=2,
            grid=(members,),
            in_specs=[parent_spec],
            out_specs=(
                edge_spec,
                pl.BlockSpec((prows, LANES), lambda i, *_: (0, 0)),
                pl.BlockSpec((2, 3, members, span + LANES), lambda i, *_: (0, 0, 0, 0)),
            ),
        ),
        compiler_params=pltpu.CompilerParams(vmem_limit_bytes=limit),
        name="gather",
    )(offsets, band, parent_state)

    vmem = pl.BlockSpec(memory_space=pltpu.VMEM)
    hbm = pl.BlockSpec(memory_space=pl.ANY)
    dma = pltpu.SemaphoreType.DMA
    senders = bands // 2 + 1
    nest_out, patch, halo = pl.pallas_call(
        functools.partial(nest_kernel, bands, span),
        out_shape=(
            shape(nest_state.shape, f32),
            shape((members, 3, prows, span), f32),
            shape((2, members, 2, width), f32),
        ),
        in_specs=[pl.BlockSpec(memory_space=pltpu.SMEM), hbm, hbm, vmem, vmem],
        out_specs=(vmem, vmem, hbm),
        scratch_shapes=[
            pltpu.VMEM((members, 3, nrows + 2 * HALO, nwidth), f32),
            pltpu.VMEM(((bands + 2) * prows, LANES), f32),
            pltpu.VMEM((senders, 3, members, span + LANES), f32),
            pltpu.VMEM((3, members, nwidth), f32),
            pltpu.VMEM((3, members, span + LANES), f32),
            pltpu.VMEM((members, 3, tile, nwidth), f32),
            pltpu.VMEM((members, span // LANES, 3, tile, LANES), f32),
            pltpu.VMEM((span // LANES, 3, bands * tile + 2 * prows, LANES), f32),
            pltpu.VMEM((bands, 3, prows, span), f32),
            dma((2,)),
            dma((2,)),
            dma((2,)),
            dma((2,)),
            dma((bands,)),
            dma((bands,)),
            dma((2,)),
            dma((senders,)),
            dma((members,)),
            dma((bands,)),
            dma((bands,)),
            dma((members,)),
            dma,
        ],
        compiler_params=pltpu.CompilerParams(collective_id=0, has_side_effects=True, vmem_limit_bytes=limit),
        name="nest",
    )(offsets, nest_state, edges, strip, ends)

    parent_out = pl.pallas_call(
        functools.partial(parent_kernel, span, bands),
        out_shape=shape(parent_state.shape, f32),
        grid_spec=pltpu.PrefetchScalarGridSpec(
            num_scalar_prefetch=2,
            grid=(members,),
            in_specs=[
                parent_spec,
                edge_spec,
                pl.BlockSpec((1, 3, prows, span), lambda i, *_: (i, 0, 0, 0)),
            ],
            out_specs=parent_spec,
        ),
        compiler_params=pltpu.CompilerParams(vmem_limit_bytes=limit),
        name="parent",
    )(offsets, band, parent_state, halo, patch)
    return (parent_out, nest_out)


def solution(mesh):
    in_specs = (P("member", None, "band", None), P("member", None, "band", None), P("member", None))
    out_specs = (P("member", None, "band", None), P("member", None, "band", None))
    return jax.shard_map(
        functools.partial(per_device, mesh.shape["band"]),
        mesh=mesh,
        in_specs=in_specs,
        out_specs=out_specs,
        check_vma=False,
    )
```

```python
import functools

import jax
import jax.numpy as jnp
from jax import lax
from jax.experimental import pallas as pl
from jax.experimental.pallas import tpu as pltpu
from jax.sharding import PartitionSpec as P

NSTEPS = 3
MESH = pl.DeviceIdType.MESH

courant = 0.9
friction = 0.02
rotation = 0.05
half = 0.5 * courant
keep = 1.0 - friction
highest = lax.Precision.HIGHEST
LANES = 128
HALO = 8


def lane_roll(x, shift):
    size = x.shape[-1]
    return pltpu.roll(x, shift % size, x.ndim - 1)


def row_roll(x, shift):
    size = x.shape[-2]
    return pltpu.roll(x, shift % size, x.ndim - 2)


def dx(x):
    return 0.5 * (lane_roll(x, -1) - lane_roll(x, 1))


def iota(shape, dim):
    return lax.broadcasted_iota(jnp.int32, shape, dim)


def split(x):
    high = x.astype(jnp.bfloat16)
    rest = x - high.astype(jnp.float32)
    mid = rest.astype(jnp.bfloat16)
    return high, mid, (rest - mid.astype(jnp.float32)).astype(jnp.bfloat16)


def exact_dot(x, weights):
    return sum(jnp.dot(part, weights, preferred_element_type=jnp.float32) for part in split(x))


def gather_kernel(span, bands, off_ref, band_ref, par_ref, edge_ref, strip_ref, ends_ref):
    mem = pl.program_id(0)
    rows, width = par_ref.shape[2], par_ref.shape[3]
    row0, col0 = off_ref[mem, 0], off_ref[mem, 1]
    band = band_ref[0]

    z_top, z_bot = par_ref[0, 1, 0:1, :], par_ref[0, 1, rows - 1 : rows, :]
    m_top, m_bot = par_ref[0, 2, 0:1, :], par_ref[0, 2, rows - 1 : rows, :]
    edge_ref[0, 0, 0:1, :] = m_top
    edge_ref[0, 0, 1:2, :] = par_ref[0, 0, 0:1, :] - courant * dx(z_top) - half * par_ref[0, 2, 1:2, :]
    edge_ref[1, 0, 0:1, :] = m_bot
    edge_ref[1, 0, 1:2, :] = (
        par_ref[0, 0, rows - 1 : rows, :] - courant * dx(z_bot) + half * par_ref[0, 2, rows - 2 : rows - 1, :]
    )

    blocks = width // LANES
    count = span // LANES + 2
    first = lax.rem(col0 - 4 + width, width)
    block0 = first // LANES
    shift = first - block0 * LANES
    parts = [
        par_ref[0, :, :, pl.ds(pl.multiple_of(lax.rem(block0 + k, blocks) * LANES, LANES), LANES)]
        for k in range(count)
    ]
    wide = jnp.concatenate(parts, axis=-1).reshape(3 * rows, count * LANES)
    wide = pltpu.roll(wide, lax.rem(count * LANES - shift, count * LANES), 1)
    wide = wide[:, : span + LANES].reshape(3, rows, span + LANES)
    h, z, m = wide[0], wide[1], wide[2]
    a = h - courant * dx(z)
    b = keep * z - courant * dx(a) + rotation * m
    cc = keep * m - rotation * z
    shape = h.shape
    lane = iota(shape, 1)
    west = jnp.where(lane == 3, 2.0 / 3.0, 0.0) + jnp.where(lane == 4, 1.0 / 3.0, 0.0)
    east = jnp.where(lane == span + 3, 1.0 / 3.0, 0.0) + jnp.where(lane == span + 4, 2.0 / 3.0, 0.0)
    slot = iota((rows, LANES), 1)
    total = jnp.zeros((rows, LANES), jnp.float32)
    for q, field in enumerate((a, m, b, dx(m), cc)):
        for s, weight in enumerate((west, east)):
            value = jnp.sum(field * weight, axis=1, keepdims=True)
            total = total + jnp.where(slot == q * 16 + s + 2 * mem, value, 0.0)

    @pl.when(mem == 0)
    def _():
        strip_ref[...] = jnp.zeros_like(strip_ref)

    strip_ref[...] += total

    row = iota(shape, 0) + band * rows
    for end in range(2):
        near = row0 - 1 if end == 0 else row0 + span - 1
        lo, hi = (2.0 / 3.0, 1.0 / 3.0) if end == 0 else (1.0 / 3.0, 2.0 / 3.0)

        def w(i):
            return jnp.where(i == near, lo, 0.0) + jnp.where(i == near + 1, hi, 0.0)

        def u(i):
            return -half * (w(i - 1) - w(i + 1))

        wr, ur = w(row), u(row)
        vr = -half * (u(row - 1) - u(row + 1))
        h1 = jnp.sum(wr * a + ur * m, axis=0, keepdims=True)
        z1 = jnp.sum(wr * (keep * z + rotation * m), axis=0, keepdims=True) - courant * dx(h1)
        m1 = jnp.sum(wr * cc + ur * a + vr * m, axis=0, keepdims=True)
        for f, value in enumerate((h1, z1, m1)):
            ends_ref[end, f, pl.ds(mem, 1), :] = value


def nest_kernel(
    bands,
    span,
    off_ref,
    nest_ref,
    edge_ref,
    strip_ref,
    ends_ref,
    nest_out,
    patch,
    halo,
    ext,
    strips,
    endbuf,
    cols,
    side,
    ghost,
    acc,
    fine,
    thinned,
    dealt,
    cbuf,
    sbuf,
    nest_send,
    nest_recv,
    edge_send,
    edge_recv,
    strip_send,
    strip_recv,
    end_send,
    end_recv,
    mid_send,
    mid_recv,
    out_send,
    out_recv,
    local_sem,
):
    me = lax.axis_index("band")
    group = lax.axis_index("member")
    members, _, nrows, nwidth = nest_ref.shape
    prows = strip_ref.shape[0]
    tile = nrows // 3
    per = bands // members
    top_senders = bands // 2 + 1

    def remote(src, dst, send, recv, to):
        return pltpu.make_async_remote_copy(
            src_ref=src, dst_ref=dst, send_sem=send, recv_sem=recv, device_id=(group, to), device_id_type=MESH
        )

    barrier = pltpu.get_barrier_semaphore()

    def greet(j, _):
        pl.semaphore_signal(barrier, inc=1, device_id=(group, lax.rem(me + j, bands)), device_id_type=MESH)
        return 0

    lax.fori_loop(1, bands, greet, 0)
    own = pltpu.make_async_copy(nest_ref, ext.at[:, :, pl.ds(HALO, nrows), :], local_sem)
    own.start()
    pl.semaphore_wait(barrier, bands - 1)

    reach = 2 * NSTEPS

    def nest_down(mem, to):
        return remote(
            nest_ref.at[mem, :, pl.ds(nrows - reach, reach), :],
            ext.at[mem, :, pl.ds(HALO - reach, reach), :],
            nest_send.at[0, mem],
            nest_recv.at[0, mem],
            to,
        )

    def nest_up(mem, to):
        return remote(
            nest_ref.at[mem, :, pl.ds(0, reach), :],
            ext.at[mem, :, pl.ds(HALO + nrows, reach), :],
            nest_send.at[1, mem],
            nest_recv.at[1, mem],
            to,
        )

    def edge_down(to):
        return remote(edge_ref.at[1], halo.at[0], edge_send.at[0], edge_recv.at[0], to)

    def edge_up(to):
        return remote(edge_ref.at[0], halo.at[1], edge_send.at[1], edge_recv.at[1], to)

    def strip_copy(slot, to, index):
        return remote(strip_ref, strips.at[pl.ds(pl.multiple_of((slot + 1) * prows, prows), prows), :], strip_send.at[index], strip_recv.at[slot], to)

    def end_copy(end, slot, to):
        return remote(ends_ref.at[end], endbuf.at[slot], end_send.at[end], end_recv.at[slot], to)

    first, last = me == 0, me == bands - 1

    def send_strip(j, _):
        strip_copy(me, lax.rem(me + j, bands), j).start()
        return 0

    lax.fori_loop(1, bands, send_strip, 0)

    sends_top = jnp.logical_and(me > 0, me < top_senders)
    sends_bottom = jnp.logical_and(me < bands - 1, me >= bands - top_senders)

    @pl.when(sends_top)
    def _():
        end_copy(0, me, 0).start()

    @pl.when(sends_bottom)
    def _():
        end_copy(1, bands - 1 - me, bands - 1).start()

    def send_nest(mem, _):
        @pl.when(jnp.logical_not(first))
        def _():
            nest_up(mem, me - 1).start()

        @pl.when(jnp.logical_not(last))
        def _():
            nest_down(mem, me + 1).start()

        return 0

    lax.fori_loop(0, members, send_nest, 0)

    @pl.when(jnp.logical_not(first))
    def _():
        edge_up(me - 1).start()

    @pl.when(jnp.logical_not(last))
    def _():
        edge_down(me + 1).start()

    pad = strips.shape[0] - (bands + 1) * prows
    strips[pl.ds(0, prows), :] = jnp.zeros((prows, LANES), jnp.float32)
    strips[pl.ds((bands + 1) * prows, pad), :] = jnp.zeros((pad, LANES), jnp.float32)
    strips[pl.ds(pl.multiple_of((me + 1) * prows, prows), prows), :] = strip_ref[...]
    cpad = (cbuf.shape[2] - bands * tile) // 2
    blank = jnp.zeros((span // LANES, 3, cpad, LANES), jnp.float32)
    cbuf[:, :, pl.ds(0, cpad), :] = blank
    cbuf[:, :, pl.ds(cpad + bands * tile, cpad), :] = blank

    ends_lane = span + LANES

    @pl.when(jnp.logical_or(first, last))
    def _():
        j = iota((1, nwidth), 1) + 2
        q, t = j // 3, j % 3
        k = iota((ends_lane, nwidth), 0) - 3
        fine[...] = (jnp.where(k == q, 3 - t, 0) + jnp.where(k == q + 1, t, 0)).astype(jnp.float32).astype(jnp.bfloat16)

    erows = nrows + 2 * HALO
    e = iota((erows, prows), 0)
    q, t = e // 3, e % 3
    k = iota((erows, prows), 1)
    weights = jnp.where(k == q, (3 - t).astype(jnp.float32) / 3.0, 0.0) + jnp.where(
        k == q + 1, t.astype(jnp.float32) / 3.0, 0.0
    )
    thin = jnp.where(iota((nwidth, span), 0) // 3 == iota((nwidth, span), 1), 1.0, 0.0).astype(jnp.bfloat16)
    row = iota((erows, nwidth), 0)
    col = iota((erows, nwidth), 1)
    is_ghost = jnp.logical_or(
        jnp.logical_and(row == HALO - 1, first), jnp.logical_and(row == HALO + nrows, last)
    )
    at_west, at_east = col == 0, col == nwidth - 1
    lanes = iota((erows, LANES), 1)

    def recv_strip(j, _):
        strip_copy(lax.rem(me + j, bands), me, j).wait_recv()
        return 0

    lax.fori_loop(1, bands, recv_strip, 0)

    g = strips[...]
    lane = iota((1, LANES), 1)
    turn = lane_roll(g, -16)
    height = g + jnp.where(lane < 16, -half, courant * half) * (row_roll(turn, -1) - row_roll(turn, 1))
    turn = lane_roll(height, 64)
    cols[...] = jnp.where(lane < 64, height, g - half * (row_roll(turn, -1) - row_roll(turn, 1)))
    picked = jnp.zeros((prows, LANES), jnp.float32)
    for mem in range(members):
        begin = off_ref[mem, 0] + (me * tile - 3 + prows)
        picked = jnp.where(lane % 32 // 2 == mem, cols[pl.ds(begin, prows), :], picked)
    side[...] = jnp.dot(weights, picked, precision=highest, preferred_element_type=jnp.float32)


    def add_end(k, _):
        @pl.when(k > 0)
        def _():
            end_copy(0, k, 0).wait_recv()

        acc[...] += endbuf[k]
        return 0

    @pl.when(first)
    def _():
        endbuf[0] = ends_ref[0]

    @pl.when(last)
    def _():
        endbuf[0] = ends_ref[1]

    @pl.when(jnp.logical_or(first, last))
    def _():
        acc[...] = jnp.zeros_like(acc)
        lax.fori_loop(0, top_senders, add_end, 0)
        rows_in = acc[...].reshape(3 * members, ends_lane)
        ghost[...] = (exact_dot(rows_in, fine[...]) * (1.0 / 3.0)).reshape(3, members, nwidth)

    own.wait()

    turn_of = lax.rem(group, per)

    def mid_copy(mem, slot, to):
        return remote(
            dealt.at[mem],
            cbuf.at[:, :, pl.ds(pl.multiple_of(cpad + slot * tile, tile), tile), :],
            mid_send.at[mem],
            mid_recv.at[slot],
            to,
        )

    def one_member(mem, _):
        @pl.when(jnp.logical_not(first))
        def _():
            nest_down(mem, me).wait_recv()

        @pl.when(jnp.logical_not(last))
        def _():
            nest_up(mem, me).wait_recv()

        def side_of(f, s):
            return jnp.sum(jnp.where(lanes == 32 * f + s + 2 * mem, side[...], 0.0), axis=1, keepdims=True)

        sides = [[side_of(f, s) for s in range(2)] for f in range(2)]
        ends = [ghost[f, pl.ds(mem, 1), :] for f in range(3)]

        def ddx(x, f):
            left = jnp.where(at_west, sides[f][0], lane_roll(x, 1))
            right = jnp.where(at_east, sides[f][1], lane_roll(x, -1))
            return right - left

        def ddy(x):
            return row_roll(x, -1) - row_roll(x, 1)

        def bound(x, f):
            return jnp.where(is_ghost, ends[f], x)

        h, z, m = ext[mem, 0], bound(ext[mem, 1], 1), bound(ext[mem, 2], 2)
        for _ in range(NSTEPS):
            h = bound(h - half * (ddx(z, 1) + ddy(m)), 0)
            z, m = (
                bound(keep * z - half * ddx(h, 0) + rotation * m, 1),
                bound(keep * m - half * ddy(h) - rotation * z, 2),
            )
        inner = [x[HALO : HALO + nrows] for x in (h, z, m)]
        for f, x in enumerate(inner):
            nest_out[mem, f] = x
        sums = exact_dot(jnp.concatenate(inner, axis=0), thin)
        for k in range(span // LANES):
            thinned[k] = sums[:, k * LANES : (k + 1) * LANES]
            for f in range(3):
                parts = [thinned[k, pl.ds(f * nrows + i, tile, stride=3), :] for i in range(3)]
                dealt[mem, k, f] = (parts[0] + parts[1] + parts[2]) * (1.0 / 9.0)
        to = per * mem + turn_of

        @pl.when(to != me)
        def _():
            mid_copy(mem, me, to).start()

        @pl.when(to == me)
        def _():
            cbuf[:, :, pl.ds(pl.multiple_of(cpad + me * tile, tile), tile), :] = dealt[mem]

        return 0

    lax.fori_loop(0, members, one_member, 0)
    is_mid = lax.rem(me, per) == turn_of
    mine = me // per

    def out_copy(to):
        return remote(sbuf.at[to], patch.at[mine], out_send.at[to], out_recv.at[mine], to)

    @pl.when(is_mid)
    def _():
        def recv(j, _):
            mid_copy(0, lax.rem(me + j, bands), me).wait_recv()
            return 0

        lax.fori_loop(1, bands, recv, 0)
        start_row = off_ref[mine, 0]

        def deal(j, _):
            to = lax.rem(me + j, bands)
            begin = jnp.clip(to * prows - start_row, -cpad, bands * tile) + cpad
            for k in range(0, span, LANES):
                sbuf[to, :, :, pl.ds(k, LANES)] = cbuf[k // LANES, :, pl.ds(begin, prows), :]

            @pl.when(to != me)
            def _():
                out_copy(to).start()

            return 0

        lax.fori_loop(1, bands + 1, deal, 0)
        patch[mine] = sbuf[me]

    def recv_patch(mem, _):
        @pl.when(per * mem + turn_of != me)
        def _():
            remote(sbuf.at[0], patch.at[mem], out_send.at[0], out_recv.at[mem], me).wait_recv()

        return 0

    lax.fori_loop(0, members, recv_patch, 0)

    @pl.when(jnp.logical_not(first))
    def _():
        edge_down(me).wait_recv()
        edge_up(me).wait_send()

    @pl.when(jnp.logical_not(last))
    def _():
        edge_up(me).wait_recv()
        edge_down(me).wait_send()

    @pl.when(sends_top)
    def _():
        end_copy(0, me, 0).wait_send()

    @pl.when(sends_bottom)
    def _():
        end_copy(1, bands - 1 - me, bands - 1).wait_send()

    def sent_strip(j, _):
        strip_copy(me, lax.rem(me + j, bands), j).wait_send()
        return 0

    lax.fori_loop(1, bands, sent_strip, 0)

    def sent_mid(mem, _):
        @pl.when(jnp.logical_not(first))
        def _():
            nest_up(mem, me).wait_send()

        @pl.when(jnp.logical_not(last))
        def _():
            nest_down(mem, me).wait_send()

        @pl.when(per * mem + turn_of != me)
        def _():
            mid_copy(mem, me, me).wait_send()

        return 0

    lax.fori_loop(0, members, sent_mid, 0)

    @pl.when(is_mid)
    def _():
        def sent_out(j, _):
            out_copy(lax.rem(me + j, bands)).wait_send()
            return 0

        lax.fori_loop(1, bands, sent_out, 0)


def parent_kernel(span, bands, off_ref, band_ref, par_ref, halo_ref, patch_ref, out_ref):
    mem = pl.program_id(0)
    rows, width = par_ref.shape[2], par_ref.shape[3]
    row0, col0 = off_ref[mem, 0], off_ref[mem, 1]
    band = band_ref[0]
    first, last = band == 0, band == bands - 1
    h, z, m = par_ref[0, 0], par_ref[0, 1], par_ref[0, 2]
    row = iota(h.shape, 0)

    def ddy(x, above, below):
        up = jnp.where(row == 0, above, row_roll(x, 1))
        down = jnp.where(row == rows - 1, below, row_roll(x, -1))
        return down - up

    m_above = jnp.where(first, 0.0, halo_ref[0, 0, 0:1, :])
    m_below = jnp.where(last, 0.0, halo_ref[1, 0, 0:1, :])
    h_above = jnp.where(first, 0.0, halo_ref[0, 0, 1:2, :] - half * m[0:1])
    h_below = jnp.where(last, 0.0, halo_ref[1, 0, 1:2, :] + half * m[rows - 1 : rows])
    h1 = h - courant * dx(z) - half * ddy(m, m_above, m_below)
    out_ref[0, 0] = h1
    out_ref[0, 1] = keep * z - courant * dx(h1) + rotation * m
    out_ref[0, 2] = keep * m - half * ddy(h1, h_above, h_below) - rotation * z

    block0 = col0 // LANES
    shift = col0 - block0 * LANES
    place = pl.ds(pl.multiple_of(block0 * LANES, LANES), span + LANES)
    wide = jnp.concatenate([patch_ref[0], jnp.zeros((3, rows, LANES), jnp.float32)], axis=-1)
    wide = pltpu.roll(wide.reshape(3 * rows, span + LANES), shift, 1).reshape(3, rows, span + LANES)
    lane = iota(wide.shape, 2)
    at = iota(wide.shape, 1) + (band * rows - row0)
    inside = (lane >= shift) & (lane < shift + span) & (at >= 0) & (at < span)
    out_ref[0, :, :, place] = jnp.where(inside, wide, out_ref[0, :, :, place])


def per_device(bands, parent_state, nest_state, offsets):
    members, _, prows, width = parent_state.shape
    nrows, nwidth = nest_state.shape[2:]
    span = nwidth // 3
    tile = nrows // 3
    f32 = jnp.float32
    band = lax.axis_index("band").reshape(1).astype(jnp.int32)
    shape = jax.ShapeDtypeStruct
    limit = 48 * 1024 * 1024
    parent_spec = pl.BlockSpec((1, 3, prows, width), lambda i, *_: (i, 0, 0, 0))
    edge_spec = pl.BlockSpec((2, 1, 2, width), lambda i, *_: (0, i, 0, 0))

    edges, strip, ends = pl.pallas_call(
        functools.partial(gather_kernel, span, bands),
        out_shape=(
            shape((2, members, 2, width), f32),
            shape((prows, LANES), f32),
            shape((2, 3, members, span + LANES), f32),
        ),
        grid_spec=pltpu.PrefetchScalarGridSpec(
            num_scalar_prefetch=2,
            grid=(members,),
            in_specs=[parent_spec],
            out_specs=(
                edge_spec,
                pl.BlockSpec((prows, LANES), lambda i, *_: (0, 0)),
                pl.BlockSpec((2, 3, members, span + LANES), lambda i, *_: (0, 0, 0, 0)),
            ),
        ),
        compiler_params=pltpu.CompilerParams(vmem_limit_bytes=limit),
        name="gather",
    )(offsets, band, parent_state)

    vmem = pl.BlockSpec(memory_space=pltpu.VMEM)
    hbm = pl.BlockSpec(memory_space=pl.ANY)
    dma = pltpu.SemaphoreType.DMA
    senders = bands // 2 + 1
    nest_out, patch, halo = pl.pallas_call(
        functools.partial(nest_kernel, bands, span),
        out_shape=(
            shape(nest_state.shape, f32),
            shape((members, 3, prows, span), f32),
            shape((2, members, 2, width), f32),
        ),
        in_specs=[pl.BlockSpec(memory_space=pltpu.SMEM), hbm, hbm, vmem, vmem],
        out_specs=(vmem, vmem, hbm),
        scratch_shapes=[
            pltpu.VMEM((members, 3, nrows + 2 * HALO, nwidth), f32),
            pltpu.VMEM(((bands + 2) * prows, LANES), f32),
            pltpu.VMEM((senders, 3, members, span + LANES), f32),
            pltpu.VMEM(((bands + 2) * prows, LANES), f32),
            pltpu.VMEM((nrows + 2 * HALO, LANES), f32),
            pltpu.VMEM((3, members, nwidth), f32),
            pltpu.VMEM((3, members, span + LANES), f32),
            pltpu.VMEM((span + LANES, nwidth), jnp.bfloat16),
            pltpu.VMEM((span // LANES, 3 * nrows, LANES), f32),
            pltpu.VMEM((members, span // LANES, 3, tile, LANES), f32),
            pltpu.VMEM((span // LANES, 3, bands * tile + 2 * prows, LANES), f32),
            pltpu.VMEM((bands, 3, prows, span), f32),
            dma((2, members)),
            dma((2, members)),
            dma((2,)),
            dma((2,)),
            dma((bands,)),
            dma((bands,)),
            dma((2,)),
            dma((senders,)),
            dma((members,)),
            dma((bands,)),
            dma((bands,)),
            dma((members,)),
            dma,
        ],
        compiler_params=pltpu.CompilerParams(collective_id=0, has_side_effects=True, vmem_limit_bytes=limit),
        name="nest",
    )(offsets, nest_state, edges, strip, ends)

    parent_out = pl.pallas_call(
        functools.partial(parent_kernel, span, bands),
        out_shape=shape(parent_state.shape, f32),
        grid_spec=pltpu.PrefetchScalarGridSpec(
            num_scalar_prefetch=2,
            grid=(members,),
            in_specs=[
                parent_spec,
                edge_spec,
                pl.BlockSpec((1, 3, prows, span), lambda i, *_: (i, 0, 0, 0)),
            ],
            out_specs=parent_spec,
        ),
        compiler_params=pltpu.CompilerParams(vmem_limit_bytes=limit),
        name="parent",
    )(offsets, band, parent_state, halo, patch)
    return (parent_out, nest_out)


def solution(mesh):
    in_specs = (P("member", None, "band", None), P("member", None, "band", None), P("member", None))
    out_specs = (P("member", None, "band", None), P("member", None, "band", None))
    return jax.shard_map(
        functools.partial(per_device, mesh.shape["band"]),
        mesh=mesh,
        in_specs=in_specs,
        out_specs=out_specs,
        check_vma=False,
    )
```

```python
import functools

import jax
import jax.numpy as jnp
from jax import lax
from jax.experimental import pallas as pl
from jax.experimental.pallas import tpu as pltpu
from jax.sharding import PartitionSpec as P

NSTEPS = 3
MESH = pl.DeviceIdType.MESH

courant = 0.9
friction = 0.02
rotation = 0.05
half = 0.5 * courant
keep = 1.0 - friction
highest = lax.Precision.HIGHEST
LANES = 128


def lane_roll(x, shift):
    size = x.shape[-1]
    return pltpu.roll(x, shift % size, x.ndim - 1)


def row_roll(x, shift):
    size = x.shape[-2]
    return pltpu.roll(x, shift % size, x.ndim - 2)


def dx(x):
    return 0.5 * (lane_roll(x, -1) - lane_roll(x, 1))


def iota(shape, dim):
    return lax.broadcasted_iota(jnp.int32, shape, dim)


def split(x):
    high = x.astype(jnp.bfloat16)
    rest = x - high.astype(jnp.float32)
    mid = rest.astype(jnp.bfloat16)
    return high, mid, (rest - mid.astype(jnp.float32)).astype(jnp.bfloat16)


def exact_dot(x, weights):
    return sum(jnp.dot(part, weights, preferred_element_type=jnp.float32) for part in split(x))


def gather_kernel(span, bands, off_ref, band_ref, par_ref, edge_ref, strip_ref, ends_ref):
    mem = pl.program_id(0)
    rows, width = par_ref.shape[2], par_ref.shape[3]
    row0, col0 = off_ref[mem, 0], off_ref[mem, 1]
    band = band_ref[0]

    z_top, z_bot = par_ref[0, 1, 0:1, :], par_ref[0, 1, rows - 1 : rows, :]
    m_top, m_bot = par_ref[0, 2, 0:1, :], par_ref[0, 2, rows - 1 : rows, :]
    edge_ref[0, 0, 0:1, :] = m_top
    edge_ref[0, 0, 1:2, :] = par_ref[0, 0, 0:1, :] - courant * dx(z_top) - half * par_ref[0, 2, 1:2, :]
    edge_ref[1, 0, 0:1, :] = m_bot
    edge_ref[1, 0, 1:2, :] = (
        par_ref[0, 0, rows - 1 : rows, :] - courant * dx(z_bot) + half * par_ref[0, 2, rows - 2 : rows - 1, :]
    )

    blocks = width // LANES
    count = span // LANES + 2
    first = lax.rem(col0 - 4 + width, width)
    block0 = first // LANES
    shift = first - block0 * LANES
    parts = [
        par_ref[0, :, :, pl.ds(pl.multiple_of(lax.rem(block0 + k, blocks) * LANES, LANES), LANES)]
        for k in range(count)
    ]
    wide = jnp.concatenate(parts, axis=-1).reshape(3 * rows, count * LANES)
    wide = pltpu.roll(wide, lax.rem(count * LANES - shift, count * LANES), 1)
    wide = wide[:, : span + LANES].reshape(3, rows, span + LANES)
    h, z, m = wide[0], wide[1], wide[2]
    a = h - courant * dx(z)
    b = keep * z - courant * dx(a) + rotation * m
    cc = keep * m - rotation * z
    shape = h.shape
    lane = iota(shape, 1)
    west = jnp.where(lane == 3, 2.0 / 3.0, 0.0) + jnp.where(lane == 4, 1.0 / 3.0, 0.0)
    east = jnp.where(lane == span + 3, 1.0 / 3.0, 0.0) + jnp.where(lane == span + 4, 2.0 / 3.0, 0.0)
    slot = iota((rows, LANES), 1)
    total = jnp.zeros((rows, LANES), jnp.float32)
    for q, field in enumerate((a, m, b, dx(m), cc)):
        for s, weight in enumerate((west, east)):
            value = jnp.sum(field * weight, axis=1, keepdims=True)
            total = total + jnp.where(slot == q * 16 + s + 2 * mem, value, 0.0)

    @pl.when(mem == 0)
    def _():
        strip_ref[...] = jnp.zeros_like(strip_ref)

    strip_ref[...] += total

    row = iota(shape, 0) + band * rows
    for end in range(2):
        near = row0 - 1 if end == 0 else row0 + span - 1
        lo, hi = (2.0 / 3.0, 1.0 / 3.0) if end == 0 else (1.0 / 3.0, 2.0 / 3.0)

        def w(i):
            return jnp.where(i == near, lo, 0.0) + jnp.where(i == near + 1, hi, 0.0)

        def u(i):
            return -half * (w(i - 1) - w(i + 1))

        wr, ur = w(row), u(row)
        vr = -half * (u(row - 1) - u(row + 1))
        h1 = jnp.sum(wr * a + ur * m, axis=0, keepdims=True)
        z1 = jnp.sum(wr * (keep * z + rotation * m), axis=0, keepdims=True) - courant * dx(h1)
        m1 = jnp.sum(wr * cc + ur * a + vr * m, axis=0, keepdims=True)
        for f, value in enumerate((h1, z1, m1)):
            ends_ref[end, f, pl.ds(mem, 1), :] = value


def nest_kernel(
    bands,
    span,
    off_ref,
    nest_ref,
    edge_ref,
    strip_ref,
    ends_ref,
    nest_out,
    patch,
    halo,
    given,
    taken,
    known,
    strips,
    endbuf,
    cols,
    sides,
    ghost,
    acc,
    fine,
    thinned,
    dealt,
    cbuf,
    sbuf,
    nest_send,
    nest_recv,
    edge_send,
    edge_recv,
    strip_send,
    strip_recv,
    end_send,
    end_recv,
    mid_send,
    mid_recv,
    out_send,
    out_recv,
    local_sem,
):
    me = lax.axis_index("band")
    group = lax.axis_index("member")
    members, _, nrows, nwidth = nest_ref.shape
    prows = strip_ref.shape[0]
    tile = nrows // 3
    per = bands // members
    top_senders = bands // 2 + 1

    def remote(src, dst, send, recv, to):
        return pltpu.make_async_remote_copy(
            src_ref=src, dst_ref=dst, send_sem=send, recv_sem=recv, device_id=(group, to), device_id_type=MESH
        )

    barrier = pltpu.get_barrier_semaphore()

    def greet(j, _):
        pl.semaphore_signal(barrier, inc=1, device_id=(group, lax.rem(me + j, bands)), device_id_type=MESH)
        return 0

    lax.fori_loop(1, bands, greet, 0)
    own = pltpu.make_async_copy(nest_ref, nest_out, local_sem)
    own.start()
    pl.semaphore_wait(barrier, bands - 1)

    def nest_copy(step, way, mem, to):
        return remote(
            given.at[step, way, mem], taken.at[step, way, mem], nest_send.at[step, way, mem], nest_recv.at[step, way, mem], to
        )

    part = edge_ref.shape[3] // 2

    def edge_copy(piece, way, mem, to):
        place = pl.ds(piece * part, part)
        return remote(
            edge_ref.at[way, mem, :, place],
            halo.at[way, mem, :, place],
            edge_send.at[piece, way, mem],
            edge_recv.at[piece, way, mem],
            to,
        )

    def strip_copy(slot, to, index):
        return remote(strip_ref, strips.at[pl.ds(pl.multiple_of((slot + 1) * prows, prows), prows), :], strip_send.at[index], strip_recv.at[slot], to)

    def end_copy(end, slot, to):
        return remote(ends_ref.at[end], endbuf.at[slot], end_send.at[end], end_recv.at[slot], to)

    first, last = me == 0, me == bands - 1

    def send_strip(j, _):
        strip_copy(me, lax.rem(me + j, bands), j).start()
        return 0

    lax.fori_loop(1, bands, send_strip, 0)

    sends_top = jnp.logical_and(me > 0, me < top_senders)
    sends_bottom = jnp.logical_and(me < bands - 1, me >= bands - top_senders)

    @pl.when(sends_top)
    def _():
        end_copy(0, me, 0).start()

    @pl.when(sends_bottom)
    def _():
        end_copy(1, bands - 1 - me, bands - 1).start()

    def send_up_down(copy, a, mem):
        @pl.when(jnp.logical_not(first))
        def _():
            copy(a, 0, mem, me - 1).start()

        @pl.when(jnp.logical_not(last))
        def _():
            copy(a, 1, mem, me + 1).start()

    def await_up_down(copy, a, mem):
        @pl.when(jnp.logical_not(last))
        def _():
            copy(a, 0, mem, me).wait_recv()

        @pl.when(jnp.logical_not(first))
        def _():
            copy(a, 1, mem, me).wait_recv()

    def sent_up_down(copy, a, mem):
        @pl.when(jnp.logical_not(first))
        def _():
            copy(a, 0, mem, me).wait_send()

        @pl.when(jnp.logical_not(last))
        def _():
            copy(a, 1, mem, me).wait_send()

    pad = strips.shape[0] - (bands + 1) * prows
    strips[pl.ds(0, prows), :] = jnp.zeros((prows, LANES), jnp.float32)
    strips[pl.ds((bands + 1) * prows, pad), :] = jnp.zeros((pad, LANES), jnp.float32)
    strips[pl.ds(pl.multiple_of((me + 1) * prows, prows), prows), :] = strip_ref[...]
    cpad = (cbuf.shape[2] - bands * tile) // 2
    blank = jnp.zeros((span // LANES, 3, cpad, LANES), jnp.float32)
    cbuf[:, :, pl.ds(0, cpad), :] = blank
    cbuf[:, :, pl.ds(cpad + bands * tile, cpad), :] = blank

    ends_lane = span + LANES

    @pl.when(jnp.logical_or(first, last))
    def _():
        j = iota((1, nwidth), 1) + 2
        q, t = j // 3, j % 3
        k = iota((ends_lane, nwidth), 0) - 3
        fine[...] = (jnp.where(k == q, 3 - t, 0) + jnp.where(k == q + 1, t, 0)).astype(jnp.float32).astype(jnp.bfloat16)

    e = iota((nrows, prows), 0) + 2
    q, t = e // 3, e % 3
    k = iota((nrows, prows), 1)
    weights = jnp.where(k == q, (3 - t).astype(jnp.float32) / 3.0, 0.0) + jnp.where(
        k == q + 1, t.astype(jnp.float32) / 3.0, 0.0
    )
    thin = jnp.where(iota((nwidth, span), 0) // 3 == iota((nwidth, span), 1), 1.0, 0.0).astype(jnp.bfloat16)
    row = iota((nrows, nwidth), 0)
    col = iota((nrows, nwidth), 1)
    at_west, at_east = col == 0, col == nwidth - 1
    at_top, at_bottom = row == 0, row == nrows - 1
    lanes = iota((nrows, LANES), 1)

    def recv_strip(j, _):
        strip_copy(lax.rem(me + j, bands), me, j).wait_recv()
        return 0

    lax.fori_loop(1, bands, recv_strip, 0)

    g = strips[...]
    lane = iota((1, LANES), 1)
    turn = lane_roll(g, -16)
    height = g + jnp.where(lane < 16, -half, courant * half) * (row_roll(turn, -1) - row_roll(turn, 1))
    turn = lane_roll(height, 64)
    cols[...] = jnp.where(lane < 64, height, g - half * (row_roll(turn, -1) - row_roll(turn, 1)))
    picked = jnp.zeros((prows, LANES), jnp.float32)
    for mem in range(members):
        begin = off_ref[mem, 0] + (me * tile - 1 + prows)
        picked = jnp.where(lane % 32 // 2 == mem, cols[pl.ds(begin, prows), :], picked)
    side = jnp.dot(weights, picked, precision=highest, preferred_element_type=jnp.float32)
    for mem in range(members):
        for f in range(2):
            for s in range(2):
                k = 32 * f + s + 2 * mem
                sides[mem, 2 * f + s] = jnp.broadcast_to(side[:, k : k + 1], (nrows, LANES))
    own.wait()

    def ddx(x, f, mem):
        west, east = [jnp.concatenate([sides[mem, 2 * f + s]] * (nwidth // LANES), axis=-1) for s in range(2)]
        return jnp.where(at_east, east, lane_roll(x, -1)) - jnp.where(at_west, west, lane_roll(x, 1))

    def ddy(x, above, below):
        return jnp.where(at_bottom, below, row_roll(x, -1)) - jnp.where(at_top, above, row_roll(x, 1))

    def give(step, mem, h, z, m):
        q = h - half * ddx(z, 1, mem)
        known[mem] = q
        given[step, 0, mem, 0:1] = m[0:1]
        given[step, 0, mem, 1:2] = q[0:1] - half * m[1:2]
        given[step, 1, mem, 0:1] = m[nrows - 1 : nrows]
        given[step, 1, mem, 1:2] = q[nrows - 1 : nrows] + half * m[nrows - 2 : nrows - 1]
        send_up_down(nest_copy, step, mem)

    def give_first(mem, _):
        give(0, mem, nest_out[mem, 0], nest_out[mem, 1], nest_out[mem, 2])
        return 0

    lax.fori_loop(0, members, give_first, 0)

    def add_end(k, _):
        @pl.when(k > 0)
        def _():
            end_copy(0, k, 0).wait_recv()

        acc[...] += endbuf[k]
        return 0

    @pl.when(first)
    def _():
        endbuf[0] = ends_ref[0]

    @pl.when(last)
    def _():
        endbuf[0] = ends_ref[1]

    @pl.when(jnp.logical_or(first, last))
    def _():
        acc[...] = jnp.zeros_like(acc)
        lax.fori_loop(0, top_senders, add_end, 0)
        rows_in = acc[...].reshape(3 * members, ends_lane)
        ghost[...] = (exact_dot(rows_in, fine[...]) * (1.0 / 3.0)).reshape(3, members, nwidth)

    turn_of = lax.rem(group, per)

    def mid_copy(mem, slot, to):
        return remote(
            dealt.at[mem],
            cbuf.at[:, :, pl.ds(pl.multiple_of(cpad + slot * tile, tile), tile), :],
            mid_send.at[mem],
            mid_recv.at[slot],
            to,
        )

    def one_member(step, mem, _):
        if step < 2:
            send_up_down(edge_copy, step, mem)
        await_up_down(nest_copy, step, mem)
        z, m = nest_out[mem, 1], nest_out[mem, 2]
        h_ghost, m_ghost = ghost[0, pl.ds(mem, 1), :], ghost[2, pl.ds(mem, 1), :]
        m_above = jnp.where(first, m_ghost, taken[step, 1, mem, 0:1])
        h_above = jnp.where(first, h_ghost, taken[step, 1, mem, 1:2] - half * m[0:1])
        m_below = jnp.where(last, m_ghost, taken[step, 0, mem, 0:1])
        h_below = jnp.where(last, h_ghost, taken[step, 0, mem, 1:2] + half * m[nrows - 1 : nrows])
        h = known[mem] - half * ddy(m, m_above, m_below)
        z, m = (
            keep * z - half * ddx(h, 0, mem) + rotation * m,
            keep * m - half * ddy(h, h_above, h_below) - rotation * z,
        )
        if step < NSTEPS - 1:
            give(step + 1, mem, h, z, m)
            nest_out[mem, 1] = z
            nest_out[mem, 2] = m
            return 0
        inner = (h, z, m)
        for f, x in enumerate(inner):
            nest_out[mem, f] = x
        sums = exact_dot(jnp.concatenate(inner, axis=0), thin)
        for k in range(span // LANES):
            thinned[k] = sums[:, k * LANES : (k + 1) * LANES]
            for f in range(3):
                parts = [thinned[k, pl.ds(f * nrows + i, tile, stride=3), :] for i in range(3)]
                dealt[mem, k, f] = (parts[0] + parts[1] + parts[2]) * (1.0 / 9.0)
        to = per * mem + turn_of

        @pl.when(to != me)
        def _():
            mid_copy(mem, me, to).start()

        @pl.when(to == me)
        def _():
            cbuf[:, :, pl.ds(pl.multiple_of(cpad + me * tile, tile), tile), :] = dealt[mem]

        return 0

    for step in range(NSTEPS):
        lax.fori_loop(0, members, functools.partial(one_member, step), 0)
    is_mid = lax.rem(me, per) == turn_of
    mine = me // per

    def out_copy(to):
        return remote(sbuf.at[to], patch.at[mine], out_send.at[to], out_recv.at[mine], to)

    @pl.when(is_mid)
    def _():
        def recv(j, _):
            mid_copy(0, lax.rem(me + j, bands), me).wait_recv()
            return 0

        lax.fori_loop(1, bands, recv, 0)
        start_row = off_ref[mine, 0]

        def deal(j, _):
            to = lax.rem(me + j, bands)
            begin = jnp.clip(to * prows - start_row, -cpad, bands * tile) + cpad
            for k in range(0, span, LANES):
                sbuf[to, :, :, pl.ds(k, LANES)] = cbuf[k // LANES, :, pl.ds(begin, prows), :]

            @pl.when(to != me)
            def _():
                out_copy(to).start()

            return 0

        lax.fori_loop(1, bands + 1, deal, 0)
        patch[mine] = sbuf[me]

    def recv_patch(mem, _):
        @pl.when(per * mem + turn_of != me)
        def _():
            remote(sbuf.at[0], patch.at[mem], out_send.at[0], out_recv.at[mem], me).wait_recv()

        return 0

    lax.fori_loop(0, members, recv_patch, 0)

    @pl.when(sends_top)
    def _():
        end_copy(0, me, 0).wait_send()

    @pl.when(sends_bottom)
    def _():
        end_copy(1, bands - 1 - me, bands - 1).wait_send()

    def sent_strip(j, _):
        strip_copy(me, lax.rem(me + j, bands), j).wait_send()
        return 0

    lax.fori_loop(1, bands, sent_strip, 0)

    def sent_mid(mem, _):
        for piece in range(2):
            await_up_down(edge_copy, piece, mem)
            sent_up_down(edge_copy, piece, mem)
        for step in range(NSTEPS):
            sent_up_down(nest_copy, step, mem)

        @pl.when(per * mem + turn_of != me)
        def _():
            mid_copy(mem, me, me).wait_send()

        return 0

    lax.fori_loop(0, members, sent_mid, 0)

    @pl.when(is_mid)
    def _():
        def sent_out(j, _):
            out_copy(lax.rem(me + j, bands)).wait_send()
            return 0

        lax.fori_loop(1, bands, sent_out, 0)


def parent_kernel(span, bands, off_ref, band_ref, par_ref, halo_ref, patch_ref, out_ref):
    mem = pl.program_id(0)
    rows, width = par_ref.shape[2], par_ref.shape[3]
    row0, col0 = off_ref[mem, 0], off_ref[mem, 1]
    band = band_ref[0]
    first, last = band == 0, band == bands - 1
    h, z, m = par_ref[0, 0], par_ref[0, 1], par_ref[0, 2]
    row = iota(h.shape, 0)

    def ddy(x, above, below):
        up = jnp.where(row == 0, above, row_roll(x, 1))
        down = jnp.where(row == rows - 1, below, row_roll(x, -1))
        return down - up

    m_above = jnp.where(first, 0.0, halo_ref[1, 0, 0:1, :])
    m_below = jnp.where(last, 0.0, halo_ref[0, 0, 0:1, :])
    h_above = jnp.where(first, 0.0, halo_ref[1, 0, 1:2, :] - half * m[0:1])
    h_below = jnp.where(last, 0.0, halo_ref[0, 0, 1:2, :] + half * m[rows - 1 : rows])
    h1 = h - courant * dx(z) - half * ddy(m, m_above, m_below)
    out_ref[0, 0] = h1
    out_ref[0, 1] = keep * z - courant * dx(h1) + rotation * m
    out_ref[0, 2] = keep * m - half * ddy(h1, h_above, h_below) - rotation * z

    block0 = col0 // LANES
    shift = col0 - block0 * LANES
    place = pl.ds(pl.multiple_of(block0 * LANES, LANES), span + LANES)
    wide = jnp.concatenate([patch_ref[0], jnp.zeros((3, rows, LANES), jnp.float32)], axis=-1)
    wide = pltpu.roll(wide.reshape(3 * rows, span + LANES), shift, 1).reshape(3, rows, span + LANES)
    lane = iota(wide.shape, 2)
    at = iota(wide.shape, 1) + (band * rows - row0)
    inside = (lane >= shift) & (lane < shift + span) & (at >= 0) & (at < span)
    out_ref[0, :, :, place] = jnp.where(inside, wide, out_ref[0, :, :, place])


def per_device(bands, parent_state, nest_state, offsets):
    members, _, prows, width = parent_state.shape
    nrows, nwidth = nest_state.shape[2:]
    span = nwidth // 3
    tile = nrows // 3
    f32 = jnp.float32
    band = lax.axis_index("band").reshape(1).astype(jnp.int32)
    shape = jax.ShapeDtypeStruct
    limit = 48 * 1024 * 1024
    parent_spec = pl.BlockSpec((1, 3, prows, width), lambda i, *_: (i, 0, 0, 0))
    edge_spec = pl.BlockSpec((2, 1, 2, width), lambda i, *_: (0, i, 0, 0))

    edges, strip, ends = pl.pallas_call(
        functools.partial(gather_kernel, span, bands),
        out_shape=(
            shape((2, members, 2, width), f32),
            shape((prows, LANES), f32),
            shape((2, 3, members, span + LANES), f32),
        ),
        grid_spec=pltpu.PrefetchScalarGridSpec(
            num_scalar_prefetch=2,
            grid=(members,),
            in_specs=[parent_spec],
            out_specs=(
                edge_spec,
                pl.BlockSpec((prows, LANES), lambda i, *_: (0, 0)),
                pl.BlockSpec((2, 3, members, span + LANES), lambda i, *_: (0, 0, 0, 0)),
            ),
        ),
        compiler_params=pltpu.CompilerParams(vmem_limit_bytes=limit),
        name="gather",
    )(offsets, band, parent_state)

    vmem = pl.BlockSpec(memory_space=pltpu.VMEM)
    hbm = pl.BlockSpec(memory_space=pl.ANY)
    dma = pltpu.SemaphoreType.DMA
    senders = bands // 2 + 1
    nest_out, patch, halo = pl.pallas_call(
        functools.partial(nest_kernel, bands, span),
        out_shape=(
            shape(nest_state.shape, f32),
            shape((members, 3, prows, span), f32),
            shape((2, members, 2, width), f32),
        ),
        in_specs=[pl.BlockSpec(memory_space=pltpu.SMEM), hbm, hbm, vmem, vmem],
        out_specs=(vmem, vmem, hbm),
        scratch_shapes=[
            pltpu.VMEM((NSTEPS, 2, members, 2, nwidth), f32),
            pltpu.VMEM((NSTEPS, 2, members, 2, nwidth), f32),
            pltpu.VMEM((members, nrows, nwidth), f32),
            pltpu.VMEM(((bands + 2) * prows, LANES), f32),
            pltpu.VMEM((senders, 3, members, span + LANES), f32),
            pltpu.VMEM(((bands + 2) * prows, LANES), f32),
            pltpu.VMEM((members, 4, nrows, LANES), f32),
            pltpu.VMEM((3, members, nwidth), f32),
            pltpu.VMEM((3, members, span + LANES), f32),
            pltpu.VMEM((span + LANES, nwidth), jnp.bfloat16),
            pltpu.VMEM((span // LANES, 3 * nrows, LANES), f32),
            pltpu.VMEM((members, span // LANES, 3, tile, LANES), f32),
            pltpu.VMEM((span // LANES, 3, bands * tile + 2 * prows, LANES), f32),
            pltpu.VMEM((bands, 3, prows, span), f32),
            dma((NSTEPS, 2, members)),
            dma((NSTEPS, 2, members)),
            dma((2, 2, members)),
            dma((2, 2, members)),
            dma((bands,)),
            dma((bands,)),
            dma((2,)),
            dma((senders,)),
            dma((members,)),
            dma((bands,)),
            dma((bands,)),
            dma((members,)),
            dma,
        ],
        compiler_params=pltpu.CompilerParams(collective_id=0, has_side_effects=True, vmem_limit_bytes=limit),
        name="nest",
    )(offsets, nest_state, edges, strip, ends)

    parent_out = pl.pallas_call(
        functools.partial(parent_kernel, span, bands),
        out_shape=shape(parent_state.shape, f32),
        grid_spec=pltpu.PrefetchScalarGridSpec(
            num_scalar_prefetch=2,
            grid=(members,),
            in_specs=[
                parent_spec,
                edge_spec,
                pl.BlockSpec((1, 3, prows, span), lambda i, *_: (i, 0, 0, 0)),
            ],
            out_specs=parent_spec,
        ),
        compiler_params=pltpu.CompilerParams(vmem_limit_bytes=limit),
        name="parent",
    )(offsets, band, parent_state, halo, patch)
    return (parent_out, nest_out)


def solution(mesh):
    in_specs = (P("member", None, "band", None), P("member", None, "band", None), P("member", None))
    out_specs = (P("member", None, "band", None), P("member", None, "band", None))
    return jax.shard_map(
        functools.partial(per_device, mesh.shape["band"]),
        mesh=mesh,
        in_specs=in_specs,
        out_specs=out_specs,
        check_vma=False,
    )
```

```python
import functools

import jax
import jax.numpy as jnp
from jax import lax
from jax.experimental import pallas as pl
from jax.experimental.pallas import tpu as pltpu
from jax.sharding import PartitionSpec as P

NSTEPS = 3
MESH = pl.DeviceIdType.MESH

courant = 0.9
friction = 0.02
rotation = 0.05
half = 0.5 * courant
keep = 1.0 - friction
highest = lax.Precision.HIGHEST
LANES = 128
HALO = 8


def lane_roll(x, shift):
    size = x.shape[-1]
    return pltpu.roll(x, shift % size, x.ndim - 1)


def row_roll(x, shift):
    size = x.shape[-2]
    return pltpu.roll(x, shift % size, x.ndim - 2)


def dx(x):
    return 0.5 * (lane_roll(x, -1) - lane_roll(x, 1))


def iota(shape, dim):
    return lax.broadcasted_iota(jnp.int32, shape, dim)


def split(x):
    high = x.astype(jnp.bfloat16)
    rest = x - high.astype(jnp.float32)
    mid = rest.astype(jnp.bfloat16)
    return high, mid, (rest - mid.astype(jnp.float32)).astype(jnp.bfloat16)


def exact_dot(x, weights):
    return sum(jnp.dot(part, weights, preferred_element_type=jnp.float32) for part in split(x))


def edge_rows(mem, par_ref, edge_ref):
    rows = par_ref.shape[2]
    z_top, z_bot = par_ref[mem, 1, 0:1, :], par_ref[mem, 1, rows - 1 : rows, :]
    m_top, m_bot = par_ref[mem, 2, 0:1, :], par_ref[mem, 2, rows - 1 : rows, :]
    edge_ref[0, mem, 0:1, :] = m_top
    edge_ref[0, mem, 1:2, :] = par_ref[mem, 0, 0:1, :] - courant * dx(z_top) - half * par_ref[mem, 2, 1:2, :]
    edge_ref[1, mem, 0:1, :] = m_bot
    edge_ref[1, mem, 1:2, :] = (
        par_ref[mem, 0, rows - 1 : rows, :] - courant * dx(z_bot) + half * par_ref[mem, 2, rows - 2 : rows - 1, :]
    )


def window_shares(mem, span, row0, col0, band, par_ref, ends_ref):
    rows, width = par_ref.shape[2], par_ref.shape[3]
    blocks = width // LANES
    count = span // LANES + 2
    first = lax.rem(col0 - 4 + width, width)
    block0 = lax.div(first, LANES)
    shift = first - block0 * LANES
    wanted = [jnp.zeros((rows, LANES), jnp.int32) + lax.rem(block0 + k, blocks) for k in range(count)]
    parts = [jnp.zeros((3, rows, LANES), jnp.float32)] * count
    for place in range(blocks):
        block = par_ref[mem, :, :, place * LANES : (place + 1) * LANES]
        parts = [jnp.where((w == place)[None], block, part) for w, part in zip(wanted, parts)]
    wide = jnp.concatenate(parts, axis=-1).reshape(3 * rows, count * LANES)
    amount = jnp.zeros(wide.shape, jnp.int32) + shift
    for bit in (64, 32, 16, 8, 4, 2, 1):
        wide = jnp.where((amount & bit) != 0, lane_roll(wide, -bit), wide)
    wide = wide[:, : span + LANES].reshape(3, rows, span + LANES)
    h, z, m = wide[0], wide[1], wide[2]
    a = h - courant * dx(z)
    b = keep * z - courant * dx(a) + rotation * m
    cc = keep * m - rotation * z
    shape = h.shape
    lane = iota(shape, 1)
    west = jnp.where(lane == 3, 2.0 / 3.0, 0.0) + jnp.where(lane == 4, 1.0 / 3.0, 0.0)
    east = jnp.where(lane == span + 3, 1.0 / 3.0, 0.0) + jnp.where(lane == span + 4, 2.0 / 3.0, 0.0)
    slot = iota((rows, LANES), 1)
    total = jnp.zeros((rows, LANES), jnp.float32)
    for q, field in enumerate((a, m, b, dx(m), cc)):
        for s, weight in enumerate((west, east)):
            value = jnp.sum(field * weight, axis=1, keepdims=True)
            total = total + jnp.where(slot == q * 16 + s + 2 * mem, value, 0.0)

    row = iota(shape, 0) + band * rows
    for end in range(2):
        near = row0 - 1 if end == 0 else row0 + span - 1
        lo, hi = (2.0 / 3.0, 1.0 / 3.0) if end == 0 else (1.0 / 3.0, 2.0 / 3.0)

        def w(i):
            return jnp.where(i == near, lo, 0.0) + jnp.where(i == near + 1, hi, 0.0)

        def u(i):
            return -half * (w(i - 1) - w(i + 1))

        wr, ur = w(row), u(row)
        vr = -half * (u(row - 1) - u(row + 1))
        h1 = jnp.sum(wr * a + ur * m, axis=0, keepdims=True)
        z1 = jnp.sum(wr * (keep * z + rotation * m), axis=0, keepdims=True) - courant * dx(h1)
        m1 = jnp.sum(wr * cc + ur * a + vr * m, axis=0, keepdims=True)
        for f, value in enumerate((h1, z1, m1)):
            ends_ref[end, f, pl.ds(mem, 1), :] = value
    return total


def nest_kernel(
    bands,
    span,
    off_ref,
    nest_ref,
    parent_ref,
    nest_out,
    patch,
    halo,
    par_ref,
    edge_ref,
    strip_ref,
    ends_ref,
    ext,
    strips,
    endbuf,
    cols,
    side,
    ghost,
    acc,
    fine,
    thinned,
    dealt,
    cbuf,
    sbuf,
    nest_send,
    nest_recv,
    edge_send,
    edge_recv,
    strip_send,
    strip_recv,
    end_send,
    end_recv,
    mid_send,
    mid_recv,
    out_send,
    out_recv,
    local_sem,
    parent_sem,
):
    me = lax.axis_index("band")
    group = lax.axis_index("member")
    members, _, nrows, nwidth = nest_ref.shape
    prows = strip_ref.shape[0]
    tile = nrows // 3
    per = bands // members
    top_senders = bands // 2 + 1

    def remote(src, dst, send, recv, to):
        return pltpu.make_async_remote_copy(
            src_ref=src, dst_ref=dst, send_sem=send, recv_sem=recv, device_id=(group, to), device_id_type=MESH
        )

    barrier = pltpu.get_barrier_semaphore()

    def greet(j, _):
        pl.semaphore_signal(barrier, inc=1, device_id=(group, lax.rem(me + j, bands)), device_id_type=MESH)
        return 0

    lax.fori_loop(1, bands, greet, 0)
    own = pltpu.make_async_copy(nest_ref, ext.at[:, :, pl.ds(HALO, nrows), :], local_sem)
    load = pltpu.make_async_copy(parent_ref, par_ref, parent_sem)
    load.start()
    own.start()
    pl.semaphore_wait(barrier, bands - 1)

    reach = 2 * NSTEPS

    def nest_down(mem, to):
        return remote(
            nest_ref.at[mem, :, pl.ds(nrows - reach, reach), :],
            ext.at[mem, :, pl.ds(HALO - reach, reach), :],
            nest_send.at[0, mem],
            nest_recv.at[0, mem],
            to,
        )

    def nest_up(mem, to):
        return remote(
            nest_ref.at[mem, :, pl.ds(0, reach), :],
            ext.at[mem, :, pl.ds(HALO + nrows, reach), :],
            nest_send.at[1, mem],
            nest_recv.at[1, mem],
            to,
        )

    def edge_down(to):
        return remote(edge_ref.at[1], halo.at[0], edge_send.at[0], edge_recv.at[0], to)

    def edge_up(to):
        return remote(edge_ref.at[0], halo.at[1], edge_send.at[1], edge_recv.at[1], to)

    def strip_copy(slot, to, index):
        return remote(strip_ref, strips.at[pl.ds(pl.multiple_of((slot + 1) * prows, prows), prows), :], strip_send.at[index], strip_recv.at[slot], to)

    def end_copy(end, slot, to):
        return remote(ends_ref.at[end], endbuf.at[slot], end_send.at[end], end_recv.at[slot], to)

    first, last = me == 0, me == bands - 1

    def gather(mem, _):
        @pl.when(jnp.logical_not(first))
        def _():
            nest_up(mem, me - 1).start()

        @pl.when(jnp.logical_not(last))
        def _():
            nest_down(mem, me + 1).start()

        strip_ref[...] += window_shares(mem, span, off_ref[mem, 0], off_ref[mem, 1], me, par_ref, ends_ref)
        return 0

    strip_ref[...] = jnp.zeros_like(strip_ref)
    load.wait()
    lax.fori_loop(0, members, gather, 0)

    def send_strip(j, _):
        strip_copy(me, lax.rem(me + j, bands), j).start()
        return 0

    lax.fori_loop(1, bands, send_strip, 0)

    sends_top = jnp.logical_and(me > 0, me < top_senders)
    sends_bottom = jnp.logical_and(me < bands - 1, me >= bands - top_senders)

    @pl.when(sends_top)
    def _():
        end_copy(0, me, 0).start()

    @pl.when(sends_bottom)
    def _():
        end_copy(1, bands - 1 - me, bands - 1).start()

    def send_edges(mem, _):
        edge_rows(mem, par_ref, edge_ref)
        return 0

    lax.fori_loop(0, members, send_edges, 0)

    @pl.when(jnp.logical_not(first))
    def _():
        edge_up(me - 1).start()

    @pl.when(jnp.logical_not(last))
    def _():
        edge_down(me + 1).start()

    pad = strips.shape[0] - (bands + 1) * prows
    strips[pl.ds(0, prows), :] = jnp.zeros((prows, LANES), jnp.float32)
    strips[pl.ds((bands + 1) * prows, pad), :] = jnp.zeros((pad, LANES), jnp.float32)
    strips[pl.ds(pl.multiple_of((me + 1) * prows, prows), prows), :] = strip_ref[...]
    cpad = (cbuf.shape[2] - bands * tile) // 2
    blank = jnp.zeros((span // LANES, 3, cpad, LANES), jnp.float32)
    cbuf[:, :, pl.ds(0, cpad), :] = blank
    cbuf[:, :, pl.ds(cpad + bands * tile, cpad), :] = blank

    ends_lane = span + LANES

    @pl.when(jnp.logical_or(first, last))
    def _():
        j = iota((1, nwidth), 1) + 2
        q, t = j // 3, j % 3
        k = iota((ends_lane, nwidth), 0) - 3
        fine[...] = (jnp.where(k == q, 3 - t, 0) + jnp.where(k == q + 1, t, 0)).astype(jnp.float32).astype(jnp.bfloat16)

    erows = nrows + 2 * HALO
    e = iota((erows, prows), 0)
    q, t = e // 3, e % 3
    k = iota((erows, prows), 1)
    weights = jnp.where(k == q, (3 - t).astype(jnp.float32) / 3.0, 0.0) + jnp.where(
        k == q + 1, t.astype(jnp.float32) / 3.0, 0.0
    )
    thin = jnp.where(iota((nwidth, span), 0) // 3 == iota((nwidth, span), 1), 1.0, 0.0).astype(jnp.bfloat16)
    row = iota((erows, nwidth), 0)
    col = iota((erows, nwidth), 1)
    is_ghost = jnp.logical_or(
        jnp.logical_and(row == HALO - 1, first), jnp.logical_and(row == HALO + nrows, last)
    )
    at_west, at_east = col == 0, col == nwidth - 1
    lanes = iota((erows, LANES), 1)

    def recv_strip(j, _):
        strip_copy(lax.rem(me + j, bands), me, j).wait_recv()
        return 0

    lax.fori_loop(1, bands, recv_strip, 0)

    g = strips[...]
    lane = iota((1, LANES), 1)
    turn = lane_roll(g, -16)
    height = g + jnp.where(lane < 16, -half, courant * half) * (row_roll(turn, -1) - row_roll(turn, 1))
    turn = lane_roll(height, 64)
    cols[...] = jnp.where(lane < 64, height, g - half * (row_roll(turn, -1) - row_roll(turn, 1)))
    picked = jnp.zeros((prows, LANES), jnp.float32)
    for mem in range(members):
        begin = off_ref[mem, 0] + (me * tile - 3 + prows)
        picked = jnp.where(lane % 32 // 2 == mem, cols[pl.ds(begin, prows), :], picked)
    side[...] = jnp.dot(weights, picked, precision=highest, preferred_element_type=jnp.float32)


    def add_end(k, _):
        @pl.when(k > 0)
        def _():
            end_copy(0, k, 0).wait_recv()

        acc[...] += endbuf[k]
        return 0

    @pl.when(first)
    def _():
        endbuf[0] = ends_ref[0]

    @pl.when(last)
    def _():
        endbuf[0] = ends_ref[1]

    @pl.when(jnp.logical_or(first, last))
    def _():
        acc[...] = jnp.zeros_like(acc)
        lax.fori_loop(0, top_senders, add_end, 0)
        rows_in = acc[...].reshape(3 * members, ends_lane)
        ghost[...] = (exact_dot(rows_in, fine[...]) * (1.0 / 3.0)).reshape(3, members, nwidth)

    own.wait()

    turn_of = lax.rem(group, per)

    def mid_copy(mem, slot, to):
        return remote(
            dealt.at[mem],
            cbuf.at[:, :, pl.ds(pl.multiple_of(cpad + slot * tile, tile), tile), :],
            mid_send.at[mem],
            mid_recv.at[slot],
            to,
        )

    def one_member(mem, _):
        @pl.when(jnp.logical_not(first))
        def _():
            nest_down(mem, me).wait_recv()

        @pl.when(jnp.logical_not(last))
        def _():
            nest_up(mem, me).wait_recv()

        def side_of(f, s):
            return jnp.sum(jnp.where(lanes == 32 * f + s + 2 * mem, side[...], 0.0), axis=1, keepdims=True)

        sides = [[side_of(f, s) for s in range(2)] for f in range(2)]
        ends = [ghost[f, pl.ds(mem, 1), :] for f in range(3)]

        def ddx(x, f):
            left = jnp.where(at_west, sides[f][0], lane_roll(x, 1))
            right = jnp.where(at_east, sides[f][1], lane_roll(x, -1))
            return right - left

        def ddy(x):
            return row_roll(x, -1) - row_roll(x, 1)

        def bound(x, f):
            return jnp.where(is_ghost, ends[f], x)

        h, z, m = ext[mem, 0], bound(ext[mem, 1], 1), bound(ext[mem, 2], 2)
        for _ in range(NSTEPS):
            h = bound(h - half * (ddx(z, 1) + ddy(m)), 0)
            z, m = (
                bound(keep * z - half * ddx(h, 0) + rotation * m, 1),
                bound(keep * m - half * ddy(h) - rotation * z, 2),
            )
        inner = [x[HALO : HALO + nrows] for x in (h, z, m)]
        for f, x in enumerate(inner):
            nest_out[mem, f] = x
        sums = exact_dot(jnp.concatenate(inner, axis=0), thin)
        for k in range(span // LANES):
            thinned[k] = sums[:, k * LANES : (k + 1) * LANES]
            for f in range(3):
                parts = [thinned[k, pl.ds(f * nrows + i, tile, stride=3), :] for i in range(3)]
                dealt[mem, k, f] = (parts[0] + parts[1] + parts[2]) * (1.0 / 9.0)
        to = per * mem + turn_of

        @pl.when(to != me)
        def _():
            mid_copy(mem, me, to).start()

        @pl.when(to == me)
        def _():
            cbuf[:, :, pl.ds(pl.multiple_of(cpad + me * tile, tile), tile), :] = dealt[mem]

        return 0

    lax.fori_loop(0, members, one_member, 0)
    is_mid = lax.rem(me, per) == turn_of
    mine = me // per

    def out_copy(to):
        return remote(sbuf.at[to], patch.at[mine], out_send.at[to], out_recv.at[mine], to)

    @pl.when(is_mid)
    def _():
        def recv(j, _):
            mid_copy(0, lax.rem(me + j, bands), me).wait_recv()
            return 0

        lax.fori_loop(1, bands, recv, 0)
        start_row = off_ref[mine, 0]

        def deal(j, _):
            to = lax.rem(me + j, bands)
            begin = jnp.clip(to * prows - start_row, -cpad, bands * tile) + cpad
            for k in range(0, span, LANES):
                sbuf[to, :, :, pl.ds(k, LANES)] = cbuf[k // LANES, :, pl.ds(begin, prows), :]

            @pl.when(to != me)
            def _():
                out_copy(to).start()

            return 0

        lax.fori_loop(1, bands + 1, deal, 0)
        patch[mine] = sbuf[me]

    def recv_patch(mem, _):
        @pl.when(per * mem + turn_of != me)
        def _():
            remote(sbuf.at[0], patch.at[mem], out_send.at[0], out_recv.at[mem], me).wait_recv()

        return 0

    lax.fori_loop(0, members, recv_patch, 0)

    @pl.when(jnp.logical_not(first))
    def _():
        edge_down(me).wait_recv()
        edge_up(me).wait_send()

    @pl.when(jnp.logical_not(last))
    def _():
        edge_up(me).wait_recv()
        edge_down(me).wait_send()

    @pl.when(sends_top)
    def _():
        end_copy(0, me, 0).wait_send()

    @pl.when(sends_bottom)
    def _():
        end_copy(1, bands - 1 - me, bands - 1).wait_send()

    def sent_strip(j, _):
        strip_copy(me, lax.rem(me + j, bands), j).wait_send()
        return 0

    lax.fori_loop(1, bands, sent_strip, 0)

    def sent_mid(mem, _):
        @pl.when(jnp.logical_not(first))
        def _():
            nest_up(mem, me).wait_send()

        @pl.when(jnp.logical_not(last))
        def _():
            nest_down(mem, me).wait_send()

        @pl.when(per * mem + turn_of != me)
        def _():
            mid_copy(mem, me, me).wait_send()

        return 0

    lax.fori_loop(0, members, sent_mid, 0)

    @pl.when(is_mid)
    def _():
        def sent_out(j, _):
            out_copy(lax.rem(me + j, bands)).wait_send()
            return 0

        lax.fori_loop(1, bands, sent_out, 0)


def parent_kernel(span, bands, off_ref, band_ref, par_ref, halo_ref, patch_ref, out_ref):
    mem = pl.program_id(0)
    rows, width = par_ref.shape[2], par_ref.shape[3]
    row0, col0 = off_ref[mem, 0], off_ref[mem, 1]
    band = band_ref[0]
    first, last = band == 0, band == bands - 1
    piece = 4 * LANES
    row = iota((rows, piece + 2 * LANES), 0)
    at_top, at_bottom = row == 0, row == rows - 1

    def ddy(x, above, below):
        return jnp.where(at_bottom, below, row_roll(x, -1)) - jnp.where(at_top, above, row_roll(x, 1))

    for begin in range(0, width, piece):

        def cut(ref, *index):
            left, right = (begin - LANES) % width, (begin + piece) % width
            if left + piece + 2 * LANES == right + LANES:
                return ref[(*index, slice(left, right + LANES))]
            parts = (left, left + LANES), (begin, begin + piece), (right, right + LANES)
            return jnp.concatenate([ref[(*index, slice(*part))] for part in parts], axis=-1)

        every = slice(None)
        h, z, m = [cut(par_ref, 0, f, every) for f in range(3)]
        above = cut(halo_ref, 0, 0, every)
        below = cut(halo_ref, 1, 0, every)
        m_above = jnp.where(first, 0.0, above[0:1])
        m_below = jnp.where(last, 0.0, below[0:1])
        h_above = jnp.where(first, 0.0, above[1:2] - half * m[0:1])
        h_below = jnp.where(last, 0.0, below[1:2] + half * m[rows - 1 : rows])
        h1 = h - half * (lane_roll(z, -1) - lane_roll(z, 1) + ddy(m, m_above, m_below))
        z1 = keep * z - half * (lane_roll(h1, -1) - lane_roll(h1, 1)) + rotation * m
        m1 = keep * m - half * ddy(h1, h_above, h_below) - rotation * z
        for f, x in enumerate((h1, z1, m1)):
            out_ref[0, f, :, begin : begin + piece] = x[:, LANES : LANES + piece]

    block0 = col0 // LANES
    shift = col0 - block0 * LANES
    place = pl.ds(pl.multiple_of(block0 * LANES, LANES), span + LANES)
    wide = jnp.concatenate([patch_ref[0], jnp.zeros((3, rows, LANES), jnp.float32)], axis=-1)
    wide = pltpu.roll(wide.reshape(3 * rows, span + LANES), shift, 1).reshape(3, rows, span + LANES)
    lane = iota(wide.shape, 2)
    at = iota(wide.shape, 1) + (band * rows - row0)
    inside = (lane >= shift) & (lane < shift + span) & (at >= 0) & (at < span)
    out_ref[0, :, :, place] = jnp.where(inside, wide, out_ref[0, :, :, place])


def per_device(bands, parent_state, nest_state, offsets):
    members, _, prows, width = parent_state.shape
    nrows, nwidth = nest_state.shape[2:]
    span = nwidth // 3
    tile = nrows // 3
    f32 = jnp.float32
    band = lax.axis_index("band").reshape(1).astype(jnp.int32)
    shape = jax.ShapeDtypeStruct
    limit = 48 * 1024 * 1024
    parent_spec = pl.BlockSpec((1, 3, prows, width), lambda i, *_: (i, 0, 0, 0))
    edge_spec = pl.BlockSpec((2, 1, 2, width), lambda i, *_: (0, i, 0, 0))

    vmem = pl.BlockSpec(memory_space=pltpu.VMEM)
    hbm = pl.BlockSpec(memory_space=pl.ANY)
    dma = pltpu.SemaphoreType.DMA
    senders = bands // 2 + 1
    nest_out, patch, halo = pl.pallas_call(
        functools.partial(nest_kernel, bands, span),
        out_shape=(
            shape(nest_state.shape, f32),
            shape((members, 3, prows, span), f32),
            shape((2, members, 2, width), f32),
        ),
        in_specs=[pl.BlockSpec(memory_space=pltpu.SMEM), hbm, hbm],
        out_specs=(vmem, vmem, hbm),
        scratch_shapes=[
            pltpu.VMEM((members, 3, prows, width), f32),
            pltpu.VMEM((2, members, 2, width), f32),
            pltpu.VMEM((prows, LANES), f32),
            pltpu.VMEM((2, 3, members, span + LANES), f32),
            pltpu.VMEM((members, 3, nrows + 2 * HALO, nwidth), f32),
            pltpu.VMEM(((bands + 2) * prows, LANES), f32),
            pltpu.VMEM((senders, 3, members, span + LANES), f32),
            pltpu.VMEM(((bands + 2) * prows, LANES), f32),
            pltpu.VMEM((nrows + 2 * HALO, LANES), f32),
            pltpu.VMEM((3, members, nwidth), f32),
            pltpu.VMEM((3, members, span + LANES), f32),
            pltpu.VMEM((span + LANES, nwidth), jnp.bfloat16),
            pltpu.VMEM((span // LANES, 3 * nrows, LANES), f32),
            pltpu.VMEM((members, span // LANES, 3, tile, LANES), f32),
            pltpu.VMEM((span // LANES, 3, bands * tile + 2 * prows, LANES), f32),
            pltpu.VMEM((bands, 3, prows, span), f32),
            dma((2, members)),
            dma((2, members)),
            dma((2,)),
            dma((2,)),
            dma((bands,)),
            dma((bands,)),
            dma((2,)),
            dma((senders,)),
            dma((members,)),
            dma((bands,)),
            dma((bands,)),
            dma((members,)),
            dma,
            dma,
        ],
        compiler_params=pltpu.CompilerParams(collective_id=0, has_side_effects=True, vmem_limit_bytes=limit),
        name="nest",
    )(offsets, nest_state, parent_state)

    parent_out = pl.pallas_call(
        functools.partial(parent_kernel, span, bands),
        out_shape=shape(parent_state.shape, f32),
        grid_spec=pltpu.PrefetchScalarGridSpec(
            num_scalar_prefetch=2,
            grid=(members,),
            in_specs=[
                parent_spec,
                edge_spec,
                pl.BlockSpec((1, 3, prows, span), lambda i, *_: (i, 0, 0, 0)),
            ],
            out_specs=parent_spec,
        ),
        compiler_params=pltpu.CompilerParams(vmem_limit_bytes=limit),
        name="parent",
    )(offsets, band, parent_state, halo, patch)
    return (parent_out, nest_out)


def solution(mesh):
    in_specs = (P("member", None, "band", None), P("member", None, "band", None), P("member", None))
    out_specs = (P("member", None, "band", None), P("member", None, "band", None))
    return jax.shard_map(
        functools.partial(per_device, mesh.shape["band"]),
        mesh=mesh,
        in_specs=in_specs,
        out_specs=out_specs,
        check_vma=False,
    )
```

```python
import functools

import jax
import jax.numpy as jnp
from jax import lax
from jax.experimental import pallas as pl
from jax.experimental.pallas import tpu as pltpu
from jax.sharding import PartitionSpec as P

NSTEPS = 3
MESH = pl.DeviceIdType.MESH

courant = 0.9
friction = 0.02
rotation = 0.05
half = 0.5 * courant
keep = 1.0 - friction
highest = lax.Precision.HIGHEST
LANES = 128


def lane_roll(x, shift):
    size = x.shape[-1]
    return pltpu.roll(x, shift % size, x.ndim - 1)


def row_roll(x, shift):
    size = x.shape[-2]
    return pltpu.roll(x, shift % size, x.ndim - 2)


def dx(x):
    return 0.5 * (lane_roll(x, -1) - lane_roll(x, 1))


def iota(shape, dim):
    return lax.broadcasted_iota(jnp.int32, shape, dim)


def split(x):
    high = x.astype(jnp.bfloat16)
    rest = x - high.astype(jnp.float32)
    mid = rest.astype(jnp.bfloat16)
    return high, mid, (rest - mid.astype(jnp.float32)).astype(jnp.bfloat16)


def exact_dot(x, weights):
    return sum(jnp.dot(part, weights, preferred_element_type=jnp.float32) for part in split(x))


def edge_rows(mem, par_ref, edge_ref):
    rows = par_ref.shape[2]
    z_top, z_bot = par_ref[mem, 1, 0:1, :], par_ref[mem, 1, rows - 1 : rows, :]
    m_top, m_bot = par_ref[mem, 2, 0:1, :], par_ref[mem, 2, rows - 1 : rows, :]
    edge_ref[0, mem, 0:1, :] = m_top
    edge_ref[0, mem, 1:2, :] = par_ref[mem, 0, 0:1, :] - courant * dx(z_top) - half * par_ref[mem, 2, 1:2, :]
    edge_ref[1, mem, 0:1, :] = m_bot
    edge_ref[1, mem, 1:2, :] = (
        par_ref[mem, 0, rows - 1 : rows, :] - courant * dx(z_bot) + half * par_ref[mem, 2, rows - 2 : rows - 1, :]
    )


def window_shares(mem, span, row0, col0, band, par_ref, ends_ref):
    rows, width = par_ref.shape[2], par_ref.shape[3]
    blocks = width // LANES
    count = span // LANES + 2
    first = lax.rem(col0 - 4 + width, width)
    block0 = lax.div(first, LANES)
    shift = first - block0 * LANES
    wanted = [jnp.zeros((rows, LANES), jnp.int32) + lax.rem(block0 + k, blocks) for k in range(count)]
    parts = [jnp.zeros((3, rows, LANES), jnp.float32)] * count
    for place in range(blocks):
        block = par_ref[mem, :, :, place * LANES : (place + 1) * LANES]
        parts = [jnp.where((w == place)[None], block, part) for w, part in zip(wanted, parts)]
    wide = jnp.concatenate(parts, axis=-1).reshape(3 * rows, count * LANES)
    amount = jnp.zeros(wide.shape, jnp.int32) + shift
    for bit in (64, 32, 16, 8, 4, 2, 1):
        wide = jnp.where((amount & bit) != 0, lane_roll(wide, -bit), wide)
    wide = wide[:, : span + LANES].reshape(3, rows, span + LANES)
    h, z, m = wide[0], wide[1], wide[2]
    a = h - courant * dx(z)
    b = keep * z - courant * dx(a) + rotation * m
    cc = keep * m - rotation * z
    shape = h.shape
    lane = iota(shape, 1)
    west = jnp.where(lane == 3, 2.0 / 3.0, 0.0) + jnp.where(lane == 4, 1.0 / 3.0, 0.0)
    east = jnp.where(lane == span + 3, 1.0 / 3.0, 0.0) + jnp.where(lane == span + 4, 2.0 / 3.0, 0.0)
    slot = iota((rows, LANES), 1)
    total = jnp.zeros((rows, LANES), jnp.float32)
    for q, field in enumerate((a, m, b, dx(m), cc)):
        for s, weight in enumerate((west, east)):
            value = jnp.sum(field * weight, axis=1, keepdims=True)
            total = total + jnp.where(slot == q * 16 + s + 2 * mem, value, 0.0)

    row = iota(shape, 0) + band * rows
    for end in range(2):
        near = row0 - 1 if end == 0 else row0 + span - 1
        lo, hi = (2.0 / 3.0, 1.0 / 3.0) if end == 0 else (1.0 / 3.0, 2.0 / 3.0)

        def w(i):
            return jnp.where(i == near, lo, 0.0) + jnp.where(i == near + 1, hi, 0.0)

        def u(i):
            return -half * (w(i - 1) - w(i + 1))

        wr, ur = w(row), u(row)
        vr = -half * (u(row - 1) - u(row + 1))
        h1 = jnp.sum(wr * a + ur * m, axis=0, keepdims=True)
        z1 = jnp.sum(wr * (keep * z + rotation * m), axis=0, keepdims=True) - courant * dx(h1)
        m1 = jnp.sum(wr * cc + ur * a + vr * m, axis=0, keepdims=True)
        for f, value in enumerate((h1, z1, m1)):
            ends_ref[end, f, pl.ds(mem, 1), :] = value
    return total


def nest_kernel(
    bands,
    span,
    off_ref,
    nest_ref,
    parent_ref,
    nest_out,
    patch,
    halo,
    par_ref,
    edge_ref,
    strip_ref,
    ends_ref,
    given,
    taken,
    known,
    strips,
    endbuf,
    cols,
    sides,
    ghost,
    acc,
    fine,
    thinned,
    dealt,
    cbuf,
    sbuf,
    nest_send,
    nest_recv,
    edge_send,
    edge_recv,
    strip_send,
    strip_recv,
    end_send,
    end_recv,
    mid_send,
    mid_recv,
    out_send,
    out_recv,
    local_sem,
    parent_sem,
):
    me = lax.axis_index("band")
    group = lax.axis_index("member")
    members, _, nrows, nwidth = nest_ref.shape
    prows = strip_ref.shape[0]
    tile = nrows // 3
    per = bands // members
    top_senders = bands // 2 + 1

    def remote(src, dst, send, recv, to):
        return pltpu.make_async_remote_copy(
            src_ref=src, dst_ref=dst, send_sem=send, recv_sem=recv, device_id=(group, to), device_id_type=MESH
        )

    barrier = pltpu.get_barrier_semaphore()

    def greet(j, _):
        pl.semaphore_signal(barrier, inc=1, device_id=(group, lax.rem(me + j, bands)), device_id_type=MESH)
        return 0

    lax.fori_loop(1, bands, greet, 0)
    own = pltpu.make_async_copy(nest_ref, nest_out, local_sem)
    load = pltpu.make_async_copy(parent_ref, par_ref, parent_sem)
    load.start()
    own.start()
    pl.semaphore_wait(barrier, bands - 1)

    def nest_copy(step, way, mem, to):
        return remote(
            given.at[step, way, mem], taken.at[step, way, mem], nest_send.at[step, way, mem], nest_recv.at[step, way, mem], to
        )

    def edge_copy(piece, way, mem, to):
        return remote(
            edge_ref.at[way, mem], halo.at[way, mem], edge_send.at[piece, way, mem], edge_recv.at[piece, way, mem], to
        )

    def strip_copy(slot, to, index):
        return remote(strip_ref, strips.at[pl.ds(pl.multiple_of((slot + 1) * prows, prows), prows), :], strip_send.at[index], strip_recv.at[slot], to)

    def end_copy(end, slot, to):
        return remote(ends_ref.at[end], endbuf.at[slot], end_send.at[end], end_recv.at[slot], to)

    first, last = me == 0, me == bands - 1

    def send_up_down(copy, a, mem):
        @pl.when(jnp.logical_not(first))
        def _():
            copy(a, 0, mem, me - 1).start()

        @pl.when(jnp.logical_not(last))
        def _():
            copy(a, 1, mem, me + 1).start()

    def await_up_down(copy, a, mem):
        @pl.when(jnp.logical_not(last))
        def _():
            copy(a, 0, mem, me).wait_recv()

        @pl.when(jnp.logical_not(first))
        def _():
            copy(a, 1, mem, me).wait_recv()

    def sent_up_down(copy, a, mem):
        @pl.when(jnp.logical_not(first))
        def _():
            copy(a, 0, mem, me).wait_send()

        @pl.when(jnp.logical_not(last))
        def _():
            copy(a, 1, mem, me).wait_send()

    def gather(mem, _):
        edge_rows(mem, par_ref, edge_ref)
        send_up_down(edge_copy, 0, mem)
        strip_ref[...] += window_shares(mem, span, off_ref[mem, 0], off_ref[mem, 1], me, par_ref, ends_ref)
        return 0

    strip_ref[...] = jnp.zeros_like(strip_ref)
    load.wait()
    lax.fori_loop(0, members, gather, 0)

    def send_strip(j, _):
        strip_copy(me, lax.rem(me + j, bands), j).start()
        return 0

    lax.fori_loop(1, bands, send_strip, 0)

    sends_top = jnp.logical_and(me > 0, me < top_senders)
    sends_bottom = jnp.logical_and(me < bands - 1, me >= bands - top_senders)

    @pl.when(sends_top)
    def _():
        end_copy(0, me, 0).start()

    @pl.when(sends_bottom)
    def _():
        end_copy(1, bands - 1 - me, bands - 1).start()

    pad = strips.shape[0] - (bands + 1) * prows
    strips[pl.ds(0, prows), :] = jnp.zeros((prows, LANES), jnp.float32)
    strips[pl.ds((bands + 1) * prows, pad), :] = jnp.zeros((pad, LANES), jnp.float32)
    strips[pl.ds(pl.multiple_of((me + 1) * prows, prows), prows), :] = strip_ref[...]
    cpad = (cbuf.shape[2] - bands * tile) // 2
    blank = jnp.zeros((span // LANES, 3, cpad, LANES), jnp.float32)
    cbuf[:, :, pl.ds(0, cpad), :] = blank
    cbuf[:, :, pl.ds(cpad + bands * tile, cpad), :] = blank

    ends_lane = span + LANES

    @pl.when(jnp.logical_or(first, last))
    def _():
        j = iota((1, nwidth), 1) + 2
        q, t = j // 3, j % 3
        k = iota((ends_lane, nwidth), 0) - 3
        fine[...] = (jnp.where(k == q, 3 - t, 0) + jnp.where(k == q + 1, t, 0)).astype(jnp.float32).astype(jnp.bfloat16)

    e = iota((nrows, prows), 0) + 2
    q, t = e // 3, e % 3
    k = iota((nrows, prows), 1)
    weights = jnp.where(k == q, (3 - t).astype(jnp.float32) / 3.0, 0.0) + jnp.where(
        k == q + 1, t.astype(jnp.float32) / 3.0, 0.0
    )
    thin = jnp.where(iota((nwidth, span), 0) // 3 == iota((nwidth, span), 1), 1.0, 0.0).astype(jnp.bfloat16)
    row = iota((nrows, nwidth), 0)
    col = iota((nrows, nwidth), 1)
    at_west, at_east = col == 0, col == nwidth - 1
    at_top, at_bottom = row == 0, row == nrows - 1
    lanes = iota((nrows, LANES), 1)

    def recv_strip(j, _):
        strip_copy(lax.rem(me + j, bands), me, j).wait_recv()
        return 0

    lax.fori_loop(1, bands, recv_strip, 0)

    g = strips[...]
    lane = iota((1, LANES), 1)
    turn = lane_roll(g, -16)
    height = g + jnp.where(lane < 16, -half, courant * half) * (row_roll(turn, -1) - row_roll(turn, 1))
    turn = lane_roll(height, 64)
    cols[...] = jnp.where(lane < 64, height, g - half * (row_roll(turn, -1) - row_roll(turn, 1)))
    picked = jnp.zeros((prows, LANES), jnp.float32)
    for mem in range(members):
        begin = off_ref[mem, 0] + (me * tile - 1 + prows)
        picked = jnp.where(lane % 32 // 2 == mem, cols[pl.ds(begin, prows), :], picked)
    side = jnp.dot(weights, picked, precision=highest, preferred_element_type=jnp.float32)
    for mem in range(members):
        for f in range(2):
            for s in range(2):
                k = 32 * f + s + 2 * mem
                sides[mem, 2 * f + s] = jnp.broadcast_to(side[:, k : k + 1], (nrows, LANES))
    own.wait()

    def ddx(x, f, mem):
        west, east = [jnp.concatenate([sides[mem, 2 * f + s]] * (nwidth // LANES), axis=-1) for s in range(2)]
        return jnp.where(at_east, east, lane_roll(x, -1)) - jnp.where(at_west, west, lane_roll(x, 1))

    def ddy(x, above, below):
        return jnp.where(at_bottom, below, row_roll(x, -1)) - jnp.where(at_top, above, row_roll(x, 1))

    def give(step, mem, h, z, m):
        q = h - half * ddx(z, 1, mem)
        known[mem] = q
        given[step, 0, mem, 0:1] = m[0:1]
        given[step, 0, mem, 1:2] = q[0:1] - half * m[1:2]
        given[step, 1, mem, 0:1] = m[nrows - 1 : nrows]
        given[step, 1, mem, 1:2] = q[nrows - 1 : nrows] + half * m[nrows - 2 : nrows - 1]
        send_up_down(nest_copy, step, mem)

    def give_first(mem, _):
        give(0, mem, nest_out[mem, 0], nest_out[mem, 1], nest_out[mem, 2])
        return 0

    lax.fori_loop(0, members, give_first, 0)

    def add_end(k, _):
        @pl.when(k > 0)
        def _():
            end_copy(0, k, 0).wait_recv()

        acc[...] += endbuf[k]
        return 0

    @pl.when(first)
    def _():
        endbuf[0] = ends_ref[0]

    @pl.when(last)
    def _():
        endbuf[0] = ends_ref[1]

    @pl.when(jnp.logical_or(first, last))
    def _():
        acc[...] = jnp.zeros_like(acc)
        lax.fori_loop(0, top_senders, add_end, 0)
        rows_in = acc[...].reshape(3 * members, ends_lane)
        ghost[...] = (exact_dot(rows_in, fine[...]) * (1.0 / 3.0)).reshape(3, members, nwidth)

    turn_of = lax.rem(group, per)

    def mid_copy(mem, slot, to):
        return remote(
            dealt.at[mem],
            cbuf.at[:, :, pl.ds(pl.multiple_of(cpad + slot * tile, tile), tile), :],
            mid_send.at[mem],
            mid_recv.at[slot],
            to,
        )

    def one_member(step, mem, _):
        await_up_down(nest_copy, step, mem)
        z, m = nest_out[mem, 1], nest_out[mem, 2]
        h_ghost, m_ghost = ghost[0, pl.ds(mem, 1), :], ghost[2, pl.ds(mem, 1), :]
        m_above = jnp.where(first, m_ghost, taken[step, 1, mem, 0:1])
        h_above = jnp.where(first, h_ghost, taken[step, 1, mem, 1:2] - half * m[0:1])
        m_below = jnp.where(last, m_ghost, taken[step, 0, mem, 0:1])
        h_below = jnp.where(last, h_ghost, taken[step, 0, mem, 1:2] + half * m[nrows - 1 : nrows])
        h = known[mem] - half * ddy(m, m_above, m_below)
        z, m = (
            keep * z - half * ddx(h, 0, mem) + rotation * m,
            keep * m - half * ddy(h, h_above, h_below) - rotation * z,
        )
        if step < NSTEPS - 1:
            give(step + 1, mem, h, z, m)
            nest_out[mem, 1] = z
            nest_out[mem, 2] = m
            return 0
        inner = (h, z, m)
        for f, x in enumerate(inner):
            nest_out[mem, f] = x
        sums = exact_dot(jnp.concatenate(inner, axis=0), thin)
        for k in range(span // LANES):
            thinned[k] = sums[:, k * LANES : (k + 1) * LANES]
            for f in range(3):
                parts = [thinned[k, pl.ds(f * nrows + i, tile, stride=3), :] for i in range(3)]
                dealt[mem, k, f] = (parts[0] + parts[1] + parts[2]) * (1.0 / 9.0)
        to = per * mem + turn_of

        @pl.when(to != me)
        def _():
            mid_copy(mem, me, to).start()

        @pl.when(to == me)
        def _():
            cbuf[:, :, pl.ds(pl.multiple_of(cpad + me * tile, tile), tile), :] = dealt[mem]

        return 0

    for step in range(NSTEPS):
        lax.fori_loop(0, members, functools.partial(one_member, step), 0)
    is_mid = lax.rem(me, per) == turn_of
    mine = me // per

    def out_copy(to):
        return remote(sbuf.at[to], patch.at[mine], out_send.at[to], out_recv.at[mine], to)

    @pl.when(is_mid)
    def _():
        def recv(j, _):
            mid_copy(0, lax.rem(me + j, bands), me).wait_recv()
            return 0

        lax.fori_loop(1, bands, recv, 0)
        start_row = off_ref[mine, 0]

        def deal(j, _):
            to = lax.rem(me + j, bands)
            begin = jnp.clip(to * prows - start_row, -cpad, bands * tile) + cpad
            for k in range(0, span, LANES):
                sbuf[to, :, :, pl.ds(k, LANES)] = cbuf[k // LANES, :, pl.ds(begin, prows), :]

            @pl.when(to != me)
            def _():
                out_copy(to).start()

            return 0

        lax.fori_loop(1, bands + 1, deal, 0)
        patch[mine] = sbuf[me]

    def recv_patch(mem, _):
        @pl.when(per * mem + turn_of != me)
        def _():
            remote(sbuf.at[0], patch.at[mem], out_send.at[0], out_recv.at[mem], me).wait_recv()

        return 0

    lax.fori_loop(0, members, recv_patch, 0)

    @pl.when(sends_top)
    def _():
        end_copy(0, me, 0).wait_send()

    @pl.when(sends_bottom)
    def _():
        end_copy(1, bands - 1 - me, bands - 1).wait_send()

    def sent_strip(j, _):
        strip_copy(me, lax.rem(me + j, bands), j).wait_send()
        return 0

    lax.fori_loop(1, bands, sent_strip, 0)

    def sent_mid(mem, _):
        await_up_down(edge_copy, 0, mem)
        sent_up_down(edge_copy, 0, mem)
        for step in range(NSTEPS):
            sent_up_down(nest_copy, step, mem)

        @pl.when(per * mem + turn_of != me)
        def _():
            mid_copy(mem, me, me).wait_send()

        return 0

    lax.fori_loop(0, members, sent_mid, 0)

    @pl.when(is_mid)
    def _():
        def sent_out(j, _):
            out_copy(lax.rem(me + j, bands)).wait_send()
            return 0

        lax.fori_loop(1, bands, sent_out, 0)


def parent_kernel(span, bands, off_ref, band_ref, par_ref, halo_ref, patch_ref, out_ref):
    mem = pl.program_id(0)
    rows, width = par_ref.shape[2], par_ref.shape[3]
    row0, col0 = off_ref[mem, 0], off_ref[mem, 1]
    band = band_ref[0]
    first, last = band == 0, band == bands - 1
    h, z, m = par_ref[0, 0], par_ref[0, 1], par_ref[0, 2]
    row = iota(h.shape, 0)

    def ddy(x, above, below):
        up = jnp.where(row == 0, above, row_roll(x, 1))
        down = jnp.where(row == rows - 1, below, row_roll(x, -1))
        return down - up

    m_above = jnp.where(first, 0.0, halo_ref[1, 0, 0:1, :])
    m_below = jnp.where(last, 0.0, halo_ref[0, 0, 0:1, :])
    h_above = jnp.where(first, 0.0, halo_ref[1, 0, 1:2, :] - half * m[0:1])
    h_below = jnp.where(last, 0.0, halo_ref[0, 0, 1:2, :] + half * m[rows - 1 : rows])
    h1 = h - courant * dx(z) - half * ddy(m, m_above, m_below)
    out_ref[0, 0] = h1
    out_ref[0, 1] = keep * z - courant * dx(h1) + rotation * m
    out_ref[0, 2] = keep * m - half * ddy(h1, h_above, h_below) - rotation * z

    block0 = col0 // LANES
    shift = col0 - block0 * LANES
    place = pl.ds(pl.multiple_of(block0 * LANES, LANES), span + LANES)
    wide = jnp.concatenate([patch_ref[0], jnp.zeros((3, rows, LANES), jnp.float32)], axis=-1)
    wide = pltpu.roll(wide.reshape(3 * rows, span + LANES), shift, 1).reshape(3, rows, span + LANES)
    lane = iota(wide.shape, 2)
    at = iota(wide.shape, 1) + (band * rows - row0)
    inside = (lane >= shift) & (lane < shift + span) & (at >= 0) & (at < span)
    out_ref[0, :, :, place] = jnp.where(inside, wide, out_ref[0, :, :, place])


def per_device(bands, parent_state, nest_state, offsets):
    members, _, prows, width = parent_state.shape
    nrows, nwidth = nest_state.shape[2:]
    span = nwidth // 3
    tile = nrows // 3
    f32 = jnp.float32
    band = lax.axis_index("band").reshape(1).astype(jnp.int32)
    shape = jax.ShapeDtypeStruct
    limit = 48 * 1024 * 1024
    parent_spec = pl.BlockSpec((1, 3, prows, width), lambda i, *_: (i, 0, 0, 0))
    edge_spec = pl.BlockSpec((2, 1, 2, width), lambda i, *_: (0, i, 0, 0))

    vmem = pl.BlockSpec(memory_space=pltpu.VMEM)
    hbm = pl.BlockSpec(memory_space=pl.ANY)
    dma = pltpu.SemaphoreType.DMA
    senders = bands // 2 + 1
    nest_out, patch, halo = pl.pallas_call(
        functools.partial(nest_kernel, bands, span),
        out_shape=(
            shape(nest_state.shape, f32),
            shape((members, 3, prows, span), f32),
            shape((2, members, 2, width), f32),
        ),
        in_specs=[pl.BlockSpec(memory_space=pltpu.SMEM), hbm, hbm],
        out_specs=(vmem, vmem, hbm),
        scratch_shapes=[
            pltpu.VMEM((members, 3, prows, width), f32),
            pltpu.VMEM((2, members, 2, width), f32),
            pltpu.VMEM((prows, LANES), f32),
            pltpu.VMEM((2, 3, members, span + LANES), f32),
            pltpu.VMEM((NSTEPS, 2, members, 2, nwidth), f32),
            pltpu.VMEM((NSTEPS, 2, members, 2, nwidth), f32),
            pltpu.VMEM((members, nrows, nwidth), f32),
            pltpu.VMEM(((bands + 2) * prows, LANES), f32),
            pltpu.VMEM((senders, 3, members, span + LANES), f32),
            pltpu.VMEM(((bands + 2) * prows, LANES), f32),
            pltpu.VMEM((members, 4, nrows, LANES), f32),
            pltpu.VMEM((3, members, nwidth), f32),
            pltpu.VMEM((3, members, span + LANES), f32),
            pltpu.VMEM((span + LANES, nwidth), jnp.bfloat16),
            pltpu.VMEM((span // LANES, 3 * nrows, LANES), f32),
            pltpu.VMEM((members, span // LANES, 3, tile, LANES), f32),
            pltpu.VMEM((span // LANES, 3, bands * tile + 2 * prows, LANES), f32),
            pltpu.VMEM((bands, 3, prows, span), f32),
            dma((NSTEPS, 2, members)),
            dma((NSTEPS, 2, members)),
            dma((1, 2, members)),
            dma((1, 2, members)),
            dma((bands,)),
            dma((bands,)),
            dma((2,)),
            dma((senders,)),
            dma((members,)),
            dma((bands,)),
            dma((bands,)),
            dma((members,)),
            dma,
            dma,
        ],
        compiler_params=pltpu.CompilerParams(collective_id=0, has_side_effects=True, vmem_limit_bytes=limit),
        name="nest",
    )(offsets, nest_state, parent_state)

    parent_out = pl.pallas_call(
        functools.partial(parent_kernel, span, bands),
        out_shape=shape(parent_state.shape, f32),
        grid_spec=pltpu.PrefetchScalarGridSpec(
            num_scalar_prefetch=2,
            grid=(members,),
            in_specs=[
                parent_spec,
                edge_spec,
                pl.BlockSpec((1, 3, prows, span), lambda i, *_: (i, 0, 0, 0)),
            ],
            out_specs=parent_spec,
        ),
        compiler_params=pltpu.CompilerParams(vmem_limit_bytes=limit),
        name="parent",
    )(offsets, band, parent_state, halo, patch)
    return (parent_out, nest_out)


def solution(mesh):
    in_specs = (P("member", None, "band", None), P("member", None, "band", None), P("member", None))
    out_specs = (P("member", None, "band", None), P("member", None, "band", None))
    return jax.shard_map(
        functools.partial(per_device, mesh.shape["band"]),
        mesh=mesh,
        in_specs=in_specs,
        out_specs=out_specs,
        check_vma=False,
    )
```

```python
import functools

import jax
import jax.numpy as jnp
from jax import lax
from jax.experimental import pallas as pl
from jax.experimental.pallas import tpu as pltpu
from jax.sharding import PartitionSpec as P

NSTEPS = 3
MESH = pl.DeviceIdType.MESH

courant = 0.9
friction = 0.02
rotation = 0.05
half = 0.5 * courant
keep = 1.0 - friction
highest = lax.Precision.HIGHEST
LANES = 128
HALO = 8


def lane_roll(x, shift):
    size = x.shape[-1]
    return pltpu.roll(x, shift % size, x.ndim - 1)


def row_roll(x, shift):
    size = x.shape[-2]
    return pltpu.roll(x, shift % size, x.ndim - 2)


def dx(x):
    return 0.5 * (lane_roll(x, -1) - lane_roll(x, 1))


def iota(shape, dim):
    return lax.broadcasted_iota(jnp.int32, shape, dim)


def split(x):
    high = x.astype(jnp.bfloat16)
    rest = x - high.astype(jnp.float32)
    mid = rest.astype(jnp.bfloat16)
    return high, mid, (rest - mid.astype(jnp.float32)).astype(jnp.bfloat16)


def exact_dot(x, weights):
    count = x.shape[0]
    parts = jnp.concatenate([part.astype(jnp.float32) for part in split(x)], axis=0).astype(jnp.bfloat16)
    out = jnp.dot(parts, weights, preferred_element_type=jnp.float32)
    return out[:count] + out[count : 2 * count] + out[2 * count :]


def edge_rows(mem, par_ref, edge_ref):
    rows = par_ref.shape[2]
    z_top, z_bot = par_ref[mem, 1, 0:1, :], par_ref[mem, 1, rows - 1 : rows, :]
    m_top, m_bot = par_ref[mem, 2, 0:1, :], par_ref[mem, 2, rows - 1 : rows, :]
    edge_ref[0, mem, 0:1, :] = m_top
    edge_ref[0, mem, 1:2, :] = par_ref[mem, 0, 0:1, :] - courant * dx(z_top) - half * par_ref[mem, 2, 1:2, :]
    edge_ref[1, mem, 0:1, :] = m_bot
    edge_ref[1, mem, 1:2, :] = (
        par_ref[mem, 0, rows - 1 : rows, :] - courant * dx(z_bot) + half * par_ref[mem, 2, rows - 2 : rows - 1, :]
    )


def window_shares(mem, span, row0, col0, band, par_ref, ends_ref):
    rows, width = par_ref.shape[2], par_ref.shape[3]
    blocks = width // LANES
    count = span // LANES + 2
    first = lax.rem(col0 - 4 + width, width)
    block0 = lax.div(first, LANES)
    shift = first - block0 * LANES
    wanted = [jnp.zeros((rows, LANES), jnp.int32) + lax.rem(block0 + k, blocks) for k in range(count)]
    parts = [jnp.zeros((3, rows, LANES), jnp.float32)] * count
    for place in range(blocks):
        block = par_ref[mem, :, :, place * LANES : (place + 1) * LANES]
        parts = [jnp.where((w == place)[None], block, part) for w, part in zip(wanted, parts)]
    wide = jnp.concatenate(parts, axis=-1).reshape(3 * rows, count * LANES)
    amount = jnp.zeros(wide.shape, jnp.int32) + shift
    for bit in (64, 32, 16, 8, 4, 2, 1):
        wide = jnp.where((amount & bit) != 0, lane_roll(wide, -bit), wide)
    wide = wide[:, : span + LANES].reshape(3, rows, span + LANES)
    h, z, m = wide[0], wide[1], wide[2]
    a = h - courant * dx(z)
    b = keep * z - courant * dx(a) + rotation * m
    cc = keep * m - rotation * z
    shape = h.shape
    lane = iota(shape, 1)
    west = jnp.where(lane == 3, 2.0 / 3.0, 0.0) + jnp.where(lane == 4, 1.0 / 3.0, 0.0)
    east = jnp.where(lane == span + 3, 1.0 / 3.0, 0.0) + jnp.where(lane == span + 4, 2.0 / 3.0, 0.0)
    slot = iota((rows, LANES), 1)
    total = jnp.zeros((rows, LANES), jnp.float32)
    for q, field in enumerate((a, m, b, dx(m), cc)):
        for s, weight in enumerate((west, east)):
            value = jnp.sum(field * weight, axis=1, keepdims=True)
            total = total + jnp.where(slot == q * 16 + s + 2 * mem, value, 0.0)

    row = iota(shape, 0) + band * rows
    for end in range(2):
        near = row0 - 1 if end == 0 else row0 + span - 1
        lo, hi = (2.0 / 3.0, 1.0 / 3.0) if end == 0 else (1.0 / 3.0, 2.0 / 3.0)

        def w(i):
            return jnp.where(i == near, lo, 0.0) + jnp.where(i == near + 1, hi, 0.0)

        def u(i):
            return -half * (w(i - 1) - w(i + 1))

        wr, ur = w(row), u(row)
        vr = -half * (u(row - 1) - u(row + 1))
        h1 = jnp.sum(wr * a + ur * m, axis=0, keepdims=True)
        z1 = jnp.sum(wr * (keep * z + rotation * m), axis=0, keepdims=True) - courant * dx(h1)
        m1 = jnp.sum(wr * cc + ur * a + vr * m, axis=0, keepdims=True)
        for f, value in enumerate((h1, z1, m1)):
            ends_ref[end, f, pl.ds(mem, 1), :] = value
    return total


def nest_kernel(
    bands,
    span,
    off_ref,
    nest_ref,
    parent_ref,
    nest_out,
    patch,
    halo,
    par_ref,
    edge_ref,
    strip_ref,
    ends_ref,
    ext,
    strips,
    endbuf,
    cols,
    side,
    ghost,
    acc,
    fine,
    thinned,
    dealt,
    cbuf,
    sbuf,
    nest_send,
    nest_recv,
    edge_send,
    edge_recv,
    strip_send,
    strip_recv,
    end_send,
    end_recv,
    mid_send,
    mid_recv,
    out_send,
    out_recv,
    local_sem,
    parent_sem,
):
    me = lax.axis_index("band")
    group = lax.axis_index("member")
    members, _, nrows, nwidth = nest_ref.shape
    prows = strip_ref.shape[0]
    tile = nrows // 3
    per = bands // members
    top_senders = bands // 2 + 1

    def remote(src, dst, send, recv, to):
        return pltpu.make_async_remote_copy(
            src_ref=src, dst_ref=dst, send_sem=send, recv_sem=recv, device_id=(group, to), device_id_type=MESH
        )

    barrier = pltpu.get_barrier_semaphore()

    def greet(j, _):
        pl.semaphore_signal(barrier, inc=1, device_id=(group, lax.rem(me + j, bands)), device_id_type=MESH)
        return 0

    lax.fori_loop(1, bands, greet, 0)
    own = pltpu.make_async_copy(nest_ref, ext.at[:, :, pl.ds(HALO, nrows), :], local_sem)
    load = pltpu.make_async_copy(parent_ref, par_ref, parent_sem)
    load.start()
    own.start()
    pl.semaphore_wait(barrier, bands - 1)

    reach = 2 * NSTEPS

    def nest_down(mem, to):
        return remote(
            nest_ref.at[mem, :, pl.ds(nrows - reach, reach), :],
            ext.at[mem, :, pl.ds(HALO - reach, reach), :],
            nest_send.at[0, mem],
            nest_recv.at[0, mem],
            to,
        )

    def nest_up(mem, to):
        return remote(
            nest_ref.at[mem, :, pl.ds(0, reach), :],
            ext.at[mem, :, pl.ds(HALO + nrows, reach), :],
            nest_send.at[1, mem],
            nest_recv.at[1, mem],
            to,
        )

    def edge_down(to):
        return remote(edge_ref.at[1], halo.at[0], edge_send.at[0], edge_recv.at[0], to)

    def edge_up(to):
        return remote(edge_ref.at[0], halo.at[1], edge_send.at[1], edge_recv.at[1], to)

    def strip_copy(slot, to, index):
        return remote(strip_ref, strips.at[pl.ds(pl.multiple_of((slot + 1) * prows, prows), prows), :], strip_send.at[index], strip_recv.at[slot], to)

    def end_copy(end, slot, to):
        return remote(ends_ref.at[end], endbuf.at[slot], end_send.at[end], end_recv.at[slot], to)

    first, last = me == 0, me == bands - 1

    def gather(mem, _):
        @pl.when(jnp.logical_not(first))
        def _():
            nest_up(mem, me - 1).start()

        @pl.when(jnp.logical_not(last))
        def _():
            nest_down(mem, me + 1).start()

        strip_ref[...] += window_shares(mem, span, off_ref[0, mem], off_ref[1, mem], me, par_ref, ends_ref)
        return 0

    strip_ref[...] = jnp.zeros_like(strip_ref)
    load.wait()
    lax.fori_loop(0, members, gather, 0)

    def send_strip(j, _):
        strip_copy(me, lax.rem(me + j, bands), j).start()
        return 0

    lax.fori_loop(1, bands, send_strip, 0)

    sends_top = jnp.logical_and(me > 0, me < top_senders)
    sends_bottom = jnp.logical_and(me < bands - 1, me >= bands - top_senders)

    @pl.when(sends_top)
    def _():
        end_copy(0, me, 0).start()

    @pl.when(sends_bottom)
    def _():
        end_copy(1, bands - 1 - me, bands - 1).start()

    def send_edges(mem, _):
        edge_rows(mem, par_ref, edge_ref)
        return 0

    lax.fori_loop(0, members, send_edges, 0)

    @pl.when(jnp.logical_not(first))
    def _():
        edge_up(me - 1).start()

    @pl.when(jnp.logical_not(last))
    def _():
        edge_down(me + 1).start()

    pad = strips.shape[0] - (bands + 1) * prows
    strips[pl.ds(0, prows), :] = jnp.zeros((prows, LANES), jnp.float32)
    strips[pl.ds((bands + 1) * prows, pad), :] = jnp.zeros((pad, LANES), jnp.float32)
    strips[pl.ds(pl.multiple_of((me + 1) * prows, prows), prows), :] = strip_ref[...]
    cpad = (cbuf.shape[2] - bands * tile) // 2
    blank = jnp.zeros((span // LANES, 3, cpad, LANES), jnp.float32)
    cbuf[:, :, pl.ds(0, cpad), :] = blank
    cbuf[:, :, pl.ds(cpad + bands * tile, cpad), :] = blank

    ends_lane = span + LANES

    @pl.when(jnp.logical_or(first, last))
    def _():
        j = iota((1, nwidth), 1) + 2
        q, t = j // 3, j % 3
        k = iota((ends_lane, nwidth), 0) - 3
        fine[...] = (jnp.where(k == q, 3 - t, 0) + jnp.where(k == q + 1, t, 0)).astype(jnp.float32).astype(jnp.bfloat16)

    erows = nrows + 2 * HALO
    e = iota((erows, prows), 0)
    q, t = e // 3, e % 3
    k = iota((erows, prows), 1)
    weights = jnp.where(k == q, (3 - t).astype(jnp.float32) / 3.0, 0.0) + jnp.where(
        k == q + 1, t.astype(jnp.float32) / 3.0, 0.0
    )
    thin = jnp.where(iota((nwidth, span), 0) // 3 == iota((nwidth, span), 1), 1.0, 0.0).astype(jnp.bfloat16)
    row = iota((erows, nwidth), 0)
    col = iota((erows, nwidth), 1)
    is_ghost = jnp.logical_or(
        jnp.logical_and(row == HALO - 1, first), jnp.logical_and(row == HALO + nrows, last)
    )
    at_west, at_east = col == 0, col == nwidth - 1
    lanes = iota((erows, LANES), 1)

    def recv_strip(j, _):
        strip_copy(lax.rem(me + j, bands), me, j).wait_recv()
        return 0

    lax.fori_loop(1, bands, recv_strip, 0)

    g = strips[...]
    lane = iota((1, LANES), 1)
    turn = lane_roll(g, -16)
    height = g + jnp.where(lane < 16, -half, courant * half) * (row_roll(turn, -1) - row_roll(turn, 1))
    turn = lane_roll(height, 64)
    cols[...] = jnp.where(lane < 64, height, g - half * (row_roll(turn, -1) - row_roll(turn, 1)))
    picked = jnp.zeros((prows, LANES), jnp.float32)
    for mem in range(members):
        begin = off_ref[0, mem] + (me * tile - 3 + prows)
        picked = jnp.where(lane % 32 // 2 == mem, cols[pl.ds(begin, prows), :], picked)
    side[...] = jnp.dot(weights, picked, precision=highest, preferred_element_type=jnp.float32)


    def add_end(k, _):
        @pl.when(k > 0)
        def _():
            end_copy(0, k, 0).wait_recv()

        acc[...] += endbuf[k]
        return 0

    @pl.when(first)
    def _():
        endbuf[0] = ends_ref[0]

    @pl.when(last)
    def _():
        endbuf[0] = ends_ref[1]

    @pl.when(jnp.logical_or(first, last))
    def _():
        acc[...] = jnp.zeros_like(acc)
        lax.fori_loop(0, top_senders, add_end, 0)
        rows_in = acc[...].reshape(3 * members, ends_lane)
        ghost[...] = (exact_dot(rows_in, fine[...]) * (1.0 / 3.0)).reshape(3, members, nwidth)

    own.wait()

    turn_of = lax.rem(group, per)

    def mid_copy(mem, slot, to):
        return remote(
            dealt.at[mem],
            cbuf.at[:, :, pl.ds(pl.multiple_of(cpad + slot * tile, tile), tile), :],
            mid_send.at[mem],
            mid_recv.at[slot],
            to,
        )

    def one_member(mem, slot):
        def side_of(f, s):
            return jnp.sum(jnp.where(lanes == 32 * f + s + 2 * mem, side[...], 0.0), axis=1, keepdims=True)

        sides = [[side_of(f, s) for s in range(2)] for f in range(2)]
        ends = [ghost[f, pl.ds(mem, 1), :] for f in range(3)]

        def ddx(x, f):
            left = jnp.where(at_west, sides[f][0], lane_roll(x, 1))
            right = jnp.where(at_east, sides[f][1], lane_roll(x, -1))
            return right - left

        def ddy(x):
            return row_roll(x, -1) - row_roll(x, 1)

        def bound(x, f):
            return jnp.where(is_ghost, ends[f], x)

        h, z, m = ext[mem, 0], bound(ext[mem, 1], 1), bound(ext[mem, 2], 2)
        for _ in range(NSTEPS):
            h = bound(h - half * (ddx(z, 1) + ddy(m)), 0)
            z, m = (
                bound(keep * z - half * ddx(h, 0) + rotation * m, 1),
                bound(keep * m - half * ddy(h) - rotation * z, 2),
            )
        lines = []
        for f, x in enumerate((h, z, m)):
            x = x[HALO : HALO + nrows]
            nest_out[mem, f] = x
            pieces = []
            for k in range(nwidth // LANES):
                thinned[slot, f, k] = x[:, k * LANES : (k + 1) * LANES]
                a, b, c = [thinned[slot, f, k, pl.ds(i, tile, stride=3), :] for i in range(3)]
                pieces.append(a + b + c)
            lines.append(jnp.concatenate(pieces, axis=-1))
        return lines

    def pair(i, _):
        group_of = [2 * i, 2 * i + 1]
        for mem in group_of:
            @pl.when(jnp.logical_not(first))
            def _():
                nest_down(mem, me).wait_recv()

            @pl.when(jnp.logical_not(last))
            def _():
                nest_up(mem, me).wait_recv()

        lines = [one_member(mem, slot) for slot, mem in enumerate(group_of)]
        means = exact_dot(jnp.concatenate(lines[0] + lines[1], axis=0), thin) * (1.0 / 9.0)
        for slot, mem in enumerate(group_of):
            for f in range(3):
                at = (3 * slot + f) * tile
                for k in range(span // LANES):
                    dealt[mem, k, f] = means[at : at + tile, k * LANES : (k + 1) * LANES]
            to = per * mem + turn_of

            @pl.when(to != me)
            def _():
                mid_copy(mem, me, to).start()

            @pl.when(to == me)
            def _():
                cbuf[:, :, pl.ds(pl.multiple_of(cpad + me * tile, tile), tile), :] = dealt[mem]

        return 0

    lax.fori_loop(0, members // 2, pair, 0)
    is_mid = lax.rem(me, per) == turn_of
    mine = me // per

    def out_copy(to):
        return remote(sbuf.at[to], patch.at[mine], out_send.at[to], out_recv.at[mine], to)

    @pl.when(is_mid)
    def _():
        def recv(j, _):
            mid_copy(0, lax.rem(me + j, bands), me).wait_recv()
            return 0

        lax.fori_loop(1, bands, recv, 0)
        start_row = off_ref[0, mine]

        def deal(j, _):
            to = lax.rem(me + j, bands)
            begin = jnp.clip(to * prows - start_row, -cpad, bands * tile) + cpad
            for k in range(0, span, LANES):
                sbuf[to, :, :, pl.ds(k, LANES)] = cbuf[k // LANES, :, pl.ds(begin, prows), :]

            @pl.when(to != me)
            def _():
                out_copy(to).start()

            return 0

        lax.fori_loop(1, bands + 1, deal, 0)
        patch[mine] = sbuf[me]

    def recv_patch(mem, _):
        @pl.when(per * mem + turn_of != me)
        def _():
            remote(sbuf.at[0], patch.at[mem], out_send.at[0], out_recv.at[mem], me).wait_recv()

        return 0

    lax.fori_loop(0, members, recv_patch, 0)

    @pl.when(jnp.logical_not(first))
    def _():
        edge_down(me).wait_recv()
        edge_up(me).wait_send()

    @pl.when(jnp.logical_not(last))
    def _():
        edge_up(me).wait_recv()
        edge_down(me).wait_send()

    @pl.when(sends_top)
    def _():
        end_copy(0, me, 0).wait_send()

    @pl.when(sends_bottom)
    def _():
        end_copy(1, bands - 1 - me, bands - 1).wait_send()

    def sent_strip(j, _):
        strip_copy(me, lax.rem(me + j, bands), j).wait_send()
        return 0

    lax.fori_loop(1, bands, sent_strip, 0)

    def sent_mid(mem, _):
        @pl.when(jnp.logical_not(first))
        def _():
            nest_up(mem, me).wait_send()

        @pl.when(jnp.logical_not(last))
        def _():
            nest_down(mem, me).wait_send()

        @pl.when(per * mem + turn_of != me)
        def _():
            mid_copy(mem, me, me).wait_send()

        return 0

    lax.fori_loop(0, members, sent_mid, 0)

    @pl.when(is_mid)
    def _():
        def sent_out(j, _):
            out_copy(lax.rem(me + j, bands)).wait_send()
            return 0

        lax.fori_loop(1, bands, sent_out, 0)


def parent_kernel(span, bands, off_ref, band_ref, par_ref, halo_ref, patch_ref, nest_ref, out_ref, nest_out):
    nest_out[...] = nest_ref[...]
    mem = pl.program_id(0)
    rows, width = par_ref.shape[2], par_ref.shape[3]
    row0, col0 = off_ref[0, mem], off_ref[1, mem]
    band = band_ref[0]
    first, last = band == 0, band == bands - 1
    h, z, m = par_ref[0, 0], par_ref[0, 1], par_ref[0, 2]
    row = iota(h.shape, 0)

    def ddy(x, above, below):
        up = jnp.where(row == 0, above, row_roll(x, 1))
        down = jnp.where(row == rows - 1, below, row_roll(x, -1))
        return down - up

    m_above = jnp.where(first, 0.0, halo_ref[0, 0, 0:1, :])
    m_below = jnp.where(last, 0.0, halo_ref[1, 0, 0:1, :])
    h_above = jnp.where(first, 0.0, halo_ref[0, 0, 1:2, :] - half * m[0:1])
    h_below = jnp.where(last, 0.0, halo_ref[1, 0, 1:2, :] + half * m[rows - 1 : rows])
    h1 = h - courant * dx(z) - half * ddy(m, m_above, m_below)
    out_ref[0, 0] = h1
    out_ref[0, 1] = keep * z - courant * dx(h1) + rotation * m
    out_ref[0, 2] = keep * m - half * ddy(h1, h_above, h_below) - rotation * z

    block0 = col0 // LANES
    shift = col0 - block0 * LANES
    place = pl.ds(pl.multiple_of(block0 * LANES, LANES), span + LANES)
    wide = jnp.concatenate([patch_ref[0], jnp.zeros((3, rows, LANES), jnp.float32)], axis=-1)
    wide = pltpu.roll(wide.reshape(3 * rows, span + LANES), shift, 1).reshape(3, rows, span + LANES)
    lane = iota(wide.shape, 2)
    at = iota(wide.shape, 1) + (band * rows - row0)
    inside = (lane >= shift) & (lane < shift + span) & (at >= 0) & (at < span)
    out_ref[0, :, :, place] = jnp.where(inside, wide, out_ref[0, :, :, place])


def per_device(bands, parent_state, nest_state, offsets):
    members, _, prows, width = parent_state.shape
    nrows, nwidth = nest_state.shape[2:]
    span = nwidth // 3
    tile = nrows // 3
    f32 = jnp.float32
    band = lax.axis_index("band").reshape(1).astype(jnp.int32)
    offsets = offsets.T
    shape = jax.ShapeDtypeStruct
    limit = 60 * 1024 * 1024
    parent_spec = pl.BlockSpec((1, 3, prows, width), lambda i, *_: (i, 0, 0, 0))
    edge_spec = pl.BlockSpec((2, 1, 2, width), lambda i, *_: (0, i, 0, 0))

    vmem = pl.BlockSpec(memory_space=pltpu.VMEM)
    hbm = pl.BlockSpec(memory_space=pl.ANY)
    dma = pltpu.SemaphoreType.DMA
    senders = bands // 2 + 1
    nest_out, patch, halo = pl.pallas_call(
        functools.partial(nest_kernel, bands, span),
        out_shape=(
            shape(nest_state.shape, f32),
            shape((members, 3, prows, span), f32),
            shape((2, members, 2, width), f32),
        ),
        in_specs=[pl.BlockSpec(memory_space=pltpu.SMEM), hbm, hbm],
        out_specs=(vmem, vmem, hbm),
        scratch_shapes=[
            pltpu.VMEM((members, 3, prows, width), f32),
            pltpu.VMEM((2, members, 2, width), f32),
            pltpu.VMEM((prows, LANES), f32),
            pltpu.VMEM((2, 3, members, span + LANES), f32),
            pltpu.VMEM((members, 3, nrows + 2 * HALO, nwidth), f32),
            pltpu.VMEM(((bands + 2) * prows, LANES), f32),
            pltpu.VMEM((senders, 3, members, span + LANES), f32),
            pltpu.VMEM(((bands + 2) * prows, LANES), f32),
            pltpu.VMEM((nrows + 2 * HALO, LANES), f32),
            pltpu.VMEM((3, members, nwidth), f32),
            pltpu.VMEM((3, members, span + LANES), f32),
            pltpu.VMEM((span + LANES, nwidth), jnp.bfloat16),
            pltpu.VMEM((2, 3, nwidth // LANES, nrows, LANES), f32),
            pltpu.VMEM((members, span // LANES, 3, tile, LANES), f32),
            pltpu.VMEM((span // LANES, 3, bands * tile + 2 * prows, LANES), f32),
            pltpu.VMEM((bands, 3, prows, span), f32),
            dma((2, members)),
            dma((2, members)),
            dma((2,)),
            dma((2,)),
            dma((bands,)),
            dma((bands,)),
            dma((2,)),
            dma((senders,)),
            dma((members,)),
            dma((bands,)),
            dma((bands,)),
            dma((members,)),
            dma,
            dma,
        ],
        compiler_params=pltpu.CompilerParams(collective_id=0, has_side_effects=True, vmem_limit_bytes=limit),
        name="nest",
    )(offsets, nest_state, parent_state)

    nest_spec = pl.BlockSpec((1, 3, nrows, nwidth), lambda i, *_: (i, 0, 0, 0))
    return pl.pallas_call(
        functools.partial(parent_kernel, span, bands),
        out_shape=(shape(parent_state.shape, f32), shape(nest_state.shape, f32)),
        grid_spec=pltpu.PrefetchScalarGridSpec(
            num_scalar_prefetch=2,
            grid=(members,),
            in_specs=[
                parent_spec,
                edge_spec,
                pl.BlockSpec((1, 3, prows, span), lambda i, *_: (i, 0, 0, 0)),
                nest_spec,
            ],
            out_specs=(parent_spec, nest_spec),
        ),
        compiler_params=pltpu.CompilerParams(vmem_limit_bytes=limit),
        name="parent",
    )(offsets, band, parent_state, halo, patch, nest_out)


def solution(mesh):
    in_specs = (P("member", None, "band", None), P("member", None, "band", None), P("member", None))
    out_specs = (P("member", None, "band", None), P("member", None, "band", None))
    return jax.shard_map(
        functools.partial(per_device, mesh.shape["band"]),
        mesh=mesh,
        in_specs=in_specs,
        out_specs=out_specs,
        check_vma=False,
    )
```

```python
import functools

import jax
import jax.numpy as jnp
from jax import lax
from jax.experimental import pallas as pl
from jax.experimental.pallas import tpu as pltpu
from jax.sharding import PartitionSpec as P

NSTEPS = 3
MESH = pl.DeviceIdType.MESH

courant = 0.9
friction = 0.02
rotation = 0.05
half = 0.5 * courant
keep = 1.0 - friction
highest = lax.Precision.HIGHEST
LANES = 128
HALO = 8


def lane_roll(x, shift):
    size = x.shape[-1]
    return pltpu.roll(x, shift % size, x.ndim - 1)


def row_roll(x, shift):
    size = x.shape[-2]
    return pltpu.roll(x, shift % size, x.ndim - 2)


def dx(x):
    return 0.5 * (lane_roll(x, -1) - lane_roll(x, 1))


def iota(shape, dim):
    return lax.broadcasted_iota(jnp.int32, shape, dim)


def split(x):
    high = x.astype(jnp.bfloat16)
    rest = x - high.astype(jnp.float32)
    mid = rest.astype(jnp.bfloat16)
    return high, mid, (rest - mid.astype(jnp.float32)).astype(jnp.bfloat16)


def exact_dot(x, weights):
    count = x.shape[0]
    parts = jnp.concatenate([part.astype(jnp.float32) for part in split(x)], axis=0).astype(jnp.bfloat16)
    out = jnp.dot(parts, weights, preferred_element_type=jnp.float32)
    return out[:count] + out[count : 2 * count] + out[2 * count :]


def edge_rows(mem, par_ref, edge_ref):
    rows = par_ref.shape[2]
    z_top, z_bot = par_ref[mem, 1, 0:1, :], par_ref[mem, 1, rows - 1 : rows, :]
    m_top, m_bot = par_ref[mem, 2, 0:1, :], par_ref[mem, 2, rows - 1 : rows, :]
    edge_ref[0, mem, 0:1, :] = m_top
    edge_ref[0, mem, 1:2, :] = par_ref[mem, 0, 0:1, :] - courant * dx(z_top) - half * par_ref[mem, 2, 1:2, :]
    edge_ref[1, mem, 0:1, :] = m_bot
    edge_ref[1, mem, 1:2, :] = (
        par_ref[mem, 0, rows - 1 : rows, :] - courant * dx(z_bot) + half * par_ref[mem, 2, rows - 2 : rows - 1, :]
    )


def window_shares(mem, span, row0, col0, band, par_ref, ends_ref):
    rows, width = par_ref.shape[2], par_ref.shape[3]
    blocks = width // LANES
    count = span // LANES + 2
    first = lax.rem(col0 - 4 + width, width)
    block0 = lax.div(first, LANES)
    shift = first - block0 * LANES
    wanted = [jnp.zeros((rows, LANES), jnp.int32) + lax.rem(block0 + k, blocks) for k in range(count)]
    parts = [jnp.zeros((3, rows, LANES), jnp.float32)] * count
    for place in range(blocks):
        block = par_ref[mem, :, :, place * LANES : (place + 1) * LANES]
        parts = [jnp.where((w == place)[None], block, part) for w, part in zip(wanted, parts)]
    wide = jnp.concatenate(parts, axis=-1).reshape(3 * rows, count * LANES)
    amount = jnp.zeros(wide.shape, jnp.int32) + shift
    for bit in (64, 32, 16, 8, 4, 2, 1):
        wide = jnp.where((amount & bit) != 0, lane_roll(wide, -bit), wide)
    wide = wide[:, : span + LANES].reshape(3, rows, span + LANES)
    h, z, m = wide[0], wide[1], wide[2]
    a = h - courant * dx(z)
    b = keep * z - courant * dx(a) + rotation * m
    cc = keep * m - rotation * z
    shape = h.shape
    lane = iota(shape, 1)
    west = jnp.where(lane == 3, 2.0 / 3.0, 0.0) + jnp.where(lane == 4, 1.0 / 3.0, 0.0)
    east = jnp.where(lane == span + 3, 1.0 / 3.0, 0.0) + jnp.where(lane == span + 4, 2.0 / 3.0, 0.0)
    slot = iota((rows, LANES), 1)
    total = jnp.zeros((rows, LANES), jnp.float32)
    for q, field in enumerate((a, m, b, dx(m), cc)):
        for s, weight in enumerate((west, east)):
            value = jnp.sum(field * weight, axis=1, keepdims=True)
            total = total + jnp.where(slot == q * 16 + s + 2 * mem, value, 0.0)

    row = iota(shape, 0) + band * rows
    for end in range(2):
        near = row0 - 1 if end == 0 else row0 + span - 1
        lo, hi = (2.0 / 3.0, 1.0 / 3.0) if end == 0 else (1.0 / 3.0, 2.0 / 3.0)

        def w(i):
            return jnp.where(i == near, lo, 0.0) + jnp.where(i == near + 1, hi, 0.0)

        def u(i):
            return -half * (w(i - 1) - w(i + 1))

        wr, ur = w(row), u(row)
        vr = -half * (u(row - 1) - u(row + 1))
        h1 = jnp.sum(wr * a + ur * m, axis=0, keepdims=True)
        z1 = jnp.sum(wr * (keep * z + rotation * m), axis=0, keepdims=True) - courant * dx(h1)
        m1 = jnp.sum(wr * cc + ur * a + vr * m, axis=0, keepdims=True)
        for f, value in enumerate((h1, z1, m1)):
            ends_ref[end, f, pl.ds(mem, 1), :] = value
    return total


def inner_step(mem, ref, first, last):
    rows = ref.shape[2]
    h, z, m = ref[mem, 0], ref[mem, 1], ref[mem, 2]
    row = iota(h.shape, 0)
    h_above = jnp.where(first, 0.0, -half * m[0:1])
    h_below = jnp.where(last, 0.0, half * m[rows - 1 : rows])

    def ddy(x, above, below):
        up = jnp.where(row == 0, above, row_roll(x, 1))
        down = jnp.where(row == rows - 1, below, row_roll(x, -1))
        return down - up

    h1 = h - half * (lane_roll(z, -1) - lane_roll(z, 1) + ddy(m, 0.0, 0.0))
    ref[mem, 0] = h1
    ref[mem, 1] = keep * z - half * (lane_roll(h1, -1) - lane_roll(h1, 1)) + rotation * m
    ref[mem, 2] = keep * m - half * ddy(h1, h_above, h_below) - rotation * z


def nest_kernel(
    bands,
    span,
    off_ref,
    nest_ref,
    parent_ref,
    nest_out,
    patch,
    halo,
    stepped,
    par_ref,
    edge_ref,
    strip_ref,
    ends_ref,
    ext,
    strips,
    endbuf,
    cols,
    side,
    ghost,
    acc,
    fine,
    thinned,
    dealt,
    cbuf,
    sbuf,
    nest_send,
    nest_recv,
    edge_send,
    edge_recv,
    strip_send,
    strip_recv,
    end_send,
    end_recv,
    mid_send,
    mid_recv,
    out_send,
    out_recv,
    local_sem,
    parent_sem,
    step_sem,
):
    me = lax.axis_index("band")
    group = lax.axis_index("member")
    members, _, nrows, nwidth = nest_ref.shape
    prows = strip_ref.shape[0]
    tile = nrows // 3
    per = bands // members
    top_senders = bands // 2 + 1

    def remote(src, dst, send, recv, to):
        return pltpu.make_async_remote_copy(
            src_ref=src, dst_ref=dst, send_sem=send, recv_sem=recv, device_id=(group, to), device_id_type=MESH
        )

    barrier = pltpu.get_barrier_semaphore()

    def greet(j, _):
        pl.semaphore_signal(barrier, inc=1, device_id=(group, lax.rem(me + j, bands)), device_id_type=MESH)
        return 0

    lax.fori_loop(1, bands, greet, 0)
    own = pltpu.make_async_copy(nest_ref, ext.at[:, :, pl.ds(HALO, nrows), :], local_sem)
    load = pltpu.make_async_copy(parent_ref, par_ref, parent_sem)
    load.start()
    own.start()
    pl.semaphore_wait(barrier, bands - 1)

    reach = 2 * NSTEPS

    def nest_down(mem, to):
        return remote(
            nest_ref.at[mem, :, pl.ds(nrows - reach, reach), :],
            ext.at[mem, :, pl.ds(HALO - reach, reach), :],
            nest_send.at[0, mem],
            nest_recv.at[0, mem],
            to,
        )

    def nest_up(mem, to):
        return remote(
            nest_ref.at[mem, :, pl.ds(0, reach), :],
            ext.at[mem, :, pl.ds(HALO + nrows, reach), :],
            nest_send.at[1, mem],
            nest_recv.at[1, mem],
            to,
        )

    def edge_down(to):
        return remote(edge_ref.at[1], halo.at[0], edge_send.at[0], edge_recv.at[0], to)

    def edge_up(to):
        return remote(edge_ref.at[0], halo.at[1], edge_send.at[1], edge_recv.at[1], to)

    def strip_copy(slot, to, index):
        return remote(strip_ref, strips.at[pl.ds(pl.multiple_of((slot + 1) * prows, prows), prows), :], strip_send.at[index], strip_recv.at[slot], to)

    def end_copy(end, slot, to):
        return remote(ends_ref.at[end], endbuf.at[slot], end_send.at[end], end_recv.at[slot], to)

    first, last = me == 0, me == bands - 1

    def gather(mem, _):
        @pl.when(jnp.logical_not(first))
        def _():
            nest_up(mem, me - 1).start()

        @pl.when(jnp.logical_not(last))
        def _():
            nest_down(mem, me + 1).start()

        strip_ref[...] += window_shares(mem, span, off_ref[0, mem], off_ref[1, mem], me, par_ref, ends_ref)
        return 0

    strip_ref[...] = jnp.zeros_like(strip_ref)
    load.wait()
    lax.fori_loop(0, members, gather, 0)

    def send_strip(j, _):
        strip_copy(me, lax.rem(me + j, bands), j).start()
        return 0

    lax.fori_loop(1, bands, send_strip, 0)

    sends_top = jnp.logical_and(me > 0, me < top_senders)
    sends_bottom = jnp.logical_and(me < bands - 1, me >= bands - top_senders)

    @pl.when(sends_top)
    def _():
        end_copy(0, me, 0).start()

    @pl.when(sends_bottom)
    def _():
        end_copy(1, bands - 1 - me, bands - 1).start()

    pad = strips.shape[0] - (bands + 1) * prows
    strips[pl.ds(0, prows), :] = jnp.zeros((prows, LANES), jnp.float32)
    strips[pl.ds((bands + 1) * prows, pad), :] = jnp.zeros((pad, LANES), jnp.float32)
    strips[pl.ds(pl.multiple_of((me + 1) * prows, prows), prows), :] = strip_ref[...]
    cpad = (cbuf.shape[2] - bands * tile) // 2
    blank = jnp.zeros((span // LANES, 3, cpad, LANES), jnp.float32)
    cbuf[:, :, pl.ds(0, cpad), :] = blank
    cbuf[:, :, pl.ds(cpad + bands * tile, cpad), :] = blank

    ends_lane = span + LANES

    @pl.when(jnp.logical_or(first, last))
    def _():
        j = iota((1, nwidth), 1) + 2
        q, t = j // 3, j % 3
        k = iota((ends_lane, nwidth), 0) - 3
        fine[...] = (jnp.where(k == q, 3 - t, 0) + jnp.where(k == q + 1, t, 0)).astype(jnp.float32).astype(jnp.bfloat16)

    erows = nrows + 2 * HALO
    e = iota((erows, prows), 0)
    q, t = e // 3, e % 3
    k = iota((erows, prows), 1)
    weights = jnp.where(k == q, (3 - t).astype(jnp.float32) / 3.0, 0.0) + jnp.where(
        k == q + 1, t.astype(jnp.float32) / 3.0, 0.0
    )
    thin = jnp.where(iota((nwidth, span), 0) // 3 == iota((nwidth, span), 1), 1.0, 0.0).astype(jnp.bfloat16)
    row = iota((erows, nwidth), 0)
    col = iota((erows, nwidth), 1)
    is_ghost = jnp.logical_or(
        jnp.logical_and(row == HALO - 1, first), jnp.logical_and(row == HALO + nrows, last)
    )
    at_west, at_east = col == 0, col == nwidth - 1
    lanes = iota((erows, LANES), 1)

    def recv_strip(j, _):
        strip_copy(lax.rem(me + j, bands), me, j).wait_recv()
        return 0

    lax.fori_loop(1, bands, recv_strip, 0)

    g = strips[...]
    lane = iota((1, LANES), 1)
    turn = lane_roll(g, -16)
    height = g + jnp.where(lane < 16, -half, courant * half) * (row_roll(turn, -1) - row_roll(turn, 1))
    turn = lane_roll(height, 64)
    cols[...] = jnp.where(lane < 64, height, g - half * (row_roll(turn, -1) - row_roll(turn, 1)))
    picked = jnp.zeros((prows, LANES), jnp.float32)
    for mem in range(members):
        begin = off_ref[0, mem] + (me * tile - 3 + prows)
        picked = jnp.where(lane % 32 // 2 == mem, cols[pl.ds(begin, prows), :], picked)
    side[...] = jnp.dot(weights, picked, precision=highest, preferred_element_type=jnp.float32)


    def add_end(k, _):
        @pl.when(k > 0)
        def _():
            end_copy(0, k, 0).wait_recv()

        acc[...] += endbuf[k]
        return 0

    @pl.when(first)
    def _():
        endbuf[0] = ends_ref[0]

    @pl.when(last)
    def _():
        endbuf[0] = ends_ref[1]

    @pl.when(jnp.logical_or(first, last))
    def _():
        acc[...] = jnp.zeros_like(acc)
        lax.fori_loop(0, top_senders, add_end, 0)
        rows_in = acc[...].reshape(3 * members, ends_lane)
        ghost[...] = (exact_dot(rows_in, fine[...]) * (1.0 / 3.0)).reshape(3, members, nwidth)

    own.wait()

    turn_of = lax.rem(group, per)

    def mid_copy(mem, slot, to):
        return remote(
            dealt.at[mem],
            cbuf.at[:, :, pl.ds(pl.multiple_of(cpad + slot * tile, tile), tile), :],
            mid_send.at[mem],
            mid_recv.at[slot],
            to,
        )

    def one_member(mem, slot):
        def side_of(f, s):
            return jnp.sum(jnp.where(lanes == 32 * f + s + 2 * mem, side[...], 0.0), axis=1, keepdims=True)

        sides = [[side_of(f, s) for s in range(2)] for f in range(2)]
        ends = [ghost[f, pl.ds(mem, 1), :] for f in range(3)]

        def ddx(x, f):
            left = jnp.where(at_west, sides[f][0], lane_roll(x, 1))
            right = jnp.where(at_east, sides[f][1], lane_roll(x, -1))
            return right - left

        def ddy(x):
            return row_roll(x, -1) - row_roll(x, 1)

        def bound(x, f):
            return jnp.where(is_ghost, ends[f], x)

        h, z, m = ext[mem, 0], bound(ext[mem, 1], 1), bound(ext[mem, 2], 2)
        for _ in range(NSTEPS):
            h = bound(h - half * (ddx(z, 1) + ddy(m)), 0)
            z, m = (
                bound(keep * z - half * ddx(h, 0) + rotation * m, 1),
                bound(keep * m - half * ddy(h) - rotation * z, 2),
            )
        lines = []
        for f, x in enumerate((h, z, m)):
            x = x[HALO : HALO + nrows]
            nest_out[mem, f] = x
            pieces = []
            for k in range(nwidth // LANES):
                thinned[slot, f, k] = x[:, k * LANES : (k + 1) * LANES]
                a, b, c = [thinned[slot, f, k, pl.ds(i, tile, stride=3), :] for i in range(3)]
                pieces.append(a + b + c)
            lines.append(jnp.concatenate(pieces, axis=-1))
        return lines

    def pair(i, _):
        group_of = [2 * i, 2 * i + 1]
        for mem in group_of:
            @pl.when(jnp.logical_not(first))
            def _():
                nest_down(mem, me).wait_recv()

            @pl.when(jnp.logical_not(last))
            def _():
                nest_up(mem, me).wait_recv()

        lines = [one_member(mem, slot) for slot, mem in enumerate(group_of)]
        means = exact_dot(jnp.concatenate(lines[0] + lines[1], axis=0), thin) * (1.0 / 9.0)
        for slot, mem in enumerate(group_of):
            for f in range(3):
                at = (3 * slot + f) * tile
                for k in range(span // LANES):
                    dealt[mem, k, f] = means[at : at + tile, k * LANES : (k + 1) * LANES]
            to = per * mem + turn_of

            @pl.when(to != me)
            def _():
                mid_copy(mem, me, to).start()

            @pl.when(to == me)
            def _():
                cbuf[:, :, pl.ds(pl.multiple_of(cpad + me * tile, tile), tile), :] = dealt[mem]

        return 0

    lax.fori_loop(0, members // 2, pair, 0)
    def form_edges(mem, _):
        edge_rows(mem, par_ref, edge_ref)
        return 0

    lax.fori_loop(0, members, form_edges, 0)
    is_mid = lax.rem(me, per) == turn_of
    mine = me // per

    def out_copy(to):
        return remote(sbuf.at[to], patch.at[mine], out_send.at[to], out_recv.at[mine], to)

    @pl.when(is_mid)
    def _():
        def recv(j, _):
            mid_copy(0, lax.rem(me + j, bands), me).wait_recv()
            return 0

        lax.fori_loop(1, bands, recv, 0)
        start_row = off_ref[0, mine]

        def deal(j, _):
            to = lax.rem(me + j, bands)
            begin = jnp.clip(to * prows - start_row, -cpad, bands * tile) + cpad
            for k in range(0, span, LANES):
                sbuf[to, :, :, pl.ds(k, LANES)] = cbuf[k // LANES, :, pl.ds(begin, prows), :]

            @pl.when(to != me)
            def _():
                out_copy(to).start()

            return 0

        lax.fori_loop(1, bands + 1, deal, 0)
        patch[mine] = sbuf[me]

    @pl.when(jnp.logical_not(first))
    def _():
        edge_up(me - 1).start()

    @pl.when(jnp.logical_not(last))
    def _():
        edge_down(me + 1).start()

    def out_stepped(mem):
        return pltpu.make_async_copy(par_ref.at[mem], stepped.at[mem], step_sem.at[mem])

    def step_parent(mem, _):
        inner_step(mem, par_ref, first, last)
        out_stepped(mem).start()
        return 0

    lax.fori_loop(0, members, step_parent, 0)

    def recv_patch(mem, _):
        out_stepped(mem).wait()


        @pl.when(per * mem + turn_of != me)
        def _():
            remote(sbuf.at[0], patch.at[mem], out_send.at[0], out_recv.at[mem], me).wait_recv()

        return 0

    lax.fori_loop(0, members, recv_patch, 0)

    @pl.when(jnp.logical_not(first))
    def _():
        edge_down(me).wait_recv()
        edge_up(me).wait_send()

    @pl.when(jnp.logical_not(last))
    def _():
        edge_up(me).wait_recv()
        edge_down(me).wait_send()

    @pl.when(sends_top)
    def _():
        end_copy(0, me, 0).wait_send()

    @pl.when(sends_bottom)
    def _():
        end_copy(1, bands - 1 - me, bands - 1).wait_send()

    def sent_strip(j, _):
        strip_copy(me, lax.rem(me + j, bands), j).wait_send()
        return 0

    lax.fori_loop(1, bands, sent_strip, 0)

    def sent_mid(mem, _):
        @pl.when(jnp.logical_not(first))
        def _():
            nest_up(mem, me).wait_send()

        @pl.when(jnp.logical_not(last))
        def _():
            nest_down(mem, me).wait_send()

        @pl.when(per * mem + turn_of != me)
        def _():
            mid_copy(mem, me, me).wait_send()

        return 0

    lax.fori_loop(0, members, sent_mid, 0)

    @pl.when(is_mid)
    def _():
        def sent_out(j, _):
            out_copy(lax.rem(me + j, bands)).wait_send()
            return 0

        lax.fori_loop(1, bands, sent_out, 0)


def parent_kernel(span, bands, off_ref, band_ref, par_ref, halo_ref, patch_ref, nest_ref, out_ref, nest_out):
    nest_out[...] = nest_ref[...]
    mem = pl.program_id(0)
    rows = par_ref.shape[2]
    row0, col0 = off_ref[0, mem], off_ref[1, mem]
    band = band_ref[0]
    out_ref[...] = par_ref[...]

    def add(first_row, second_row, sign, halo):
        m, p = half * halo[0:1], half * halo[1:2]
        out_ref[0, 0, first_row : first_row + 1, :] += sign * m
        out_ref[0, 1, first_row : first_row + 1, :] -= sign * half * (lane_roll(m, -1) - lane_roll(m, 1))
        out_ref[0, 2, first_row : first_row + 1, :] += sign * p
        out_ref[0, 2, second_row : second_row + 1, :] += half * m

    @pl.when(band > 0)
    def _():
        add(0, 1, 1.0, halo_ref[0, 0])

    @pl.when(band < bands - 1)
    def _():
        add(rows - 1, rows - 2, -1.0, halo_ref[1, 0])

    block0 = col0 // LANES
    shift = col0 - block0 * LANES
    place = pl.ds(pl.multiple_of(block0 * LANES, LANES), span + LANES)
    wide = jnp.concatenate([patch_ref[0], jnp.zeros((3, rows, LANES), jnp.float32)], axis=-1)
    wide = pltpu.roll(wide.reshape(3 * rows, span + LANES), shift, 1).reshape(3, rows, span + LANES)
    lane = iota(wide.shape, 2)
    at = iota(wide.shape, 1) + (band * rows - row0)
    inside = (lane >= shift) & (lane < shift + span) & (at >= 0) & (at < span)
    out_ref[0, :, :, place] = jnp.where(inside, wide, out_ref[0, :, :, place])


def per_device(bands, parent_state, nest_state, offsets):
    members, _, prows, width = parent_state.shape
    nrows, nwidth = nest_state.shape[2:]
    span = nwidth // 3
    tile = nrows // 3
    f32 = jnp.float32
    band = lax.axis_index("band").reshape(1).astype(jnp.int32)
    offsets = offsets.T
    shape = jax.ShapeDtypeStruct
    limit = 60 * 1024 * 1024
    parent_spec = pl.BlockSpec((1, 3, prows, width), lambda i, *_: (i, 0, 0, 0))
    edge_spec = pl.BlockSpec((2, 1, 2, width), lambda i, *_: (0, i, 0, 0))

    vmem = pl.BlockSpec(memory_space=pltpu.VMEM)
    hbm = pl.BlockSpec(memory_space=pl.ANY)
    dma = pltpu.SemaphoreType.DMA
    senders = bands // 2 + 1
    nest_out, patch, halo, stepped = pl.pallas_call(
        functools.partial(nest_kernel, bands, span),
        out_shape=(
            shape(nest_state.shape, f32),
            shape((members, 3, prows, span), f32),
            shape((2, members, 2, width), f32),
            shape(parent_state.shape, f32),
        ),
        in_specs=[pl.BlockSpec(memory_space=pltpu.SMEM), hbm, hbm],
        out_specs=(vmem, vmem, hbm, hbm),
        scratch_shapes=[
            pltpu.VMEM((members, 3, prows, width), f32),
            pltpu.VMEM((2, members, 2, width), f32),
            pltpu.VMEM((prows, LANES), f32),
            pltpu.VMEM((2, 3, members, span + LANES), f32),
            pltpu.VMEM((members, 3, nrows + 2 * HALO, nwidth), f32),
            pltpu.VMEM(((bands + 2) * prows, LANES), f32),
            pltpu.VMEM((senders, 3, members, span + LANES), f32),
            pltpu.VMEM(((bands + 2) * prows, LANES), f32),
            pltpu.VMEM((nrows + 2 * HALO, LANES), f32),
            pltpu.VMEM((3, members, nwidth), f32),
            pltpu.VMEM((3, members, span + LANES), f32),
            pltpu.VMEM((span + LANES, nwidth), jnp.bfloat16),
            pltpu.VMEM((2, 3, nwidth // LANES, nrows, LANES), f32),
            pltpu.VMEM((members, span // LANES, 3, tile, LANES), f32),
            pltpu.VMEM((span // LANES, 3, bands * tile + 2 * prows, LANES), f32),
            pltpu.VMEM((bands, 3, prows, span), f32),
            dma((2, members)),
            dma((2, members)),
            dma((2,)),
            dma((2,)),
            dma((bands,)),
            dma((bands,)),
            dma((2,)),
            dma((senders,)),
            dma((members,)),
            dma((bands,)),
            dma((bands,)),
            dma((members,)),
            dma,
            dma,
            dma((members,)),
        ],
        compiler_params=pltpu.CompilerParams(collective_id=0, has_side_effects=True, vmem_limit_bytes=limit),
        name="nest",
    )(offsets, nest_state, parent_state)

    nest_spec = pl.BlockSpec((1, 3, nrows, nwidth), lambda i, *_: (i, 0, 0, 0))
    return pl.pallas_call(
        functools.partial(parent_kernel, span, bands),
        out_shape=(shape(parent_state.shape, f32), shape(nest_state.shape, f32)),
        grid_spec=pltpu.PrefetchScalarGridSpec(
            num_scalar_prefetch=2,
            grid=(members,),
            in_specs=[
                parent_spec,
                edge_spec,
                pl.BlockSpec((1, 3, prows, span), lambda i, *_: (i, 0, 0, 0)),
                nest_spec,
            ],
            out_specs=(parent_spec, nest_spec),
        ),
        compiler_params=pltpu.CompilerParams(vmem_limit_bytes=limit),
        name="parent",
    )(offsets, band, stepped, halo, patch, nest_out)


def solution(mesh):
    in_specs = (P("member", None, "band", None), P("member", None, "band", None), P("member", None))
    out_specs = (P("member", None, "band", None), P("member", None, "band", None))
    return jax.shard_map(
        functools.partial(per_device, mesh.shape["band"]),
        mesh=mesh,
        in_specs=in_specs,
        out_specs=out_specs,
        check_vma=False,
    )
```

```python
import functools

import jax
import jax.numpy as jnp
from jax import lax
from jax.experimental import pallas as pl
from jax.experimental.pallas import tpu as pltpu
from jax.sharding import PartitionSpec as P

NSTEPS = 3
MESH = pl.DeviceIdType.MESH

courant = 0.9
friction = 0.02
rotation = 0.05
half = 0.5 * courant
keep = 1.0 - friction
highest = lax.Precision.HIGHEST
LANES = 128
HALO = 8


def lane_roll(x, shift):
    size = x.shape[-1]
    return pltpu.roll(x, shift % size, x.ndim - 1)


def row_roll(x, shift):
    size = x.shape[-2]
    return pltpu.roll(x, shift % size, x.ndim - 2)


def dx(x):
    return 0.5 * (lane_roll(x, -1) - lane_roll(x, 1))


def iota(shape, dim):
    return lax.broadcasted_iota(jnp.int32, shape, dim)


def split(x):
    high = x.astype(jnp.bfloat16)
    rest = x - high.astype(jnp.float32)
    mid = rest.astype(jnp.bfloat16)
    return high, mid, (rest - mid.astype(jnp.float32)).astype(jnp.bfloat16)


def exact_dot(x, weights):
    count = x.shape[0]
    parts = jnp.concatenate([part.astype(jnp.float32) for part in split(x)], axis=0).astype(jnp.bfloat16)
    out = jnp.dot(parts, weights, preferred_element_type=jnp.float32)
    return out[:count] + out[count : 2 * count] + out[2 * count :]


def edge_rows(mem, par_ref, edge_ref):
    rows = par_ref.shape[2]
    z_top, z_bot = par_ref[mem, 1, 0:1, :], par_ref[mem, 1, rows - 1 : rows, :]
    m_top, m_bot = par_ref[mem, 2, 0:1, :], par_ref[mem, 2, rows - 1 : rows, :]
    edge_ref[0, mem, 0:1, :] = m_top
    edge_ref[0, mem, 1:2, :] = par_ref[mem, 0, 0:1, :] - courant * dx(z_top) - half * par_ref[mem, 2, 1:2, :]
    edge_ref[1, mem, 0:1, :] = m_bot
    edge_ref[1, mem, 1:2, :] = (
        par_ref[mem, 0, rows - 1 : rows, :] - courant * dx(z_bot) + half * par_ref[mem, 2, rows - 2 : rows - 1, :]
    )


def window_shares(mem, span, row0, col0, band, par_ref, ends_ref):
    rows, width = par_ref.shape[2], par_ref.shape[3]
    blocks = width // LANES
    count = span // LANES + 2
    first = lax.rem(col0 - 4 + width, width)
    block0 = lax.div(first, LANES)
    shift = first - block0 * LANES
    wanted = [jnp.zeros((rows, LANES), jnp.int32) + lax.rem(block0 + k, blocks) for k in range(count)]
    parts = [jnp.zeros((3, rows, LANES), jnp.float32)] * count
    for place in range(blocks):
        block = par_ref[mem, :, :, place * LANES : (place + 1) * LANES]
        parts = [jnp.where((w == place)[None], block, part) for w, part in zip(wanted, parts)]
    wide = jnp.concatenate(parts, axis=-1).reshape(3 * rows, count * LANES)
    amount = jnp.zeros(wide.shape, jnp.int32) + shift
    for bit in (64, 32, 16, 8, 4, 2, 1):
        wide = jnp.where((amount & bit) != 0, lane_roll(wide, -bit), wide)
    wide = wide[:, : span + LANES].reshape(3, rows, span + LANES)
    h, z, m = wide[0], wide[1], wide[2]
    a = h - courant * dx(z)
    b = keep * z - courant * dx(a) + rotation * m
    cc = keep * m - rotation * z
    shape = h.shape
    lane = iota(shape, 1)
    west = jnp.where(lane == 3, 2.0 / 3.0, 0.0) + jnp.where(lane == 4, 1.0 / 3.0, 0.0)
    east = jnp.where(lane == span + 3, 1.0 / 3.0, 0.0) + jnp.where(lane == span + 4, 2.0 / 3.0, 0.0)
    slot = iota((rows, LANES), 1)
    total = jnp.zeros((rows, LANES), jnp.float32)
    for q, field in enumerate((a, m, b, dx(m), cc)):
        for s, weight in enumerate((west, east)):
            value = jnp.sum(field * weight, axis=1, keepdims=True)
            total = total + jnp.where(slot == q * 16 + s + 2 * mem, value, 0.0)

    row = iota(shape, 0) + band * rows
    for end in range(2):
        near = row0 - 1 if end == 0 else row0 + span - 1
        lo, hi = (2.0 / 3.0, 1.0 / 3.0) if end == 0 else (1.0 / 3.0, 2.0 / 3.0)

        def w(i):
            return jnp.where(i == near, lo, 0.0) + jnp.where(i == near + 1, hi, 0.0)

        def u(i):
            return -half * (w(i - 1) - w(i + 1))

        wr, ur = w(row), u(row)
        vr = -half * (u(row - 1) - u(row + 1))
        h1 = jnp.sum(wr * a + ur * m, axis=0, keepdims=True)
        z1 = jnp.sum(wr * (keep * z + rotation * m), axis=0, keepdims=True) - courant * dx(h1)
        m1 = jnp.sum(wr * cc + ur * a + vr * m, axis=0, keepdims=True)
        for f, value in enumerate((h1, z1, m1)):
            ends_ref[end, f, pl.ds(mem, 1), :] = value
    return total


def inner_step(mem, ref, first, last):
    rows = ref.shape[2]
    h, z, m = ref[mem, 0], ref[mem, 1], ref[mem, 2]
    row = iota(h.shape, 0)
    h_above = jnp.where(first, 0.0, -half * m[0:1])
    h_below = jnp.where(last, 0.0, half * m[rows - 1 : rows])

    def ddy(x, above, below):
        up = jnp.where(row == 0, above, row_roll(x, 1))
        down = jnp.where(row == rows - 1, below, row_roll(x, -1))
        return down - up

    h1 = h - half * (lane_roll(z, -1) - lane_roll(z, 1) + ddy(m, 0.0, 0.0))
    ref[mem, 0] = h1
    ref[mem, 1] = keep * z - half * (lane_roll(h1, -1) - lane_roll(h1, 1)) + rotation * m
    ref[mem, 2] = keep * m - half * ddy(h1, h_above, h_below) - rotation * z


def nest_kernel(
    bands,
    span,
    off_ref,
    nest_ref,
    parent_ref,
    nest_out,
    patch,
    halo,
    stepped,
    par_ref,
    edge_ref,
    strip_ref,
    ends_ref,
    ext,
    strips,
    endbuf,
    cols,
    side,
    ghost,
    acc,
    fine,
    thinned,
    dealt,
    cbuf,
    sbuf,
    nest_send,
    nest_recv,
    edge_send,
    edge_recv,
    strip_send,
    strip_recv,
    end_send,
    end_recv,
    mid_send,
    mid_recv,
    out_send,
    out_recv,
    local_sem,
    parent_sem,
    step_sem,
):
    me = lax.axis_index("band")
    group = lax.axis_index("member")
    members, _, nrows, nwidth = nest_ref.shape
    prows = strip_ref.shape[0]
    tile = nrows // 3
    per = bands // members
    top_senders = bands // 2 + 1

    def remote(src, dst, send, recv, to):
        return pltpu.make_async_remote_copy(
            src_ref=src, dst_ref=dst, send_sem=send, recv_sem=recv, device_id=(group, to), device_id_type=MESH
        )

    barrier = pltpu.get_barrier_semaphore()

    def greet(j, _):
        pl.semaphore_signal(barrier, inc=1, device_id=(group, lax.rem(me + j, bands)), device_id_type=MESH)
        return 0

    lax.fori_loop(1, bands, greet, 0)
    own = pltpu.make_async_copy(nest_ref, ext.at[:, :, pl.ds(HALO, nrows), :], local_sem)

    def load(mem):
        return pltpu.make_async_copy(parent_ref.at[mem], par_ref.at[mem], parent_sem.at[mem])

    for mem in range(members):
        load(mem).start()
    own.start()
    pl.semaphore_wait(barrier, bands - 1)

    reach = 2 * NSTEPS

    def nest_down(mem, to):
        return remote(
            nest_ref.at[mem, :, pl.ds(nrows - reach, reach), :],
            ext.at[mem, :, pl.ds(HALO - reach, reach), :],
            nest_send.at[0, mem],
            nest_recv.at[0, mem],
            to,
        )

    def nest_up(mem, to):
        return remote(
            nest_ref.at[mem, :, pl.ds(0, reach), :],
            ext.at[mem, :, pl.ds(HALO + nrows, reach), :],
            nest_send.at[1, mem],
            nest_recv.at[1, mem],
            to,
        )

    def edge_down(to):
        return remote(edge_ref.at[1], halo.at[0], edge_send.at[0], edge_recv.at[0], to)

    def edge_up(to):
        return remote(edge_ref.at[0], halo.at[1], edge_send.at[1], edge_recv.at[1], to)

    def strip_copy(slot, to, index):
        return remote(strip_ref, strips.at[pl.ds(pl.multiple_of((slot + 1) * prows, prows), prows), :], strip_send.at[index], strip_recv.at[slot], to)

    def end_copy(end, slot, to):
        return remote(ends_ref.at[end], endbuf.at[slot], end_send.at[end], end_recv.at[slot], to)

    first, last = me == 0, me == bands - 1

    def gather(mem, _):
        load(mem).wait()

        @pl.when(jnp.logical_not(first))
        def _():
            nest_up(mem, me - 1).start()

        @pl.when(jnp.logical_not(last))
        def _():
            nest_down(mem, me + 1).start()

        strip_ref[...] += window_shares(mem, span, off_ref[0, mem], off_ref[1, mem], me, par_ref, ends_ref)
        return 0

    strip_ref[...] = jnp.zeros_like(strip_ref)
    lax.fori_loop(0, members, gather, 0)

    def send_strip(j, _):
        strip_copy(me, lax.rem(me + j, bands), j).start()
        return 0

    lax.fori_loop(1, bands, send_strip, 0)

    sends_top = jnp.logical_and(me > 0, me < top_senders)
    sends_bottom = jnp.logical_and(me < bands - 1, me >= bands - top_senders)

    @pl.when(sends_top)
    def _():
        end_copy(0, me, 0).start()

    @pl.when(sends_bottom)
    def _():
        end_copy(1, bands - 1 - me, bands - 1).start()

    pad = strips.shape[0] - (bands + 1) * prows
    strips[pl.ds(0, prows), :] = jnp.zeros((prows, LANES), jnp.float32)
    strips[pl.ds((bands + 1) * prows, pad), :] = jnp.zeros((pad, LANES), jnp.float32)
    strips[pl.ds(pl.multiple_of((me + 1) * prows, prows), prows), :] = strip_ref[...]
    cpad = (cbuf.shape[2] - bands * tile) // 2
    blank = jnp.zeros((span // LANES, 3, cpad, LANES), jnp.float32)
    cbuf[:, :, pl.ds(0, cpad), :] = blank
    cbuf[:, :, pl.ds(cpad + bands * tile, cpad), :] = blank

    ends_lane = span + LANES

    @pl.when(jnp.logical_or(first, last))
    def _():
        j = iota((1, nwidth), 1) + 2
        q, t = j // 3, j % 3
        k = iota((ends_lane, nwidth), 0) - 3
        fine[...] = (jnp.where(k == q, 3 - t, 0) + jnp.where(k == q + 1, t, 0)).astype(jnp.float32).astype(jnp.bfloat16)

    erows = nrows + 2 * HALO
    e = iota((erows, prows), 0)
    q, t = e // 3, e % 3
    k = iota((erows, prows), 1)
    weights = jnp.where(k == q, (3 - t).astype(jnp.float32) / 3.0, 0.0) + jnp.where(
        k == q + 1, t.astype(jnp.float32) / 3.0, 0.0
    )
    thin = jnp.where(iota((nwidth, span), 0) // 3 == iota((nwidth, span), 1), 1.0, 0.0).astype(jnp.bfloat16)
    row = iota((erows, nwidth), 0)
    col = iota((erows, nwidth), 1)
    is_ghost = jnp.logical_or(
        jnp.logical_and(row == HALO - 1, first), jnp.logical_and(row == HALO + nrows, last)
    )
    at_west, at_east = col == 0, col == nwidth - 1
    lanes = iota((erows, LANES), 1)

    def recv_strip(j, _):
        strip_copy(lax.rem(me + j, bands), me, j).wait_recv()
        return 0

    lax.fori_loop(1, bands, recv_strip, 0)

    g = strips[...]
    lane = iota((1, LANES), 1)
    turn = lane_roll(g, -16)
    height = g + jnp.where(lane < 16, -half, courant * half) * (row_roll(turn, -1) - row_roll(turn, 1))
    turn = lane_roll(height, 64)
    cols[...] = jnp.where(lane < 64, height, g - half * (row_roll(turn, -1) - row_roll(turn, 1)))
    picked = jnp.zeros((prows, LANES), jnp.float32)
    for mem in range(members):
        begin = off_ref[0, mem] + (me * tile - 3 + prows)
        picked = jnp.where(lane % 32 // 2 == mem, cols[pl.ds(begin, prows), :], picked)
    side[...] = jnp.dot(weights, picked, precision=highest, preferred_element_type=jnp.float32)


    def add_end(k, _):
        @pl.when(k > 0)
        def _():
            end_copy(0, k, 0).wait_recv()

        acc[...] += endbuf[k]
        return 0

    @pl.when(first)
    def _():
        endbuf[0] = ends_ref[0]

    @pl.when(last)
    def _():
        endbuf[0] = ends_ref[1]

    @pl.when(jnp.logical_or(first, last))
    def _():
        acc[...] = jnp.zeros_like(acc)
        lax.fori_loop(0, top_senders, add_end, 0)
        rows_in = acc[...].reshape(3 * members, ends_lane)
        ghost[...] = (exact_dot(rows_in, fine[...]) * (1.0 / 3.0)).reshape(3, members, nwidth)

    own.wait()

    turn_of = lax.rem(group, per)

    def mid_copy(mem, slot, to):
        return remote(
            dealt.at[mem],
            cbuf.at[:, :, pl.ds(pl.multiple_of(cpad + slot * tile, tile), tile), :],
            mid_send.at[mem],
            mid_recv.at[slot],
            to,
        )

    def one_member(mem, slot):
        def side_of(f, s):
            return jnp.sum(jnp.where(lanes == 32 * f + s + 2 * mem, side[...], 0.0), axis=1, keepdims=True)

        sides = [[side_of(f, s) for s in range(2)] for f in range(2)]
        ends = [ghost[f, pl.ds(mem, 1), :] for f in range(3)]

        def ddx(x, f):
            left = jnp.where(at_west, sides[f][0], lane_roll(x, 1))
            right = jnp.where(at_east, sides[f][1], lane_roll(x, -1))
            return right - left

        def ddy(x):
            return row_roll(x, -1) - row_roll(x, 1)

        def bound(x, f):
            return jnp.where(is_ghost, ends[f], x)

        h, z, m = ext[mem, 0], bound(ext[mem, 1], 1), bound(ext[mem, 2], 2)
        for _ in range(NSTEPS):
            h = bound(h - half * (ddx(z, 1) + ddy(m)), 0)
            z, m = (
                bound(keep * z - half * ddx(h, 0) + rotation * m, 1),
                bound(keep * m - half * ddy(h) - rotation * z, 2),
            )
        lines = []
        for f, x in enumerate((h, z, m)):
            x = x[HALO : HALO + nrows]
            nest_out[mem, f] = x
            pieces = []
            for k in range(nwidth // LANES):
                thinned[slot, f, k] = x[:, k * LANES : (k + 1) * LANES]
                a, b, c = [thinned[slot, f, k, pl.ds(i, tile, stride=3), :] for i in range(3)]
                pieces.append(a + b + c)
            lines.append(jnp.concatenate(pieces, axis=-1))
        return lines

    def pair(i, _):
        group_of = [2 * i, 2 * i + 1]
        for mem in group_of:
            @pl.when(jnp.logical_not(first))
            def _():
                nest_down(mem, me).wait_recv()

            @pl.when(jnp.logical_not(last))
            def _():
                nest_up(mem, me).wait_recv()

        lines = [one_member(mem, slot) for slot, mem in enumerate(group_of)]
        means = exact_dot(jnp.concatenate(lines[0] + lines[1], axis=0), thin) * (1.0 / 9.0)
        for slot, mem in enumerate(group_of):
            for f in range(3):
                at = (3 * slot + f) * tile
                for k in range(span // LANES):
                    dealt[mem, k, f] = means[at : at + tile, k * LANES : (k + 1) * LANES]
            to = per * mem + turn_of

            @pl.when(to != me)
            def _():
                mid_copy(mem, me, to).start()

            @pl.when(to == me)
            def _():
                cbuf[:, :, pl.ds(pl.multiple_of(cpad + me * tile, tile), tile), :] = dealt[mem]

        return 0

    lax.fori_loop(0, members // 2, pair, 0)
    def form_edges(mem, _):
        edge_rows(mem, par_ref, edge_ref)
        return 0

    lax.fori_loop(0, members, form_edges, 0)
    is_mid = lax.rem(me, per) == turn_of
    mine = me // per

    def out_copy(to):
        return remote(sbuf.at[to], patch.at[mine], out_send.at[to], out_recv.at[mine], to)

    @pl.when(is_mid)
    def _():
        def recv(j, _):
            mid_copy(0, lax.rem(me + j, bands), me).wait_recv()
            return 0

        lax.fori_loop(1, bands, recv, 0)
        start_row = off_ref[0, mine]

        def deal(j, _):
            to = lax.rem(me + j, bands)
            begin = jnp.clip(to * prows - start_row, -cpad, bands * tile) + cpad
            for k in range(0, span, LANES):
                sbuf[to, :, :, pl.ds(k, LANES)] = cbuf[k // LANES, :, pl.ds(begin, prows), :]

            @pl.when(to != me)
            def _():
                out_copy(to).start()

            return 0

        lax.fori_loop(1, bands + 1, deal, 0)
        patch[mine] = sbuf[me]

    @pl.when(jnp.logical_not(first))
    def _():
        edge_up(me - 1).start()

    @pl.when(jnp.logical_not(last))
    def _():
        edge_down(me + 1).start()

    def out_stepped(mem):
        return pltpu.make_async_copy(par_ref.at[mem], stepped.at[mem], step_sem.at[mem])

    def step_parent(mem, _):
        inner_step(mem, par_ref, first, last)
        out_stepped(mem).start()
        return 0

    lax.fori_loop(0, members, step_parent, 0)

    def recv_patch(mem, _):
        out_stepped(mem).wait()


        @pl.when(per * mem + turn_of != me)
        def _():
            remote(sbuf.at[0], patch.at[mem], out_send.at[0], out_recv.at[mem], me).wait_recv()

        return 0

    lax.fori_loop(0, members, recv_patch, 0)

    @pl.when(jnp.logical_not(first))
    def _():
        edge_down(me).wait_recv()
        edge_up(me).wait_send()

    @pl.when(jnp.logical_not(last))
    def _():
        edge_up(me).wait_recv()
        edge_down(me).wait_send()

    @pl.when(sends_top)
    def _():
        end_copy(0, me, 0).wait_send()

    @pl.when(sends_bottom)
    def _():
        end_copy(1, bands - 1 - me, bands - 1).wait_send()

    def sent_strip(j, _):
        strip_copy(me, lax.rem(me + j, bands), j).wait_send()
        return 0

    lax.fori_loop(1, bands, sent_strip, 0)

    def sent_mid(mem, _):
        @pl.when(jnp.logical_not(first))
        def _():
            nest_up(mem, me).wait_send()

        @pl.when(jnp.logical_not(last))
        def _():
            nest_down(mem, me).wait_send()

        @pl.when(per * mem + turn_of != me)
        def _():
            mid_copy(mem, me, me).wait_send()

        return 0

    lax.fori_loop(0, members, sent_mid, 0)

    @pl.when(is_mid)
    def _():
        def sent_out(j, _):
            out_copy(lax.rem(me + j, bands)).wait_send()
            return 0

        lax.fori_loop(1, bands, sent_out, 0)


def finish(mem, span, bands, off_ref, band_ref, halo_ref, patch_ref, out_ref):
    rows = out_ref.shape[2]
    row0, col0 = off_ref[0, mem], off_ref[1, mem]
    band = band_ref[0]

    def add(first_row, second_row, sign, halo):
        m, p = half * halo[0:1], half * halo[1:2]
        out_ref[mem, 0, first_row : first_row + 1, :] += sign * m
        out_ref[mem, 1, first_row : first_row + 1, :] -= sign * half * (lane_roll(m, -1) - lane_roll(m, 1))
        out_ref[mem, 2, first_row : first_row + 1, :] += sign * p
        out_ref[mem, 2, second_row : second_row + 1, :] += half * m

    @pl.when(band > 0)
    def _():
        add(0, 1, 1.0, halo_ref[0, mem])

    @pl.when(band < bands - 1)
    def _():
        add(rows - 1, rows - 2, -1.0, halo_ref[1, mem])

    block0 = col0 // LANES
    shift = col0 - block0 * LANES
    place = pl.ds(pl.multiple_of(block0 * LANES, LANES), span + LANES)
    wide = jnp.concatenate([patch_ref[mem], jnp.zeros((3, rows, LANES), jnp.float32)], axis=-1)
    wide = pltpu.roll(wide.reshape(3 * rows, span + LANES), shift, 1).reshape(3, rows, span + LANES)
    lane = iota(wide.shape, 2)
    at = iota(wide.shape, 1) + (band * rows - row0)
    inside = (lane >= shift) & (lane < shift + span) & (at >= 0) & (at < span)
    out_ref[mem, :, :, place] = jnp.where(inside, wide, out_ref[mem, :, :, place])


def parent_kernel(
    span,
    bands,
    off_ref,
    band_ref,
    par_ref,
    halo_ref,
    patch_ref,
    nest_ref,
    out_ref,
    nest_out,
    work,
    halos,
    nests,
    in_sem,
    out_sem,
    halo_sem,
    nest_in,
    nest_back,
):
    members = work.shape[0]

    def move_halo(mem):
        return pltpu.make_async_copy(halo_ref.at[:, mem], halos.at[:, mem], halo_sem.at[mem])

    def move_in(mem):
        return pltpu.make_async_copy(par_ref.at[mem], work.at[mem], in_sem.at[mem])

    def move_out(mem):
        return pltpu.make_async_copy(work.at[mem], out_ref.at[mem], out_sem.at[mem])

    def nest_to(mem):
        return pltpu.make_async_copy(nest_ref.at[mem], nests.at[mem], nest_in.at[mem])

    def nest_from(mem):
        return pltpu.make_async_copy(nests.at[mem], nest_out.at[mem], nest_back.at[mem])

    for mem in range(members):
        move_halo(mem).start()
        move_in(mem).start()
        nest_to(mem).start()

    def one_member(mem, _):
        move_halo(mem).wait()
        move_in(mem).wait()
        finish(mem, span, bands, off_ref, band_ref, halos, patch_ref, work)
        move_out(mem).start()
        nest_to(mem).wait()
        nest_from(mem).start()
        return 0

    lax.fori_loop(0, members, one_member, 0)

    def last_wait(mem, _):
        move_out(mem).wait()
        nest_from(mem).wait()
        return 0

    lax.fori_loop(0, members, last_wait, 0)


def per_device(bands, parent_state, nest_state, offsets):
    members, _, prows, width = parent_state.shape
    nrows, nwidth = nest_state.shape[2:]
    span = nwidth // 3
    tile = nrows // 3
    f32 = jnp.float32
    band = lax.axis_index("band").reshape(1).astype(jnp.int32)
    offsets = offsets.T
    shape = jax.ShapeDtypeStruct
    limit = 60 * 1024 * 1024
    vmem = pl.BlockSpec(memory_space=pltpu.VMEM)
    hbm = pl.BlockSpec(memory_space=pl.ANY)
    dma = pltpu.SemaphoreType.DMA
    senders = bands // 2 + 1
    nest_out, patch, halo, stepped = pl.pallas_call(
        functools.partial(nest_kernel, bands, span),
        out_shape=(
            shape(nest_state.shape, f32),
            shape((members, 3, prows, span), f32),
            shape((2, members, 2, width), f32),
            shape(parent_state.shape, f32),
        ),
        in_specs=[pl.BlockSpec(memory_space=pltpu.SMEM), hbm, hbm],
        out_specs=(vmem, vmem, hbm, hbm),
        scratch_shapes=[
            pltpu.VMEM((members, 3, prows, width), f32),
            pltpu.VMEM((2, members, 2, width), f32),
            pltpu.VMEM((prows, LANES), f32),
            pltpu.VMEM((2, 3, members, span + LANES), f32),
            pltpu.VMEM((members, 3, nrows + 2 * HALO, nwidth), f32),
            pltpu.VMEM(((bands + 2) * prows, LANES), f32),
            pltpu.VMEM((senders, 3, members, span + LANES), f32),
            pltpu.VMEM(((bands + 2) * prows, LANES), f32),
            pltpu.VMEM((nrows + 2 * HALO, LANES), f32),
            pltpu.VMEM((3, members, nwidth), f32),
            pltpu.VMEM((3, members, span + LANES), f32),
            pltpu.VMEM((span + LANES, nwidth), jnp.bfloat16),
            pltpu.VMEM((2, 3, nwidth // LANES, nrows, LANES), f32),
            pltpu.VMEM((members, span // LANES, 3, tile, LANES), f32),
            pltpu.VMEM((span // LANES, 3, bands * tile + 2 * prows, LANES), f32),
            pltpu.VMEM((bands, 3, prows, span), f32),
            dma((2, members)),
            dma((2, members)),
            dma((2,)),
            dma((2,)),
            dma((bands,)),
            dma((bands,)),
            dma((2,)),
            dma((senders,)),
            dma((members,)),
            dma((bands,)),
            dma((bands,)),
            dma((members,)),
            dma,
            dma((members,)),
            dma((members,)),
        ],
        compiler_params=pltpu.CompilerParams(collective_id=0, has_side_effects=True, vmem_limit_bytes=limit),
        name="nest",
    )(offsets, nest_state, parent_state)

    smem = pl.BlockSpec(memory_space=pltpu.SMEM)
    return pl.pallas_call(
        functools.partial(parent_kernel, span, bands),
        out_shape=(shape(parent_state.shape, f32), shape(nest_state.shape, f32)),
        in_specs=[smem, smem, hbm, hbm, vmem, hbm],
        out_specs=(hbm, hbm),
        scratch_shapes=[
            pltpu.VMEM((members, 3, prows, width), f32),
            pltpu.VMEM((2, members, 2, width), f32),
            pltpu.VMEM((members, 3, nrows, nwidth), f32),
            dma((members,)),
            dma((members,)),
            dma((members,)),
            dma((members,)),
            dma((members,)),
        ],
        compiler_params=pltpu.CompilerParams(vmem_limit_bytes=limit),
        name="parent",
    )(offsets, band, stepped, halo, patch, nest_out)


def solution(mesh):
    in_specs = (P("member", None, "band", None), P("member", None, "band", None), P("member", None))
    out_specs = (P("member", None, "band", None), P("member", None, "band", None))
    return jax.shard_map(
        functools.partial(per_device, mesh.shape["band"]),
        mesh=mesh,
        in_specs=in_specs,
        out_specs=out_specs,
        check_vma=False,
    )
```

```python
import functools

import jax
import jax.numpy as jnp
from jax import lax
from jax.experimental import pallas as pl
from jax.experimental.pallas import tpu as pltpu
from jax.sharding import PartitionSpec as P

NSTEPS = 3
MESH = pl.DeviceIdType.MESH

courant = 0.9
friction = 0.02
rotation = 0.05
half = 0.5 * courant
keep = 1.0 - friction
highest = lax.Precision.HIGHEST
LANES = 128
HALO = 8


def lane_roll(x, shift):
    size = x.shape[-1]
    return pltpu.roll(x, shift % size, x.ndim - 1)


def row_roll(x, shift):
    size = x.shape[-2]
    return pltpu.roll(x, shift % size, x.ndim - 2)


def dx(x):
    return 0.5 * (lane_roll(x, -1) - lane_roll(x, 1))


def iota(shape, dim):
    return lax.broadcasted_iota(jnp.int32, shape, dim)


def split(x):
    high = x.astype(jnp.bfloat16)
    rest = x - high.astype(jnp.float32)
    mid = rest.astype(jnp.bfloat16)
    return high, mid, (rest - mid.astype(jnp.float32)).astype(jnp.bfloat16)


def exact_dot(x, weights):
    count = x.shape[0]
    parts = jnp.concatenate([part.astype(jnp.float32) for part in split(x)], axis=0).astype(jnp.bfloat16)
    out = jnp.dot(parts, weights, preferred_element_type=jnp.float32)
    return out[:count] + out[count : 2 * count] + out[2 * count :]


def edge_rows(mem, par_ref, edge_ref):
    rows = par_ref.shape[2]
    z_top, z_bot = par_ref[mem, 1, 0:1, :], par_ref[mem, 1, rows - 1 : rows, :]
    m_top, m_bot = par_ref[mem, 2, 0:1, :], par_ref[mem, 2, rows - 1 : rows, :]
    edge_ref[0, mem, 0:1, :] = m_top
    edge_ref[0, mem, 1:2, :] = par_ref[mem, 0, 0:1, :] - courant * dx(z_top) - half * par_ref[mem, 2, 1:2, :]
    edge_ref[1, mem, 0:1, :] = m_bot
    edge_ref[1, mem, 1:2, :] = (
        par_ref[mem, 0, rows - 1 : rows, :] - courant * dx(z_bot) + half * par_ref[mem, 2, rows - 2 : rows - 1, :]
    )


def window_shares(mem, span, row0, col0, band, par_ref, ends_ref):
    rows, width = par_ref.shape[2], par_ref.shape[3]
    blocks = width // LANES
    count = span // LANES + 2
    first = lax.rem(col0 - 4 + width, width)
    block0 = lax.div(first, LANES)
    shift = first - block0 * LANES
    wanted = [jnp.zeros((rows, LANES), jnp.int32) + lax.rem(block0 + k, blocks) for k in range(count)]
    parts = [jnp.zeros((3, rows, LANES), jnp.float32)] * count
    for place in range(blocks):
        block = par_ref[mem, :, :, place * LANES : (place + 1) * LANES]
        parts = [jnp.where((w == place)[None], block, part) for w, part in zip(wanted, parts)]
    wide = jnp.concatenate(parts, axis=-1).reshape(3 * rows, count * LANES)
    amount = jnp.zeros(wide.shape, jnp.int32) + shift
    for bit in (64, 32, 16, 8, 4, 2, 1):
        wide = jnp.where((amount & bit) != 0, lane_roll(wide, -bit), wide)
    wide = wide[:, : span + LANES].reshape(3, rows, span + LANES)
    h, z, m = wide[0], wide[1], wide[2]
    a = h - courant * dx(z)
    b = keep * z - courant * dx(a) + rotation * m
    cc = keep * m - rotation * z
    shape = h.shape
    lane = iota(shape, 1)
    west = jnp.where(lane == 3, 2.0 / 3.0, 0.0) + jnp.where(lane == 4, 1.0 / 3.0, 0.0)
    east = jnp.where(lane == span + 3, 1.0 / 3.0, 0.0) + jnp.where(lane == span + 4, 2.0 / 3.0, 0.0)
    slot = iota((rows, LANES), 1)
    total = jnp.zeros((rows, LANES), jnp.float32)
    for q, field in enumerate((a, m, b, dx(m), cc)):
        for s, weight in enumerate((west, east)):
            value = jnp.sum(field * weight, axis=1, keepdims=True)
            total = total + jnp.where(slot == q * 16 + s + 2 * mem, value, 0.0)

    row = iota(shape, 0) + band * rows
    for end in range(2):
        near = row0 - 1 if end == 0 else row0 + span - 1
        lo, hi = (2.0 / 3.0, 1.0 / 3.0) if end == 0 else (1.0 / 3.0, 2.0 / 3.0)

        def w(i):
            return jnp.where(i == near, lo, 0.0) + jnp.where(i == near + 1, hi, 0.0)

        def u(i):
            return -half * (w(i - 1) - w(i + 1))

        wr, ur = w(row), u(row)
        vr = -half * (u(row - 1) - u(row + 1))
        h1 = jnp.sum(wr * a + ur * m, axis=0, keepdims=True)
        z1 = jnp.sum(wr * (keep * z + rotation * m), axis=0, keepdims=True) - courant * dx(h1)
        m1 = jnp.sum(wr * cc + ur * a + vr * m, axis=0, keepdims=True)
        for f, value in enumerate((h1, z1, m1)):
            ends_ref[end, f, pl.ds(mem, 1), :] = value
    return total


def inner_step(mem, ref, first, last):
    rows = ref.shape[2]
    h, z, m = ref[mem, 0], ref[mem, 1], ref[mem, 2]
    row = iota(h.shape, 0)
    h_above = jnp.where(first, 0.0, -half * m[0:1])
    h_below = jnp.where(last, 0.0, half * m[rows - 1 : rows])

    def ddy(x, above, below):
        up = jnp.where(row == 0, above, row_roll(x, 1))
        down = jnp.where(row == rows - 1, below, row_roll(x, -1))
        return down - up

    h1 = h - half * (lane_roll(z, -1) - lane_roll(z, 1) + ddy(m, 0.0, 0.0))
    ref[mem, 0] = h1
    ref[mem, 1] = keep * z - half * (lane_roll(h1, -1) - lane_roll(h1, 1)) + rotation * m
    ref[mem, 2] = keep * m - half * ddy(h1, h_above, h_below) - rotation * z


def nest_kernel(
    bands,
    span,
    off_ref,
    nest_ref,
    parent_ref,
    nest_out,
    patch,
    halo,
    stepped,
    par_ref,
    edge_ref,
    strip_ref,
    ends_ref,
    ext,
    strips,
    endbuf,
    cols,
    side,
    ghost,
    acc,
    fine,
    thinned,
    dealt,
    cbuf,
    sbuf,
    nest_send,
    nest_recv,
    edge_send,
    edge_recv,
    strip_send,
    strip_recv,
    end_send,
    end_recv,
    mid_send,
    mid_recv,
    out_send,
    out_recv,
    local_sem,
    parent_sem,
    step_sem,
):
    me = lax.axis_index("band")
    group = lax.axis_index("member")
    members, _, nrows, nwidth = nest_ref.shape
    prows = strip_ref.shape[0]
    tile = nrows // 3
    per = bands // members
    top_senders = bands // 2 + 1

    def remote(src, dst, send, recv, to):
        return pltpu.make_async_remote_copy(
            src_ref=src, dst_ref=dst, send_sem=send, recv_sem=recv, device_id=(group, to), device_id_type=MESH
        )

    barrier = pltpu.get_barrier_semaphore()

    def greet(j, _):
        pl.semaphore_signal(barrier, inc=1, device_id=(group, lax.rem(me + j, bands)), device_id_type=MESH)
        return 0

    lax.fori_loop(1, bands, greet, 0)
    own = pltpu.make_async_copy(nest_ref, ext.at[:, :, pl.ds(HALO, nrows), :], local_sem)

    def load(mem):
        return pltpu.make_async_copy(parent_ref.at[mem], par_ref.at[mem], parent_sem.at[mem])

    for mem in range(members):
        load(mem).start()
    own.start()
    pl.semaphore_wait(barrier, bands - 1)

    reach = 2 * NSTEPS

    def nest_down(mem, to):
        return remote(
            nest_ref.at[mem, :, pl.ds(nrows - reach, reach), :],
            ext.at[mem, :, pl.ds(HALO - reach, reach), :],
            nest_send.at[0, mem],
            nest_recv.at[0, mem],
            to,
        )

    def nest_up(mem, to):
        return remote(
            nest_ref.at[mem, :, pl.ds(0, reach), :],
            ext.at[mem, :, pl.ds(HALO + nrows, reach), :],
            nest_send.at[1, mem],
            nest_recv.at[1, mem],
            to,
        )

    def edge_down(to):
        return remote(edge_ref.at[1], halo.at[0], edge_send.at[0], edge_recv.at[0], to)

    def edge_up(to):
        return remote(edge_ref.at[0], halo.at[1], edge_send.at[1], edge_recv.at[1], to)

    def strip_copy(slot, to, index):
        return remote(strip_ref, strips.at[pl.ds(pl.multiple_of((slot + 1) * prows, prows), prows), :], strip_send.at[index], strip_recv.at[slot], to)

    def end_copy(end, slot, to):
        return remote(ends_ref.at[end], endbuf.at[slot], end_send.at[end], end_recv.at[slot], to)

    first, last = me == 0, me == bands - 1

    def gather(mem, _):
        load(mem).wait()

        @pl.when(jnp.logical_not(first))
        def _():
            nest_up(mem, me - 1).start()

        @pl.when(jnp.logical_not(last))
        def _():
            nest_down(mem, me + 1).start()

        strip_ref[...] += window_shares(mem, span, off_ref[0, mem], off_ref[1, mem], me, par_ref, ends_ref)
        return 0

    strip_ref[...] = jnp.zeros_like(strip_ref)
    lax.fori_loop(0, members, gather, 0)

    def send_strip(j, _):
        strip_copy(me, lax.rem(me + j, bands), j).start()
        return 0

    lax.fori_loop(1, bands, send_strip, 0)

    sends_top = jnp.logical_and(me > 0, me < top_senders)
    sends_bottom = jnp.logical_and(me < bands - 1, me >= bands - top_senders)

    @pl.when(sends_top)
    def _():
        end_copy(0, me, 0).start()

    @pl.when(sends_bottom)
    def _():
        end_copy(1, bands - 1 - me, bands - 1).start()

    def form_edges(mem, _):
        edge_rows(mem, par_ref, edge_ref)
        return 0

    lax.fori_loop(0, members, form_edges, 0)

    @pl.when(jnp.logical_not(first))
    def _():
        edge_up(me - 1).start()

    @pl.when(jnp.logical_not(last))
    def _():
        edge_down(me + 1).start()

    pad = strips.shape[0] - (bands + 1) * prows
    strips[pl.ds(0, prows), :] = jnp.zeros((prows, LANES), jnp.float32)
    strips[pl.ds((bands + 1) * prows, pad), :] = jnp.zeros((pad, LANES), jnp.float32)
    strips[pl.ds(pl.multiple_of((me + 1) * prows, prows), prows), :] = strip_ref[...]
    cpad = (cbuf.shape[2] - bands * tile) // 2
    blank = jnp.zeros((span // LANES, 3, cpad, LANES), jnp.float32)
    cbuf[:, :, pl.ds(0, cpad), :] = blank
    cbuf[:, :, pl.ds(cpad + bands * tile, cpad), :] = blank

    ends_lane = span + LANES

    @pl.when(jnp.logical_or(first, last))
    def _():
        j = iota((1, nwidth), 1) + 2
        q, t = j // 3, j % 3
        k = iota((ends_lane, nwidth), 0) - 3
        fine[...] = (jnp.where(k == q, 3 - t, 0) + jnp.where(k == q + 1, t, 0)).astype(jnp.float32).astype(jnp.bfloat16)

    erows = nrows + 2 * HALO
    e = iota((erows, prows), 0)
    q, t = e // 3, e % 3
    k = iota((erows, prows), 1)
    weights = jnp.where(k == q, (3 - t).astype(jnp.float32) / 3.0, 0.0) + jnp.where(
        k == q + 1, t.astype(jnp.float32) / 3.0, 0.0
    )
    thin = jnp.where(iota((nwidth, span), 0) // 3 == iota((nwidth, span), 1), 1.0, 0.0).astype(jnp.bfloat16)
    row = iota((erows, nwidth), 0)
    col = iota((erows, nwidth), 1)
    is_ghost = jnp.logical_or(
        jnp.logical_and(row == HALO - 1, first), jnp.logical_and(row == HALO + nrows, last)
    )
    at_west, at_east = col == 0, col == nwidth - 1
    lanes = iota((erows, LANES), 1)

    def recv_strip(j, _):
        strip_copy(lax.rem(me + j, bands), me, j).wait_recv()
        return 0

    lax.fori_loop(1, bands, recv_strip, 0)

    g = strips[...]
    lane = iota((1, LANES), 1)
    turn = lane_roll(g, -16)
    height = g + jnp.where(lane < 16, -half, courant * half) * (row_roll(turn, -1) - row_roll(turn, 1))
    turn = lane_roll(height, 64)
    cols[...] = jnp.where(lane < 64, height, g - half * (row_roll(turn, -1) - row_roll(turn, 1)))
    picked = jnp.zeros((prows, LANES), jnp.float32)
    for mem in range(members):
        begin = off_ref[0, mem] + (me * tile - 3 + prows)
        picked = jnp.where(lane % 32 // 2 == mem, cols[pl.ds(begin, prows), :], picked)
    side[...] = jnp.dot(weights, picked, precision=highest, preferred_element_type=jnp.float32)


    def add_end(k, _):
        @pl.when(k > 0)
        def _():
            end_copy(0, k, 0).wait_recv()

        acc[...] += endbuf[k]
        return 0

    @pl.when(first)
    def _():
        endbuf[0] = ends_ref[0]

    @pl.when(last)
    def _():
        endbuf[0] = ends_ref[1]

    @pl.when(jnp.logical_or(first, last))
    def _():
        acc[...] = jnp.zeros_like(acc)
        lax.fori_loop(0, top_senders, add_end, 0)
        rows_in = acc[...].reshape(3 * members, ends_lane)
        ghost[...] = (exact_dot(rows_in, fine[...]) * (1.0 / 3.0)).reshape(3, members, nwidth)

    own.wait()

    turn_of = lax.rem(group, per)

    def mid_copy(mem, slot, to):
        return remote(
            dealt.at[mem],
            cbuf.at[:, :, pl.ds(pl.multiple_of(cpad + slot * tile, tile), tile), :],
            mid_send.at[mem],
            mid_recv.at[slot],
            to,
        )

    def one_member(mem, slot):
        def side_of(f, s):
            return jnp.sum(jnp.where(lanes == 32 * f + s + 2 * mem, side[...], 0.0), axis=1, keepdims=True)

        sides = [[side_of(f, s) for s in range(2)] for f in range(2)]
        ends = [ghost[f, pl.ds(mem, 1), :] for f in range(3)]

        def ddx(x, f):
            left = jnp.where(at_west, sides[f][0], lane_roll(x, 1))
            right = jnp.where(at_east, sides[f][1], lane_roll(x, -1))
            return right - left

        def ddy(x):
            return row_roll(x, -1) - row_roll(x, 1)

        def bound(x, f):
            return jnp.where(is_ghost, ends[f], x)

        h, z, m = ext[mem, 0], bound(ext[mem, 1], 1), bound(ext[mem, 2], 2)
        for _ in range(NSTEPS):
            h = bound(h - half * (ddx(z, 1) + ddy(m)), 0)
            z, m = (
                bound(keep * z - half * ddx(h, 0) + rotation * m, 1),
                bound(keep * m - half * ddy(h) - rotation * z, 2),
            )
        lines = []
        for f, x in enumerate((h, z, m)):
            x = x[HALO : HALO + nrows]
            nest_out[mem, f] = x
            pieces = []
            for k in range(nwidth // LANES):
                thinned[slot, f, k] = x[:, k * LANES : (k + 1) * LANES]
                a, b, c = [thinned[slot, f, k, pl.ds(i, tile, stride=3), :] for i in range(3)]
                pieces.append(a + b + c)
            lines.append(jnp.concatenate(pieces, axis=-1))
        return lines

    def pair(i, _):
        group_of = [2 * i, 2 * i + 1]
        for mem in group_of:
            @pl.when(jnp.logical_not(first))
            def _():
                nest_down(mem, me).wait_recv()

            @pl.when(jnp.logical_not(last))
            def _():
                nest_up(mem, me).wait_recv()

        lines = [one_member(mem, slot) for slot, mem in enumerate(group_of)]
        means = exact_dot(jnp.concatenate(lines[0] + lines[1], axis=0), thin) * (1.0 / 9.0)
        for slot, mem in enumerate(group_of):
            for f in range(3):
                at = (3 * slot + f) * tile
                for k in range(span // LANES):
                    dealt[mem, k, f] = means[at : at + tile, k * LANES : (k + 1) * LANES]
            to = per * mem + turn_of

            @pl.when(to != me)
            def _():
                mid_copy(mem, me, to).start()

            @pl.when(to == me)
            def _():
                cbuf[:, :, pl.ds(pl.multiple_of(cpad + me * tile, tile), tile), :] = dealt[mem]

        return 0

    lax.fori_loop(0, members // 2, pair, 0)
    is_mid = lax.rem(me, per) == turn_of
    mine = me // per

    def out_copy(to):
        return remote(sbuf.at[to], patch.at[mine], out_send.at[to], out_recv.at[mine], to)

    @pl.when(is_mid)
    def _():
        def recv(j, _):
            mid_copy(0, lax.rem(me + j, bands), me).wait_recv()
            return 0

        lax.fori_loop(1, bands, recv, 0)
        start_row = off_ref[0, mine]

        def deal(j, _):
            to = lax.rem(me + j, bands)
            begin = jnp.clip(to * prows - start_row, -cpad, bands * tile) + cpad
            for k in range(0, span, LANES):
                sbuf[to, :, :, pl.ds(k, LANES)] = cbuf[k // LANES, :, pl.ds(begin, prows), :]

            @pl.when(to != me)
            def _():
                out_copy(to).start()

            return 0

        lax.fori_loop(1, bands + 1, deal, 0)
        patch[mine] = sbuf[me]

    def out_stepped(mem):
        return pltpu.make_async_copy(par_ref.at[mem], stepped.at[mem], step_sem.at[mem])

    def step_parent(mem, _):
        inner_step(mem, par_ref, first, last)
        out_stepped(mem).start()
        return 0

    lax.fori_loop(0, members, step_parent, 0)

    def recv_patch(mem, _):
        out_stepped(mem).wait()


        @pl.when(per * mem + turn_of != me)
        def _():
            remote(sbuf.at[0], patch.at[mem], out_send.at[0], out_recv.at[mem], me).wait_recv()

        return 0

    lax.fori_loop(0, members, recv_patch, 0)

    @pl.when(jnp.logical_not(first))
    def _():
        edge_down(me).wait_recv()
        edge_up(me).wait_send()

    @pl.when(jnp.logical_not(last))
    def _():
        edge_up(me).wait_recv()
        edge_down(me).wait_send()

    @pl.when(sends_top)
    def _():
        end_copy(0, me, 0).wait_send()

    @pl.when(sends_bottom)
    def _():
        end_copy(1, bands - 1 - me, bands - 1).wait_send()

    def sent_strip(j, _):
        strip_copy(me, lax.rem(me + j, bands), j).wait_send()
        return 0

    lax.fori_loop(1, bands, sent_strip, 0)

    def sent_mid(mem, _):
        @pl.when(jnp.logical_not(first))
        def _():
            nest_up(mem, me).wait_send()

        @pl.when(jnp.logical_not(last))
        def _():
            nest_down(mem, me).wait_send()

        @pl.when(per * mem + turn_of != me)
        def _():
            mid_copy(mem, me, me).wait_send()

        return 0

    lax.fori_loop(0, members, sent_mid, 0)

    @pl.when(is_mid)
    def _():
        def sent_out(j, _):
            out_copy(lax.rem(me + j, bands)).wait_send()
            return 0

        lax.fori_loop(1, bands, sent_out, 0)


def finish(mem, span, bands, off_ref, band_ref, halo_ref, patch_ref, out_ref):
    rows = out_ref.shape[2]
    row0, col0 = off_ref[0, mem], off_ref[1, mem]
    band = band_ref[0]

    def add(first_row, second_row, sign, halo):
        m, p = half * halo[0:1], half * halo[1:2]
        out_ref[mem, 0, first_row : first_row + 1, :] += sign * m
        out_ref[mem, 1, first_row : first_row + 1, :] -= sign * half * (lane_roll(m, -1) - lane_roll(m, 1))
        out_ref[mem, 2, first_row : first_row + 1, :] += sign * p
        out_ref[mem, 2, second_row : second_row + 1, :] += half * m

    @pl.when(band > 0)
    def _():
        add(0, 1, 1.0, halo_ref[0, mem])

    @pl.when(band < bands - 1)
    def _():
        add(rows - 1, rows - 2, -1.0, halo_ref[1, mem])

    block0 = col0 // LANES
    shift = col0 - block0 * LANES
    place = pl.ds(pl.multiple_of(block0 * LANES, LANES), span + LANES)
    wide = jnp.concatenate([patch_ref[mem], jnp.zeros((3, rows, LANES), jnp.float32)], axis=-1)
    wide = pltpu.roll(wide.reshape(3 * rows, span + LANES), shift, 1).reshape(3, rows, span + LANES)
    lane = iota(wide.shape, 2)
    at = iota(wide.shape, 1) + (band * rows - row0)
    inside = (lane >= shift) & (lane < shift + span) & (at >= 0) & (at < span)
    out_ref[mem, :, :, place] = jnp.where(inside, wide, out_ref[mem, :, :, place])


def parent_kernel(
    span,
    bands,
    off_ref,
    band_ref,
    par_ref,
    halo_ref,
    patch_ref,
    nest_ref,
    out_ref,
    nest_out,
    work,
    halos,
    nests,
    in_sem,
    out_sem,
    halo_sem,
    nest_in,
    nest_back,
):
    members = work.shape[0]

    def move_halo(mem):
        return pltpu.make_async_copy(halo_ref.at[:, mem], halos.at[:, mem], halo_sem.at[mem])

    def move_in(mem):
        return pltpu.make_async_copy(par_ref.at[mem], work.at[mem], in_sem.at[mem])

    def move_out(mem):
        return pltpu.make_async_copy(work.at[mem], out_ref.at[mem], out_sem.at[mem])

    def nest_to(mem):
        return pltpu.make_async_copy(nest_ref.at[mem], nests.at[mem], nest_in.at[mem])

    def nest_from(mem):
        return pltpu.make_async_copy(nests.at[mem], nest_out.at[mem], nest_back.at[mem])

    for mem in range(members):
        move_halo(mem).start()
        move_in(mem).start()
        nest_to(mem).start()

    def one_member(mem, _):
        move_halo(mem).wait()
        move_in(mem).wait()
        finish(mem, span, bands, off_ref, band_ref, halos, patch_ref, work)
        move_out(mem).start()
        nest_to(mem).wait()
        nest_from(mem).start()
        return 0

    lax.fori_loop(0, members, one_member, 0)

    def last_wait(mem, _):
        move_out(mem).wait()
        nest_from(mem).wait()
        return 0

    lax.fori_loop(0, members, last_wait, 0)


def per_device(bands, parent_state, nest_state, offsets):
    members, _, prows, width = parent_state.shape
    nrows, nwidth = nest_state.shape[2:]
    span = nwidth // 3
    tile = nrows // 3
    f32 = jnp.float32
    band = lax.axis_index("band").reshape(1).astype(jnp.int32)
    offsets = offsets.T
    shape = jax.ShapeDtypeStruct
    limit = 60 * 1024 * 1024
    vmem = pl.BlockSpec(memory_space=pltpu.VMEM)
    hbm = pl.BlockSpec(memory_space=pl.ANY)
    dma = pltpu.SemaphoreType.DMA
    senders = bands // 2 + 1
    nest_out, patch, halo, stepped = pl.pallas_call(
        functools.partial(nest_kernel, bands, span),
        out_shape=(
            shape(nest_state.shape, f32),
            shape((members, 3, prows, span), f32),
            shape((2, members, 2, width), f32),
            shape(parent_state.shape, f32),
        ),
        in_specs=[pl.BlockSpec(memory_space=pltpu.SMEM), hbm, hbm],
        out_specs=(vmem, vmem, hbm, hbm),
        scratch_shapes=[
            pltpu.VMEM((members, 3, prows, width), f32),
            pltpu.VMEM((2, members, 2, width), f32),
            pltpu.VMEM((prows, LANES), f32),
            pltpu.VMEM((2, 3, members, span + LANES), f32),
            pltpu.VMEM((members, 3, nrows + 2 * HALO, nwidth), f32),
            pltpu.VMEM(((bands + 2) * prows, LANES), f32),
            pltpu.VMEM((senders, 3, members, span + LANES), f32),
            pltpu.VMEM(((bands + 2) * prows, LANES), f32),
            pltpu.VMEM((nrows + 2 * HALO, LANES), f32),
            pltpu.VMEM((3, members, nwidth), f32),
            pltpu.VMEM((3, members, span + LANES), f32),
            pltpu.VMEM((span + LANES, nwidth), jnp.bfloat16),
            pltpu.VMEM((2, 3, nwidth // LANES, nrows, LANES), f32),
            pltpu.VMEM((members, span // LANES, 3, tile, LANES), f32),
            pltpu.VMEM((span // LANES, 3, bands * tile + 2 * prows, LANES), f32),
            pltpu.VMEM((bands, 3, prows, span), f32),
            dma((2, members)),
            dma((2, members)),
            dma((2,)),
            dma((2,)),
            dma((bands,)),
            dma((bands,)),
            dma((2,)),
            dma((senders,)),
            dma((members,)),
            dma((bands,)),
            dma((bands,)),
            dma((members,)),
            dma,
            dma((members,)),
            dma((members,)),
        ],
        compiler_params=pltpu.CompilerParams(collective_id=0, has_side_effects=True, vmem_limit_bytes=limit),
        name="nest",
    )(offsets, nest_state, parent_state)

    smem = pl.BlockSpec(memory_space=pltpu.SMEM)
    return pl.pallas_call(
        functools.partial(parent_kernel, span, bands),
        out_shape=(shape(parent_state.shape, f32), shape(nest_state.shape, f32)),
        in_specs=[smem, smem, hbm, hbm, vmem, hbm],
        out_specs=(hbm, hbm),
        scratch_shapes=[
            pltpu.VMEM((members, 3, prows, width), f32),
            pltpu.VMEM((2, members, 2, width), f32),
            pltpu.VMEM((members, 3, nrows, nwidth), f32),
            dma((members,)),
            dma((members,)),
            dma((members,)),
            dma((members,)),
            dma((members,)),
        ],
        compiler_params=pltpu.CompilerParams(vmem_limit_bytes=limit),
        name="parent",
    )(offsets, band, stepped, halo, patch, nest_out)


def solution(mesh):
    in_specs = (P("member", None, "band", None), P("member", None, "band", None), P("member", None))
    out_specs = (P("member", None, "band", None), P("member", None, "band", None))
    return jax.shard_map(
        functools.partial(per_device, mesh.shape["band"]),
        mesh=mesh,
        in_specs=in_specs,
        out_specs=out_specs,
        check_vma=False,
    )
```
